32 devices in a mesh: tile: 8 (over y, x, core), spec: 4 (over z).
Axes of the slice: x: 2, y: 2, z: 4, core: 2. Of those that a mesh axis runs over, the one named last changes fastest.
Arguments:
- concentrations: float32 [32, 512, 256], P('spec', 'tile'), may hold values from 0.1 to 4
- courant: float32 [512, 256], P('tile'), may hold values from 0.05 to 0.95
- first_weight: bfloat16 [32, 512], replicated, may hold values from -1 to 1
- middle_weight: bfloat16 [512, 512], replicated, may hold values from -0.25 to 0.25
- last_weight: bfloat16 [512, 32], replicated, may hold values from -0.25 to 0.25
- active_blocks: int32 [8, 4, 16], P('tile', 'spec'), may hold values from 0 to 32, as said below
- dest_tile: int32 [8, 4, 16], P('tile', 'spec'), may hold values from 0 to 7, as said below
Outputs:
- chemistry_out: bfloat16 [32, 131072], P(None, ('tile', 'spec'))
- load_share: float32 [8, 4], P('tile', 'spec')
The draws below stay inside these ranges and needn't reach their ends.
Inputs may be any that keep to these rules, and one draw needn't show every extreme that they name: `active_blocks`: each device's entries name distinct blocks of its own 32; the value 32 marks an empty slot. `dest_tile`: A listed block's tile lies within 2 tiles of its home tile along the periodic order of tiles; an empty slot names the home tile. At most 2 blocks of one device name one other tile, and at most 8 listed blocks over all devices of one spec index name one tile; both bounds are reached in every draw.
All inputs are finite; a program needn't handle non-finite values.
Results may differ from the reference program's by a relative error of at most 0.0035.
Values may be sent and summed in bfloat16 or wider, within the bound.
No kernel may reach another device: no remote copies, remote signals or barrier semaphores. Data moves between devices by JAX's collectives and lax.ppermute only.
A program may use at most 64 MiB of HBM per device.

```python
import math
import jax
import jax.numpy as jnp
from jax import lax

HID = 512
BLK = 128
NB = 32
RECV = 8
CAP = 2
NBR = 2
ACT_MAX = 16
SPECIES = 32
NYL = 256
NX = 512
CELLS = 131072
N_TILE = 8
N_SPEC = 4


def plan_lists(key):
    base_key = jax.random.fold_in(key, 11)
    subkeys = jax.random.split(base_key, 6)
    tile_ids = jnp.arange(N_TILE, dtype=jnp.int32)[:, None]
    anchor = jax.random.randint(subkeys[0], (1, N_SPEC), 0, N_TILE)
    signed = (tile_ids - anchor + N_TILE // 2) % N_TILE - N_TILE // 2
    random_toss = jax.random.randint(subkeys[1], (N_TILE, N_SPEC), 0, 2)
    daytime = jnp.where(signed == 0, 1, jnp.where(jnp.abs(signed) <= NBR, 0, random_toss))
    is_anchor = (signed == 0).astype(jnp.int32)
    distances = [step_by for step_by in range(1, NBR + 1)] + [-step_by for step_by in range(1, NBR + 1)]
    take_list = []
    for number, distance in enumerate(distances):
        source_day = jnp.roll(daytime, distance, axis=0)
        source_anchor = jnp.roll(is_anchor, distance, axis=0)
        amount = jax.random.randint(jax.random.fold_in(subkeys[2], number), (N_TILE, N_SPEC), 1, CAP + 1)
        amount = jnp.where(source_anchor == 1, CAP, amount)
        take_list.append(jnp.where((daytime == 0) & (source_day == 1), amount, 0))
    intake = sum(take_list)
    spare_slot = jax.random.randint(subkeys[3], (N_TILE, N_SPEC), 0, 2)
    own_count = jnp.where(daytime == 1, RECV, jnp.maximum(RECV - intake - spare_slot, 0))
    sent_counts = [jnp.roll(taken_count, -distance, axis=0) for taken_count, distance in zip(take_list, distances)]
    counts = jnp.stack([own_count] + sent_counts, axis=-1)
    bounds = jnp.cumsum(counts, axis=-1)
    slot_ids = jnp.arange(ACT_MAX, dtype=jnp.int32)
    category = jnp.sum((slot_ids[None, None, :, None] >= bounds[:, :, None, :]).astype(jnp.int32), axis=-1)
    offset_table = jnp.array([0] + distances + [0], dtype=jnp.int32)
    shifts = offset_table[category]
    is_valid = slot_ids[None, None, :] < bounds[:, :, -1:]
    scores = jax.random.randint(subkeys[4], (N_TILE, N_SPEC, NB), 0, 1 << 20) * NB + jnp.arange(NB, dtype=jnp.int32)
    ranking = jnp.argsort(scores, axis=-1)[..., :ACT_MAX]
    blocks = jnp.where(is_valid, ranking, NB)
    targets = (tile_ids[:, :, None] + shifts) % N_TILE
    species_blending = jax.random.randint(subkeys[5], (N_TILE, N_SPEC, ACT_MAX), 0, 1 << 20) * ACT_MAX + slot_ids
    shuffle_order = jnp.argsort(species_blending, axis=-1)
    blocks = jnp.take_along_axis(blocks, shuffle_order, axis=-1)
    targets = jnp.take_along_axis(targets, shuffle_order, axis=-1)
    return (blocks.astype(jnp.int32), targets.astype(jnp.int32))


def draw_active_blocks(key, part):
    return plan_lists(key)[0]


def draw_dest_tile(key, part):
    return plan_lists(key)[1]


def steps_of(rng, dims, shards, low, high):
    level, own = 1.0, jax.random.fold_in(rng, 6)
    for axis_at, shards_of in shards:
        steps = jnp.exp(jax.random.uniform(jax.random.fold_in(own, axis_at), (shards_of,), jnp.float32, low / len(shards), high / len(shards)))
        level = level * jnp.repeat(steps, dims[axis_at] // shards_of).reshape([-1 if axis == axis_at else 1 for axis in range(len(dims))])
    return level


def centred(rng, shape, width, bound, held_as=jnp.bfloat16):
    return jnp.clip(width * jax.random.normal(rng, shape, jnp.float32), -bound, bound).astype(held_as)


def setup_inputs(seed: int = 0) -> dict:
    keys = jax.random.split(jax.random.key(seed), 8)
    concentrations = jnp.clip(jnp.exp(math.log(4.0) - 3.6888794 * jax.random.uniform(keys[0], (SPECIES, NX, NYL), jnp.float32) ** steps_of(keys[0], (SPECIES, NX, NYL), ((0, 4), (1, 8)), -0.2, 0.2)), 0.1, 4.0)
    courant = jnp.clip(0.05 + 0.9 * jax.random.uniform(keys[1], (NX, NYL), jnp.float32) ** steps_of(keys[1], (NX, NYL), ((0, 8),), -0.2, 0.2), 0.05, 0.95)
    first_weight = centred(keys[2], (SPECIES, HID), SPECIES ** -0.5, 1.0)
    middle_weight = centred(keys[3], (HID, HID), HID ** -0.5, 0.25)
    last_weight = centred(keys[4], (HID, SPECIES), HID ** -0.5, 0.25)
    active_blocks = draw_active_blocks(jax.random.fold_in(keys[7], 71), 0)
    dest_tile = draw_dest_tile(jax.random.fold_in(keys[7], 71), 0)
    return dict(concentrations=concentrations, courant=courant, first_weight=first_weight, middle_weight=middle_weight, last_weight=last_weight, active_blocks=active_blocks, dest_tile=dest_tile)


def sweep_once(values, courant):
    left_diff = values - jnp.roll(values, 1, axis=0)
    right_diff = jnp.roll(values, -1, axis=0) - values
    slopes = jnp.where(left_diff * right_diff > 0, jnp.sign(left_diff) * jnp.minimum(jnp.abs(left_diff), jnp.abs(right_diff)), 0.0)
    fluxes = courant * (values + 0.5 * (1.0 - courant) * slopes)
    return values - fluxes + jnp.roll(fluxes, 1, axis=0)


def surrogate(inputs, first_weight, middle_weight, last_weight):
    first_layer = jax.nn.silu(jnp.dot(first_weight.T, inputs, preferred_element_type=jnp.float32)).astype(jnp.bfloat16)
    second = jax.nn.silu(jnp.dot(middle_weight.T, first_layer, preferred_element_type=jnp.float32)).astype(jnp.bfloat16)
    change = jnp.dot(last_weight.T, second, preferred_element_type=jnp.float32)
    return (inputs.astype(jnp.float32) + change).astype(jnp.bfloat16)


def reference(concentrations, courant, first_weight, middle_weight, last_weight, active_blocks, dest_tile):
    def advect_species(values):
        for repeat in range(2):
            values = sweep_once(values, courant)
        return values.astype(jnp.bfloat16)

    advected = lax.map(advect_species, concentrations)
    devices_all = N_TILE * N_SPEC
    cell_table = advected.reshape(SPECIES, devices_all, NB, BLK).transpose(1, 2, 0, 3)
    list_table = active_blocks.reshape(devices_all, ACT_MAX)

    def chem_device(operands):
        blocks_dev, listing = operands
        safe_index = jnp.minimum(listing, NB - 1).astype(jnp.int32)
        picked = blocks_dev[safe_index].transpose(1, 0, 2).reshape(SPECIES, ACT_MAX * BLK)
        refreshed_state = surrogate(picked, first_weight, middle_weight, last_weight)
        refreshed_state = refreshed_state.reshape(SPECIES, ACT_MAX, BLK).transpose(1, 0, 2)
        return blocks_dev.at[listing.astype(jnp.int32)].set(refreshed_state, mode="drop")

    new_cells = lax.map(chem_device, (cell_table, list_table))
    chemistry_out = new_cells.transpose(2, 0, 1, 3).reshape(SPECIES, CELLS)
    hit_table = (dest_tile[..., None] == jnp.arange(N_TILE, dtype=jnp.int32)) & (active_blocks < NB)[..., None]
    load_share = jnp.sum(hit_table.astype(jnp.float32), axis=(0, 2)).T / RECV
    return chemistry_out, load_share
```

```python
import functools

import jax
import jax.numpy as jnp
from jax import lax
from jax.experimental import pallas as pl
from jax.experimental.pallas import tpu as pltpu
from jax.sharding import PartitionSpec as P

BLK = 128
RECV = 8
BEHIND = 4
AHEAD = 2
VMEM_BYTES = 16 * 1024 * 1024


def silu(v):
    half = 0.5 * v
    return half + half * jnp.tanh(half)


def sweep_rows(rows, rates):
    diffs = [b - a for a, b in zip(rows[:-1], rows[1:])]
    fluxes = []
    for at in range(1, len(rows) - 1):
        left, right = diffs[at - 1], diffs[at]
        slope = jnp.maximum(jnp.minimum(left, right), 0.0) + jnp.minimum(
            jnp.maximum(left, right), 0.0
        )
        rate, damp = rates[at]
        fluxes.append(rate * (rows[at] + damp * slope))
    return [rows[at] - fluxes[at - 1] + fluxes[at - 2] for at in range(2, len(rows) - 1)]


def two_sweeps(rows, rates):
    once = sweep_rows(rows, rates)
    return sweep_rows(once, rates[2:-1])


def with_damp(rate, shape):
    rate = jnp.broadcast_to(rate, shape)
    return rate, 0.5 - 0.5 * rate


def inner_kernel(dests, length, q_ref, courant_ref, up_ref, down_ref, context_ref, *refs):
    *out_refs, held_ref, rates_ref, arrived = refs
    species = q_ref.shape[0] // length
    cols = q_ref.shape[1]
    share = length // dests
    reach = BEHIND + AHEAD
    me = lax.axis_index("spec")
    lanes = held_ref.shape[2]
    copies = [
        [
            pltpu.make_async_copy(
                source.at[:, h * lanes : (h + 1) * lanes], target.at[h], arrived.at[h, i]
            )
            for i, (source, target) in enumerate([(courant_ref, rates_ref), (q_ref, held_ref)])
        ]
        for h in range(cols // lanes)
    ]
    for pair in copies:
        for copy in pair:
            copy.start()
    for h, pair in enumerate(copies):
        here = slice(h * lanes, (h + 1) * lanes)

        def row(at):
            return held_ref[h, pl.ds(at, species, stride=length), :]

        def rate_row(at):
            return with_damp(rates_ref[h, pl.ds(at, 1), :], (species, lanes))

        for copy in pair:
            copy.wait()
        up_ref[BEHIND * species :, here] = rates_ref[h, length - 8 :, :]
        down_ref[AHEAD * species :, here] = rates_ref[h, 0:8, :]
        for j in range(BEHIND):
            up_ref[j * species : (j + 1) * species, here] = row(length - BEHIND + j)
        for j in range(AHEAD):
            down_ref[j * species : (j + 1) * species, here] = row(j)
        for j in range(reach):
            context_ref[j * species : (j + 1) * species, here] = row(j)
            context_ref[(reach + j) * species : (reach + j + 1) * species, here] = row(
                length - reach + j
            )
        for k in range(dests):
            first = lax.rem(me + k, dests) * share
            places = [
                jnp.clip(first + at, 0, length - 1) for at in range(-BEHIND, share + AHEAD)
            ]
            done = two_sweeps([row(at) for at in places], [rate_row(at) for at in places])
            for at, value in enumerate(done):
                start = at * cols + h * lanes
                out_refs[k][:, start : start + lanes] = value.astype(jnp.bfloat16)


def edge_kernel(dests, length, up_ref, down_ref, context_ref, courant_ref, *out_refs):
    species = out_refs[0].shape[0]
    cols = courant_ref.shape[1]
    me = lax.axis_index("spec")
    reach = BEHIND + AHEAD

    def part(ref, at):
        return ref[at * species : (at + 1) * species, :]

    def rate_rows(ref, start, count):
        return [with_damp(ref[at : at + 1, :], (species, cols)) for at in range(start, start + count)]

    behind = [part(up_ref, j) for j in range(BEHIND)]
    ahead = [part(down_ref, j) for j in range(AHEAD)]
    lowest = [part(context_ref, j) for j in range(reach)]
    highest = [part(context_ref, reach + j) for j in range(reach)]
    top = two_sweeps(
        behind + lowest,
        rate_rows(up_ref, BEHIND * species + 8 - BEHIND, BEHIND) + rate_rows(courant_ref, 0, reach),
    )
    bottom = two_sweeps(
        highest + ahead,
        rate_rows(courant_ref, length - reach, reach)
        + rate_rows(down_ref, AHEAD * species, AHEAD),
    )
    fill = [jnp.zeros_like(bottom[0])] * (BEHIND - AHEAD)
    for k in range(dests):
        for j, (one, other) in enumerate(zip(top, fill + bottom)):
            out_refs[k][:, j * cols : (j + 1) * cols] = jnp.where(me == k, one, other).astype(
                jnp.bfloat16
            )


def chemistry_kernel(groups, slots, list_ref, w1_ref, w2_ref, w3_ref, *refs):
    parts, edges = refs[:groups], refs[groups : 2 * groups]
    out_ref, picked_ref, fresh_ref = refs[2 * groups :]
    species, cells = out_ref.shape[1:]
    blocks = cells // BLK
    wide = edges[0].shape[1]
    narrow = wide // BEHIND * AHEAD
    me = lax.axis_index("spec")
    for k in range(groups):
        out_ref[lax.rem(me - k + groups, groups)] = parts[k][...]

    @pl.when(me == 0)
    def _():
        for k in range(groups):
            out_ref[k, :, 0:wide] = edges[k][...]

    @pl.when(me == groups - 1)
    def _():
        for k in range(groups):
            out_ref[groups - 1 - k, :, cells - narrow :] = edges[k][:, wide - narrow :]

    def place(j):
        return pl.ds(pl.multiple_of(jnp.minimum(list_ref[j], blocks - 1) * BLK, BLK), BLK)

    for j in range(slots):
        for g in range(groups):
            picked_ref[g * species : (g + 1) * species, j * BLK : (j + 1) * BLK] = out_ref[
                g, :, place(j)
            ].astype(jnp.float32)
    width = 4 * BLK
    for start in range(0, slots * BLK, width):
        x = picked_ref[:, start : start + width]
        hidden = jnp.dot(w1_ref[...], x.astype(jnp.bfloat16), preferred_element_type=jnp.float32)
        hidden = silu(hidden).astype(jnp.bfloat16)
        hidden = jnp.dot(w2_ref[...], hidden, preferred_element_type=jnp.float32)
        hidden = silu(hidden).astype(jnp.bfloat16)
        fresh_ref[:, start : start + width] = x + jnp.dot(
            w3_ref[...], hidden, preferred_element_type=jnp.float32
        )
    for j in range(slots):

        @pl.when(list_ref[j] < blocks)
        def _():
            for g in range(groups):
                out_ref[g, :, place(j)] = fresh_ref[
                    g * species : (g + 1) * species, j * BLK : (j + 1) * BLK
                ].astype(jnp.bfloat16)


def vmem():
    return pl.BlockSpec(memory_space=pltpu.VMEM)


def shards(
    concentrations, courant, first_weight, middle_weight, last_weight, active_blocks, dest_tile
):
    species, length, cols = concentrations.shape
    dests = lax.axis_size("spec")
    tiles = lax.axis_size("tile")
    cells = length // dests * cols
    slots = active_blocks.shape[-1]
    params = pltpu.CompilerParams(vmem_limit_bytes=VMEM_BYTES)
    reach = BEHIND + AHEAD
    f32, bf16 = jnp.float32, jnp.bfloat16

    up, down, context, *blocks = pl.pallas_call(
        functools.partial(inner_kernel, dests, length),
        out_shape=[
            jax.ShapeDtypeStruct((BEHIND * species + 8, cols), f32),
            jax.ShapeDtypeStruct((AHEAD * species + 8, cols), f32),
            jax.ShapeDtypeStruct((2 * reach * species, cols), f32),
        ]
        + [jax.ShapeDtypeStruct((species, cells), bf16)] * dests,
        in_specs=[pl.BlockSpec(memory_space=pltpu.HBM)] * 2,
        out_specs=[vmem()] * (3 + dests),
        scratch_shapes=[
            pltpu.VMEM((cols // BLK, species * length, BLK), f32),
            pltpu.VMEM((cols // BLK, length, BLK), f32),
            pltpu.SemaphoreType.DMA((cols // BLK, 2)),
        ],
        compiler_params=params,
        name="inner_rows",
    )(concentrations.reshape(species * length, cols), courant)

    forward = [(t, (t + 1) % tiles) for t in range(tiles)]
    backward = [(b, a) for a, b in forward]
    received = [blocks[0]] + [
        lax.ppermute(blocks[k], "spec", [(s, (s + k) % dests) for s in range(dests)])
        for k in range(1, dests)
    ]
    behind = lax.ppermute(up, "tile", forward)
    ahead = lax.ppermute(down, "tile", backward)
    edges = pl.pallas_call(
        functools.partial(edge_kernel, dests, length),
        out_shape=[jax.ShapeDtypeStruct((species, BEHIND * cols), bf16)] * dests,
        in_specs=[vmem()] * 4,
        out_specs=[vmem()] * dests,
        compiler_params=params,
        name="edge_rows",
    )(behind, ahead, context, courant)
    edges = [edges[0]] + [
        lax.ppermute(edges[k], "spec", [(k, 0), (dests - 1 - k, dests - 1)])
        for k in range(1, dests)
    ]

    listing = active_blocks.reshape(-1)
    hits = (dest_tile.reshape(-1)[None, :] == jnp.arange(tiles, dtype=jnp.int32)[:, None]) & (
        listing < cells // BLK
    )[None, :]
    share = lax.psum_scatter(
        jnp.sum(hits.astype(f32), axis=1), "tile", scatter_dimension=0, tiled=True
    )
    load_share = (share / RECV).reshape(1, 1)

    out = pl.pallas_call(
        functools.partial(chemistry_kernel, dests, slots),
        out_shape=jax.ShapeDtypeStruct((dests, species, cells), bf16),
        in_specs=[pl.BlockSpec(memory_space=pltpu.SMEM)] + [vmem()] * (3 + 2 * dests),
        out_specs=vmem(),
        scratch_shapes=[
            pltpu.VMEM((dests * species, slots * BLK), f32),
            pltpu.VMEM((dests * species, slots * BLK), f32),
        ],
        compiler_params=params,
        name="chemistry",
    )(listing, first_weight.T, middle_weight.T, last_weight.T, *received, *edges)
    return out.reshape(dests * species, cells), load_share


def solution(mesh):
    in_specs = (
        P("spec", "tile", None),
        P("tile", None),
        P(),
        P(),
        P(),
        P("tile", "spec", None),
        P("tile", "spec", None),
    )
    out_specs = (P(None, ("tile", "spec")), P("tile", "spec"))
    return jax.shard_map(shards, mesh=mesh, in_specs=in_specs, out_specs=out_specs, check_vma=False)
```

```python
import functools

import jax
import jax.numpy as jnp
from jax import lax
from jax.experimental import pallas as pl
from jax.experimental.pallas import tpu as pltpu
from jax.sharding import PartitionSpec as P

BLK = 128
RECV = 8
LANES = 128
SUB = 8
BEHIND = 4
AHEAD = 2
VMEM_BYTES = 16 * 1024 * 1024


def silu_of_half(half):
    return half + half * jnp.tanh(half)


def sweep_rows(rows, rates):
    diffs = [b - a for a, b in zip(rows[:-1], rows[1:])]
    fluxes = []
    for at in range(1, len(rows) - 1):
        left, right = diffs[at - 1], diffs[at]
        slope = jnp.maximum(jnp.minimum(left, right), 0.0) + jnp.minimum(
            jnp.maximum(left, right), 0.0
        )
        rate, damp = rates[at]
        fluxes.append(rate * (rows[at] + damp * slope))
    return [rows[at] - fluxes[at - 1] + fluxes[at - 2] for at in range(2, len(rows) - 1)]


def two_sweeps(rows, rates):
    once = sweep_rows(rows, rates)
    return sweep_rows(once, rates[2:-1])


def with_damp(rate, shape):
    rate = jnp.broadcast_to(rate, shape)
    return rate, 0.5 - 0.5 * rate


def tiled(x, halves):
    lead, (rows, cols) = x.shape[:-2], x.shape[-2:]
    x = x.reshape(lead + (rows // SUB, SUB, halves, LANES))
    axes = tuple(range(len(lead)))
    x = x.transpose(axes + tuple(len(lead) + a for a in (0, 2, 1, 3)))
    return x.reshape(lead + (rows * halves, LANES))


def spot(at, half, halves):
    return (at // SUB * halves + half) * SUB + at % SUB


def pack_kernel(
    length, halves, blocks, q_in, rates_in, list_in, dest_in,
    even_ref, odd_ref, hits_ref, q_ref, rates_ref, list_ref, dest_ref, arrived,
):
    pairs = [(q_in, q_ref), (rates_in, rates_ref), (list_in, list_ref), (dest_in, dest_ref)]
    copies = [
        pltpu.make_async_copy(source, target, arrived.at[i])
        for i, (source, target) in enumerate(pairs)
    ]
    for copy in copies:
        copy.start()
    species = q_ref.shape[0] // (length * halves)
    part = BEHIND * species + SUB

    def row(at, half):
        return q_ref[pl.ds(spot(at, half, halves), species, stride=length * halves), :]

    copies[2].wait()
    copies[3].wait()
    lane = lax.broadcasted_iota(jnp.int32, (SUB, LANES), 1)
    hits = jnp.zeros((SUB, LANES), jnp.float32)
    for j in range(list_ref.shape[0]):
        target = jnp.where(list_ref[j] < blocks, dest_ref[j], -1)
        hits = hits + jnp.where(lane == target, 1.0, 0.0)
    hits_ref[...] = hits
    copies[1].wait()
    copies[0].wait()

    def write(up_ref, down_ref):
        for half in range(halves):
            start = half * part
            for j in range(BEHIND):
                up_ref[start + j * species : start + (j + 1) * species, :] = row(
                    length - BEHIND + j, half
                )
            for j in range(AHEAD):
                down_ref[start + j * species : start + (j + 1) * species, :] = row(j, half)
            for j in range(AHEAD, BEHIND):
                down_ref[start + j * species : start + (j + 1) * species, :] = jnp.zeros(
                    (species, LANES), jnp.float32
                )
            high, low = spot(length - SUB, half, halves), spot(0, half, halves)
            up_ref[start + BEHIND * species : start + part, :] = rates_ref[high : high + SUB, :]
            down_ref[start + BEHIND * species : start + part, :] = rates_ref[low : low + SUB, :]
        up_ref[halves * part :, :] = hits
        down_ref[halves * part :, :] = hits

    even = lax.rem(lax.axis_index("tile"), 2) == 0

    @pl.when(even)
    def _():
        write(even_ref, odd_ref)

    @pl.when(jnp.logical_not(even))
    def _():
        write(odd_ref, even_ref)


def inner_kernel(dests, length, halves, q_ref, rates_ref, *out_refs):
    species = out_refs[0].shape[0]
    share = length // dests
    me = lax.axis_index("spec")
    for k in range(dests):
        first = lax.rem(me + k, dests) * share
        below = jnp.maximum(first - SUB, 0)
        above = jnp.minimum(first + share, length - SUB)
        for half in range(halves):

            def start(at):
                if at < 0:
                    return below * halves + spot(at + SUB, half, halves)
                if at >= share:
                    return above * halves + spot(at - share, half, halves)
                return first * halves + spot(at, half, halves)

            reach = range(-BEHIND, share + AHEAD)
            rows = [q_ref[pl.ds(start(at), species, stride=length * halves), :] for at in reach]
            rates = [
                with_damp(rates_ref[pl.ds(start(at), 1), :], (species, LANES)) for at in reach
            ]
            for at, value in enumerate(two_sweeps(rows, rates)):
                place = (at * halves + half) * LANES
                out_refs[k][:, place : place + LANES] = value.astype(jnp.bfloat16)


def edge_kernel(dests, length, halves, even_ref, odd_ref, hits_ref, q_ref, rates_ref, *refs):
    out_refs = refs[dests : 2 * dests]
    to_even_ref, to_odd_ref, known_ref = refs[2 * dests :]
    species, cells = out_refs[0].shape
    part = BEHIND * species + SUB
    reach = BEHIND + AHEAD
    me = lax.axis_index("spec")
    even = lax.rem(lax.axis_index("tile"), 2) == 0
    own, from_even, from_odd = hits_ref[...], even_ref[halves * part :, :], odd_ref[halves * part :, :]
    known_ref[...] = own + from_even + from_odd
    to_even_ref[...] = from_odd
    to_odd_ref[...] = from_even

    def message(behind, at, size):
        a, b = odd_ref[at : at + size, :], even_ref[at : at + size, :]
        return jnp.where(even, a, b) if behind else jnp.where(even, b, a)

    def row(at, half):
        return q_ref[pl.ds(spot(at, half, halves), species, stride=length * halves), :]

    def rates_of(values):
        return [with_damp(value, (species, LANES)) for value in values]

    tops, bottoms = [], []
    for half in range(halves):
        base = half * part
        behind = [message(True, base + j * species, species) for j in range(BEHIND)]
        ahead = [message(False, base + j * species, species) for j in range(AHEAD)]
        before = message(True, base + BEHIND * species, SUB)
        after = message(False, base + BEHIND * species, SUB)

        def own_rates(first):
            places = [spot(first + j, half, halves) for j in range(reach)]
            return [rates_ref[at : at + 1, :] for at in places]

        tops.append(
            two_sweeps(
                behind + [row(j, half) for j in range(reach)],
                rates_of([before[SUB - BEHIND + j :][:1] for j in range(BEHIND)] + own_rates(0)),
            )
        )
        bottoms.append(
            two_sweeps(
                [row(length - reach + j, half) for j in range(reach)] + ahead,
                rates_of(own_rates(length - reach) + [after[j : j + 1] for j in range(AHEAD)]),
            )
        )
    top = [tops[half][j].astype(jnp.bfloat16) for j in range(BEHIND) for half in range(halves)]
    bottom = [bottoms[half][j].astype(jnp.bfloat16) for j in range(AHEAD) for half in range(halves)]
    for k in range(dests):
        dest = lax.rem(me + k, dests)

        @pl.when(dest == 0)
        def _():
            for j, value in enumerate(top):
                out_refs[k][:, j * LANES : (j + 1) * LANES] = value

        @pl.when(dest == dests - 1)
        def _():
            for j, value in enumerate(bottom):
                at = cells + (j - len(bottom)) * LANES
                out_refs[k][:, at : at + LANES] = value


def weight_kernel(w1_ref, w2_ref, after_ref, w1_out, w2_out):
    w1_out[...] = (0.5 * w1_ref[...].astype(jnp.float32)).T.astype(jnp.bfloat16)
    w2_out[...] = (0.5 * w2_ref[...].astype(jnp.float32)).T.astype(jnp.bfloat16)


def chemistry_kernel(groups, list_in, w1_ref, w2_ref, w3_ref, known_ref, even_ref, odd_ref, *refs):
    parts = refs[:groups]
    out_ref, share_ref, list_ref, state_ref, picked_ref, fresh_ref, done = refs[groups:]
    species, cells = state_ref.shape[1:]
    slots = list_ref.shape[0]
    blocks = cells // BLK
    me = lax.axis_index("spec")
    listing = pltpu.make_async_copy(list_in, list_ref, done.at[0])
    listing.start()
    for k in range(groups):
        state_ref[lax.rem(me - k + groups, groups)] = parts[k][...]
    whole = pltpu.make_async_copy(state_ref, out_ref, done.at[1])
    whole.start()
    hits = known_ref[...] + even_ref[...] + odd_ref[...]
    lane = lax.broadcasted_iota(jnp.int32, hits.shape, 1)
    mine = jnp.where(lane == lax.axis_index("tile"), hits, 0.0)
    share_ref[...] = jnp.sum(mine[0:1], axis=1, keepdims=True) / RECV
    listing.wait()

    def place(j):
        return pl.ds(pl.multiple_of(jnp.minimum(list_ref[j], blocks - 1) * BLK, BLK), BLK)

    for j in range(slots):
        for g in range(groups):
            picked_ref[g * species : (g + 1) * species, j * BLK : (j + 1) * BLK] = state_ref[
                g, :, place(j)
            ].astype(jnp.float32)

    def result(j):
        return pltpu.make_async_copy(fresh_ref.at[j], out_ref.at[:, :, place(j)], done.at[2 + j])

    each = 4
    for first in range(0, slots, each):
        x = picked_ref[:, first * BLK : (first + each) * BLK]
        hidden = jnp.dot(w1_ref[...], x.astype(jnp.bfloat16), preferred_element_type=jnp.float32)
        hidden = silu_of_half(hidden).astype(jnp.bfloat16)
        hidden = jnp.dot(w2_ref[...], hidden, preferred_element_type=jnp.float32)
        hidden = silu_of_half(hidden).astype(jnp.bfloat16)
        y = x + jnp.dot(w3_ref[...], hidden, preferred_element_type=jnp.float32)
        for j in range(first, first + each):
            for g in range(groups):
                fresh_ref[j, g] = y[
                    g * species : (g + 1) * species, (j - first) * BLK : (j - first + 1) * BLK
                ].astype(jnp.bfloat16)
        if first == 0:
            whole.wait()
        for j in range(first, first + each):

            @pl.when(list_ref[j] < blocks)
            def _():
                result(j).start()

    for j in range(slots):

        @pl.when(list_ref[j] < blocks)
        def _():
            result(j).wait()


def vmem():
    return pl.BlockSpec(memory_space=pltpu.VMEM)


def anywhere():
    return pl.BlockSpec(memory_space=pl.ANY)


def from_hbm(x):
    return pltpu.with_memory_space_constraint(x, pltpu.HBM)


def cost(us):
    return pl.CostEstimate(flops=int(us * 1e9), bytes_accessed=int(us * 3e6), transcendentals=0)


def shards(
    concentrations, courant, first_weight, middle_weight, last_weight, active_blocks, dest_tile
):
    species, length, cols = concentrations.shape
    dests = lax.axis_size("spec")
    tiles = lax.axis_size("tile")
    cells = length // dests * cols
    slots = active_blocks.shape[-1]
    halves = cols // LANES
    f32, bf16 = jnp.float32, jnp.bfloat16
    params = pltpu.CompilerParams(vmem_limit_bytes=VMEM_BYTES)
    listing = active_blocks.reshape(-1)
    size = halves * (BEHIND * species + SUB) + SUB
    flag = jax.ShapeDtypeStruct((SUB, LANES), f32)
    block = jax.ShapeDtypeStruct((species, cells), bf16)

    to_even, to_odd, hits, field, rates = pl.pallas_call(
        functools.partial(pack_kernel, length, halves, cells // BLK),
        out_shape=[jax.ShapeDtypeStruct((size, LANES), f32)] * 2
        + [
            flag,
            jax.ShapeDtypeStruct((species * length * halves, LANES), f32),
            jax.ShapeDtypeStruct((length * halves, LANES), f32),
        ],
        in_specs=[anywhere()] * 4,
        out_specs=[vmem()] * 5,
        scratch_shapes=[
            pltpu.SMEM((slots,), jnp.int32),
            pltpu.SMEM((slots,), jnp.int32),
            pltpu.SemaphoreType.DMA((4,)),
        ],
        compiler_params=params,
        cost_estimate=cost(1.0),
        name="pack_edges",
    )(
        from_hbm(tiled(concentrations, halves).reshape(species * length * halves, LANES)),
        from_hbm(tiled(courant, halves)),
        from_hbm(listing),
        from_hbm(dest_tile.reshape(-1)),
    )
    evens = [(t, t ^ 1) for t in range(tiles)]
    odds = [(t, ((t + 1) ^ 1) - 1) for t in range(tiles)]
    odds = [(t, other % tiles) for t, other in odds]
    from_even = lax.ppermute(to_even, "tile", evens)
    from_odd = lax.ppermute(to_odd, "tile", odds)
    blocks = pl.pallas_call(
        functools.partial(inner_kernel, dests, length, halves),
        out_shape=[block] * dests,
        in_specs=[vmem()] * 2,
        out_specs=[vmem()] * dests,
        compiler_params=params,
        cost_estimate=cost(1.0),
        name="inner_rows",
    )(field, rates)
    *blocks, to_even, to_odd, known = pl.pallas_call(
        functools.partial(edge_kernel, dests, length, halves),
        out_shape=[block] * dests + [flag] * 3,
        in_specs=[vmem()] * (5 + dests),
        out_specs=[vmem()] * (dests + 3),
        input_output_aliases={5 + k: k for k in range(dests)},
        compiler_params=params,
        cost_estimate=cost(0.1),
        name="edge_rows",
    )(from_even, from_odd, hits, field, rates, *blocks)
    received = [blocks[0]] + [
        lax.ppermute(blocks[k], "spec", [(s, (s + k) % dests) for s in range(dests)])
        for k in range(1, dests)
    ]
    from_even = lax.ppermute(to_even, "tile", evens)
    from_odd = lax.ppermute(to_odd, "tile", odds)
    w1, w2 = pl.pallas_call(
        weight_kernel,
        out_shape=[jax.ShapeDtypeStruct(w.shape[::-1], bf16) for w in (first_weight, middle_weight)],
        in_specs=[vmem(), vmem(), anywhere()],
        out_specs=[vmem()] * 2,
        compiler_params=params,
        cost_estimate=cost(0.5),
        name="halved_weights",
    )(first_weight, middle_weight, known)
    out, load_share = pl.pallas_call(
        functools.partial(chemistry_kernel, dests),
        out_shape=[
            jax.ShapeDtypeStruct((dests, species, cells), bf16),
            jax.ShapeDtypeStruct((1, 1), f32),
        ],
        in_specs=[anywhere()] + [vmem()] * (6 + dests),
        out_specs=[anywhere(), vmem()],
        scratch_shapes=[
            pltpu.SMEM((slots,), jnp.int32),
            pltpu.VMEM((dests, species, cells), bf16),
            pltpu.VMEM((dests * species, slots * BLK), f32),
            pltpu.VMEM((slots, dests, species, BLK), bf16),
            pltpu.SemaphoreType.DMA((2 + slots,)),
        ],
        compiler_params=params,
        cost_estimate=cost(4.0),
        name="chemistry",
    )(
        from_hbm(listing),
        w1,
        w2,
        last_weight.T,
        known,
        from_even,
        from_odd,
        *received,
    )
    return out.reshape(dests * species, cells), load_share


def solution(mesh):
    in_specs = (
        P("spec", "tile", None),
        P("tile", None),
        P(),
        P(),
        P(),
        P("tile", "spec", None),
        P("tile", "spec", None),
    )
    out_specs = (P(None, ("tile", "spec")), P("tile", "spec"))
    return jax.shard_map(shards, mesh=mesh, in_specs=in_specs, out_specs=out_specs, check_vma=False)
```

```python
import functools

import jax
import jax.numpy as jnp
from jax import lax
from jax.experimental import pallas as pl
from jax.experimental.pallas import tpu as pltpu
from jax.sharding import PartitionSpec as P

BLK = 128
RECV = 8
LANES = 128
SUB = 8
BEHIND = 4
AHEAD = 2
VMEM_BYTES = 16 * 1024 * 1024


def silu_of_half(half):
    return half + half * jnp.tanh(half)


def sweep_rows(rows, rates):
    diffs = [b - a for a, b in zip(rows[:-1], rows[1:])]
    fluxes = []
    for at in range(1, len(rows) - 1):
        left, right = diffs[at - 1], diffs[at]
        slope = jnp.maximum(jnp.minimum(left, right), 0.0) + jnp.minimum(
            jnp.maximum(left, right), 0.0
        )
        rate, damp = rates[at]
        fluxes.append(rate * (rows[at] + damp * slope))
    return [rows[at] - fluxes[at - 1] + fluxes[at - 2] for at in range(2, len(rows) - 1)]


def two_sweeps(rows, rates):
    once = sweep_rows(rows, rates)
    return sweep_rows(once, rates[2:-1])


def with_damp(rate, shape):
    rate = jnp.broadcast_to(rate, shape)
    return rate, 0.5 - 0.5 * rate


def tiled(x, halves):
    lead, (rows, cols) = x.shape[:-2], x.shape[-2:]
    x = x.reshape(lead + (rows // SUB, SUB, halves, LANES))
    axes = tuple(range(len(lead)))
    x = x.transpose(axes + tuple(len(lead) + a for a in (0, 2, 1, 3)))
    return x.reshape(lead + (rows * halves, LANES))


def spot(at, half, halves):
    return (at // SUB * halves + half) * SUB + at % SUB


def pack_kernel(
    length, halves, blocks, q_in, rates_in, list_in, dest_in,
    even_ref, odd_ref, hits_ref, q_ref, rates_ref, list_ref, dest_ref, arrived,
):
    pairs = [(q_in, q_ref), (rates_in, rates_ref), (list_in, list_ref), (dest_in, dest_ref)]
    copies = [
        pltpu.make_async_copy(source, target, arrived.at[i])
        for i, (source, target) in enumerate(pairs)
    ]
    for copy in copies:
        copy.start()
    species = q_ref.shape[0] // (length * halves)
    part = BEHIND * species + SUB

    def row(at, half):
        return q_ref[pl.ds(spot(at, half, halves), species, stride=length * halves), :]

    copies[2].wait()
    copies[3].wait()
    lane = lax.broadcasted_iota(jnp.int32, (SUB, LANES), 1)
    hits = jnp.zeros((SUB, LANES), jnp.float32)
    for j in range(list_ref.shape[0]):
        target = jnp.where(list_ref[j] < blocks, dest_ref[j], -1)
        hits = hits + jnp.where(lane == target, 1.0, 0.0)
    hits_ref[...] = hits
    copies[1].wait()
    copies[0].wait()

    def write(up_ref, down_ref):
        for half in range(halves):
            start = half * part
            for j in range(BEHIND):
                up_ref[start + j * species : start + (j + 1) * species, :] = row(
                    length - BEHIND + j, half
                )
            for j in range(AHEAD):
                down_ref[start + j * species : start + (j + 1) * species, :] = row(j, half)
            for j in range(AHEAD, BEHIND):
                down_ref[start + j * species : start + (j + 1) * species, :] = jnp.zeros(
                    (species, LANES), jnp.float32
                )
            high, low = spot(length - SUB, half, halves), spot(0, half, halves)
            up_ref[start + BEHIND * species : start + part, :] = rates_ref[high : high + SUB, :]
            down_ref[start + BEHIND * species : start + part, :] = rates_ref[low : low + SUB, :]
        up_ref[halves * part :, :] = hits
        down_ref[halves * part :, :] = hits

    even = lax.rem(lax.axis_index("tile"), 2) == 0

    @pl.when(even)
    def _():
        write(even_ref, odd_ref)

    @pl.when(jnp.logical_not(even))
    def _():
        write(odd_ref, even_ref)


def inner_kernel(dests, length, halves, q_ref, rates_ref, *out_refs):
    species = out_refs[0].shape[0]
    share = length // dests
    me = lax.axis_index("spec")
    for k in range(dests):
        first = lax.rem(me + k, dests) * share
        below = jnp.maximum(first - SUB, 0)
        above = jnp.minimum(first + share, length - SUB)
        for half in range(halves):

            def start(at):
                if at < 0:
                    return below * halves + spot(at + SUB, half, halves)
                if at >= share:
                    return above * halves + spot(at - share, half, halves)
                return first * halves + spot(at, half, halves)

            reach = range(-BEHIND, share + AHEAD)
            rows = [q_ref[pl.ds(start(at), species, stride=length * halves), :] for at in reach]
            rates = [
                with_damp(rates_ref[pl.ds(start(at), 1), :], (species, LANES)) for at in reach
            ]
            for at, value in enumerate(two_sweeps(rows, rates)):
                place = (at * halves + half) * LANES
                out_refs[k][:, place : place + LANES] = value.astype(jnp.bfloat16)


def edge_kernel(
    dests, early, late, length, halves, even_ref, odd_ref, hits_ref, q_ref, rates_ref, *refs
):
    out_refs, refs = refs[len(late) : 2 * len(late)], refs[2 * len(late) :]
    small_refs, (to_even_ref, to_odd_ref, known_ref) = refs[: len(early)], refs[len(early) :]
    species, cells = out_refs[0].shape
    part = BEHIND * species + SUB
    reach = BEHIND + AHEAD
    me = lax.axis_index("spec")
    even = lax.rem(lax.axis_index("tile"), 2) == 0
    own, from_even, from_odd = hits_ref[...], even_ref[halves * part :, :], odd_ref[halves * part :, :]
    known_ref[...] = own + from_even + from_odd
    to_even_ref[...] = from_odd
    to_odd_ref[...] = from_even

    def message(behind, at, size):
        a, b = odd_ref[at : at + size, :], even_ref[at : at + size, :]
        return jnp.where(even, a, b) if behind else jnp.where(even, b, a)

    def row(at, half):
        return q_ref[pl.ds(spot(at, half, halves), species, stride=length * halves), :]

    def rates_of(values):
        return [with_damp(value, (species, LANES)) for value in values]

    tops, bottoms = [], []
    for half in range(halves):
        base = half * part
        behind = [message(True, base + j * species, species) for j in range(BEHIND)]
        ahead = [message(False, base + j * species, species) for j in range(AHEAD)]
        before = message(True, base + BEHIND * species, SUB)
        after = message(False, base + BEHIND * species, SUB)

        def own_rates(first):
            places = [spot(first + j, half, halves) for j in range(reach)]
            return [rates_ref[at : at + 1, :] for at in places]

        tops.append(
            two_sweeps(
                behind + [row(j, half) for j in range(reach)],
                rates_of([before[SUB - BEHIND + j :][:1] for j in range(BEHIND)] + own_rates(0)),
            )
        )
        bottoms.append(
            two_sweeps(
                [row(length - reach + j, half) for j in range(reach)] + ahead,
                rates_of(own_rates(length - reach) + [after[j : j + 1] for j in range(AHEAD)]),
            )
        )
    top = [tops[half][j] for j in range(BEHIND) for half in range(halves)]
    bottom = [bottoms[half][j] for j in range(AHEAD) for half in range(halves)]
    for k, small_ref in zip(early, small_refs):
        low = lax.rem(me + k, dests) == 0
        skip = len(top) - len(bottom)
        for j, value in enumerate(top):
            other = bottom[j - skip] if j >= skip else value
            small_ref[:, j * LANES : (j + 1) * LANES] = jnp.where(low, value, other).astype(
                jnp.bfloat16
            )
    for k, out_ref in zip(late, out_refs):
        dest = lax.rem(me + k, dests)

        @pl.when(dest == 0)
        def _():
            for j, value in enumerate(top):
                out_ref[:, j * LANES : (j + 1) * LANES] = value.astype(jnp.bfloat16)

        @pl.when(dest == dests - 1)
        def _():
            for j, value in enumerate(bottom):
                at = cells + (j - len(bottom)) * LANES
                out_ref[:, at : at + LANES] = value.astype(jnp.bfloat16)


def weight_kernel(w1_ref, w2_ref, after_ref, w1_out, w2_out):
    w1_out[...] = (0.5 * w1_ref[...].astype(jnp.float32)).T.astype(jnp.bfloat16)
    w2_out[...] = (0.5 * w2_ref[...].astype(jnp.float32)).T.astype(jnp.bfloat16)


def chemistry_kernel(
    groups, early, list_ref, w1_ref, w2_ref, w3_ref, known_ref, even_ref, odd_ref, *refs
):
    parts, edges, refs = refs[:groups], refs[groups : groups + len(early)], refs[groups + len(early) :]
    out_ref, share_ref, state_ref, picked_ref, held_ref, done = refs
    species, cells = state_ref.shape[1:]
    slots = list_ref.shape[0]
    blocks = cells // BLK
    me = lax.axis_index("spec")

    def source(k):
        return lax.rem(me - k + groups, groups)

    for k in range(groups):
        state_ref[source(k)] = parts[k][...]
    wide = edges[0].shape[1]
    narrow = wide // BEHIND * AHEAD

    @pl.when(me == 0)
    def _():
        for k, edge in zip(early, edges):
            state_ref[source(k), :, 0:wide] = edge[...]

    @pl.when(me == groups - 1)
    def _():
        for k, edge in zip(early, edges):
            state_ref[source(k), :, cells - narrow :] = edge[:, wide - narrow :]

    hits = known_ref[...] + even_ref[...] + odd_ref[...]
    lane = lax.broadcasted_iota(jnp.int32, hits.shape, 1)
    mine = jnp.where(lane == lax.axis_index("tile"), hits, 0.0)
    held_ref[...] = jnp.sum(mine[0:1], axis=1, keepdims=True) / RECV
    share = pltpu.make_async_copy(held_ref, share_ref, done.at[0])
    share.start()

    def place(j):
        return pl.ds(pl.multiple_of(jnp.minimum(list_ref[j], blocks - 1) * BLK, BLK), BLK)

    for j in range(slots):
        for g in range(groups):
            picked_ref[g * species : (g + 1) * species, j * BLK : (j + 1) * BLK] = state_ref[
                g, :, place(j)
            ].astype(jnp.float32)
    each = 4
    for first in range(0, slots, each):
        x = picked_ref[:, first * BLK : (first + each) * BLK]
        hidden = jnp.dot(w1_ref[...], x.astype(jnp.bfloat16), preferred_element_type=jnp.float32)
        hidden = silu_of_half(hidden).astype(jnp.bfloat16)
        hidden = jnp.dot(w2_ref[...], hidden, preferred_element_type=jnp.float32)
        hidden = silu_of_half(hidden).astype(jnp.bfloat16)
        picked_ref[:, first * BLK : (first + each) * BLK] = x + jnp.dot(
            w3_ref[...], hidden, preferred_element_type=jnp.float32
        )
    for j in range(slots):
        valid = list_ref[j] < blocks
        for g in range(groups):
            fresh = picked_ref[g * species : (g + 1) * species, j * BLK : (j + 1) * BLK]
            now = state_ref[g, :, place(j)].astype(jnp.float32)
            state_ref[g, :, place(j)] = jnp.where(valid, fresh, now).astype(jnp.bfloat16)
    whole = pltpu.make_async_copy(state_ref, out_ref, done.at[1])
    whole.start()
    share.wait()
    whole.wait()


def vmem():
    return pl.BlockSpec(memory_space=pltpu.VMEM)


def anywhere():
    return pl.BlockSpec(memory_space=pl.ANY)


def from_hbm(x):
    return pltpu.with_memory_space_constraint(x, pltpu.HBM)


def cost(us):
    return pl.CostEstimate(flops=int(us * 1e9), bytes_accessed=int(us * 3e6), transcendentals=0)


def shards(
    concentrations, courant, first_weight, middle_weight, last_weight, active_blocks, dest_tile
):
    species, length, cols = concentrations.shape
    dests = lax.axis_size("spec")
    tiles = lax.axis_size("tile")
    cells = length // dests * cols
    slots = active_blocks.shape[-1]
    halves = cols // LANES
    f32, bf16 = jnp.float32, jnp.bfloat16
    params = pltpu.CompilerParams(vmem_limit_bytes=VMEM_BYTES)
    size = halves * (BEHIND * species + SUB) + SUB
    flag = jax.ShapeDtypeStruct((SUB, LANES), f32)
    block = jax.ShapeDtypeStruct((species, cells), bf16)

    to_even, to_odd, hits, field, rates, listing = pl.pallas_call(
        functools.partial(pack_kernel, length, halves, cells // BLK),
        out_shape=[jax.ShapeDtypeStruct((size, LANES), f32)] * 2
        + [
            flag,
            jax.ShapeDtypeStruct((species * length * halves, LANES), f32),
            jax.ShapeDtypeStruct((length * halves, LANES), f32),
            jax.ShapeDtypeStruct((slots,), jnp.int32),
        ],
        in_specs=[anywhere()] * 4,
        out_specs=[vmem()] * 5 + [pl.BlockSpec(memory_space=pltpu.SMEM)],
        scratch_shapes=[
            pltpu.SMEM((slots,), jnp.int32),
            pltpu.SemaphoreType.DMA((4,)),
        ],
        compiler_params=params,
        cost_estimate=cost(1.0),
        name="pack_edges",
    )(
        from_hbm(tiled(concentrations, halves).reshape(species * length * halves, LANES)),
        from_hbm(tiled(courant, halves)),
        from_hbm(active_blocks.reshape(-1)),
        from_hbm(dest_tile.reshape(-1)),
    )
    evens = [(t, t ^ 1) for t in range(tiles)]
    odds = [(t, ((t + 1) ^ 1) - 1) for t in range(tiles)]
    odds = [(t, other % tiles) for t, other in odds]
    from_even = lax.ppermute(to_even, "tile", evens)
    from_odd = lax.ppermute(to_odd, "tile", odds)
    blocks = pl.pallas_call(
        functools.partial(inner_kernel, dests, length, halves),
        out_shape=[block] * dests,
        in_specs=[vmem()] * 2,
        out_specs=[vmem()] * dests,
        compiler_params=params,
        cost_estimate=cost(1.0),
        name="inner_rows",
    )(field, rates)
    def ring(k, x):
        return lax.ppermute(x, "spec", [(s, (s + k) % dests) for s in range(dests)])

    order = [k for k in (2, 1) if k < dests] + list(range(3, dests))
    early, late = order[: dests // 2], [0] + order[dests // 2 :]
    received = {k: ring(k, blocks[k]) for k in early}
    edge = jax.ShapeDtypeStruct((species, BEHIND * cols), bf16)
    outs = pl.pallas_call(
        functools.partial(edge_kernel, dests, early, late, length, halves),
        out_shape=[block] * len(late) + [edge] * len(early) + [flag] * 3,
        in_specs=[vmem()] * (5 + len(late)),
        out_specs=[vmem()] * (dests + 3),
        input_output_aliases={5 + i: i for i in range(len(late))},
        compiler_params=params,
        cost_estimate=cost(0.1),
        name="edge_rows",
    )(from_even, from_odd, hits, field, rates, *[blocks[k] for k in late])
    full, edges, (to_even, to_odd, known) = outs[: len(late)], outs[len(late) : dests], outs[dests:]
    received |= {k: ring(k, x) if k else x for k, x in zip(late, full)}
    edges = [ring(k, x) for k, x in zip(early, edges)]
    from_even = lax.ppermute(to_even, "tile", evens)
    from_odd = lax.ppermute(to_odd, "tile", odds)
    w1, w2 = pl.pallas_call(
        weight_kernel,
        out_shape=[jax.ShapeDtypeStruct(w.shape[::-1], bf16) for w in (first_weight, middle_weight)],
        in_specs=[vmem(), vmem(), anywhere()],
        out_specs=[vmem()] * 2,
        compiler_params=params,
        cost_estimate=cost(0.5),
        name="halved_weights",
    )(first_weight, middle_weight, known)
    out, load_share = pl.pallas_call(
        functools.partial(chemistry_kernel, dests, early),
        out_shape=[
            jax.ShapeDtypeStruct((dests, species, cells), bf16),
            jax.ShapeDtypeStruct((1, 1), f32),
        ],
        in_specs=[pl.BlockSpec(memory_space=pltpu.SMEM)] + [vmem()] * (6 + dests + len(early)),
        out_specs=[anywhere()] * 2,
        scratch_shapes=[
            pltpu.VMEM((dests, species, cells), bf16),
            pltpu.VMEM((dests * species, slots * BLK), f32),
            pltpu.VMEM((1, 1), f32),
            pltpu.SemaphoreType.DMA((2,)),
        ],
        compiler_params=params,
        cost_estimate=cost(4.0),
        name="chemistry",
    )(
        listing,
        w1,
        w2,
        last_weight.T,
        known,
        from_even,
        from_odd,
        *[received[k] for k in range(dests)],
        *edges,
    )
    return out.reshape(dests * species, cells), load_share


def solution(mesh):
    in_specs = (
        P("spec", "tile", None),
        P("tile", None),
        P(),
        P(),
        P(),
        P("tile", "spec", None),
        P("tile", "spec", None),
    )
    out_specs = (P(None, ("tile", "spec")), P("tile", "spec"))
    return jax.shard_map(shards, mesh=mesh, in_specs=in_specs, out_specs=out_specs, check_vma=False)
```

```python
import functools

import jax
import jax.numpy as jnp
from jax import lax
from jax.experimental import pallas as pl
from jax.experimental.pallas import tpu as pltpu
from jax.sharding import PartitionSpec as P

BLK = 128
RECV = 8
LANES = 128
SUB = 8
BEHIND = 4
AHEAD = 2
VMEM_BYTES = 16 * 1024 * 1024


def silu_of_half(half):
    return half + half * jnp.tanh(half)


def sweep_rows(rows, rates):
    diffs = [b - a for a, b in zip(rows[:-1], rows[1:])]
    fluxes = []
    for at in range(1, len(rows) - 1):
        left, right = diffs[at - 1], diffs[at]
        slope = jnp.maximum(jnp.minimum(left, right), 0.0) + jnp.minimum(
            jnp.maximum(left, right), 0.0
        )
        rate, damp = rates[at]
        fluxes.append(rate * (rows[at] + damp * slope))
    return [rows[at] - fluxes[at - 1] + fluxes[at - 2] for at in range(2, len(rows) - 1)]


def two_sweeps(rows, rates):
    once = sweep_rows(rows, rates)
    return sweep_rows(once, rates[2:-1])


def with_damp(rate, shape):
    rate = jnp.broadcast_to(rate, shape)
    return rate, 0.5 - 0.5 * rate


def tiled(x, halves):
    lead, (rows, cols) = x.shape[:-2], x.shape[-2:]
    x = x.reshape(lead + (rows // SUB, SUB, halves, LANES))
    axes = tuple(range(len(lead)))
    x = x.transpose(axes + tuple(len(lead) + a for a in (0, 2, 1, 3)))
    return x.reshape(lead + (rows * halves, LANES))


def spot(at, half, halves):
    return (at // SUB * halves + half) * SUB + at % SUB


def pack_kernel(
    length, halves, blocks, q_in, rates_in, list_in, dest_in,
    even_ref, odd_ref, hits_ref, q_ref, rates_ref, list_ref, dest_ref, arrived,
):
    pairs = [(q_in, q_ref), (rates_in, rates_ref), (list_in, list_ref), (dest_in, dest_ref)]
    copies = [
        pltpu.make_async_copy(source, target, arrived.at[i])
        for i, (source, target) in enumerate(pairs)
    ]
    for copy in copies:
        copy.start()
    species = q_ref.shape[0] // (length * halves)
    part = BEHIND * species + SUB

    def row(at, half):
        return q_ref[pl.ds(spot(at, half, halves), species, stride=length * halves), :]

    copies[2].wait()
    copies[3].wait()
    lane = lax.broadcasted_iota(jnp.int32, (SUB, LANES), 1)
    hits = jnp.zeros((SUB, LANES), jnp.float32)
    for j in range(list_ref.shape[0]):
        target = jnp.where(list_ref[j] < blocks, dest_ref[j], -1)
        hits = hits + jnp.where(lane == target, 1.0, 0.0)
    hits_ref[...] = hits
    copies[1].wait()
    copies[0].wait()

    def write(up_ref, down_ref):
        for half in range(halves):
            start = half * part
            for j in range(BEHIND):
                up_ref[start + j * species : start + (j + 1) * species, :] = row(
                    length - BEHIND + j, half
                )
            for j in range(AHEAD):
                down_ref[start + j * species : start + (j + 1) * species, :] = row(j, half)
            for j in range(AHEAD, BEHIND):
                down_ref[start + j * species : start + (j + 1) * species, :] = jnp.zeros(
                    (species, LANES), jnp.float32
                )
            high, low = spot(length - SUB, half, halves), spot(0, half, halves)
            up_ref[start + BEHIND * species : start + part, :] = rates_ref[high : high + SUB, :]
            down_ref[start + BEHIND * species : start + part, :] = rates_ref[low : low + SUB, :]
        up_ref[halves * part :, :] = hits
        down_ref[halves * part :, :] = hits

    even = lax.rem(lax.axis_index("tile"), 2) == 0

    @pl.when(even)
    def _():
        write(even_ref, odd_ref)

    @pl.when(jnp.logical_not(even))
    def _():
        write(odd_ref, even_ref)


def inner_kernel(dests, length, halves, q_ref, rates_ref, out_ref):
    species = out_ref.shape[1]
    share = length // dests
    for dest in range(dests):
        places = [
            min(max(dest * share + at, 0), length - 1) for at in range(-BEHIND, share + AHEAD)
        ]
        for half in range(halves):
            starts = [spot(at, half, halves) for at in places]
            rows = [q_ref[pl.ds(at, species, stride=length * halves), :] for at in starts]
            rates = [with_damp(rates_ref[at : at + 1, :], (species, LANES)) for at in starts]
            for at, value in enumerate(two_sweeps(rows, rates)):
                place = (at * halves + half) * LANES
                out_ref[dest, :, place : place + LANES] = value.astype(jnp.bfloat16)


def edge_kernel(
    length, halves, even_ref, odd_ref, hits_ref, q_ref, rates_ref, inner_ref, out_ref,
    to_even_ref, to_odd_ref, known_ref,
):
    dests, species, cells = out_ref.shape
    out_ref[...] = inner_ref[...]
    part = BEHIND * species + SUB
    reach = BEHIND + AHEAD
    even = lax.rem(lax.axis_index("tile"), 2) == 0
    own, from_even, from_odd = hits_ref[...], even_ref[halves * part :, :], odd_ref[halves * part :, :]
    known_ref[...] = own + from_even + from_odd
    to_even_ref[...] = from_odd
    to_odd_ref[...] = from_even

    def message(behind, at, size):
        a, b = odd_ref[at : at + size, :], even_ref[at : at + size, :]
        return jnp.where(even, a, b) if behind else jnp.where(even, b, a)

    def row(at, half):
        return q_ref[pl.ds(spot(at, half, halves), species, stride=length * halves), :]

    def rates_of(values):
        return [with_damp(value, (species, LANES)) for value in values]

    tops, bottoms = [], []
    for half in range(halves):
        base = half * part
        behind = [message(True, base + j * species, species) for j in range(BEHIND)]
        ahead = [message(False, base + j * species, species) for j in range(AHEAD)]
        before = message(True, base + BEHIND * species, SUB)
        after = message(False, base + BEHIND * species, SUB)

        def own_rates(first):
            places = [spot(first + j, half, halves) for j in range(reach)]
            return [rates_ref[at : at + 1, :] for at in places]

        tops.append(
            two_sweeps(
                behind + [row(j, half) for j in range(reach)],
                rates_of([before[SUB - BEHIND + j :][:1] for j in range(BEHIND)] + own_rates(0)),
            )
        )
        bottoms.append(
            two_sweeps(
                [row(length - reach + j, half) for j in range(reach)] + ahead,
                rates_of(own_rates(length - reach) + [after[j : j + 1] for j in range(AHEAD)]),
            )
        )
    for half in range(halves):
        for j, value in enumerate(tops[half]):
            at = (j * halves + half) * LANES
            out_ref[0, :, at : at + LANES] = value.astype(jnp.bfloat16)
        for j, value in enumerate(bottoms[half]):
            at = cells + ((j - AHEAD) * halves + half) * LANES
            out_ref[dests - 1, :, at : at + LANES] = value.astype(jnp.bfloat16)


def weight_kernel(w1_ref, w2_ref, list_ref, after_ref, w1_out, w2_out, list_out):
    list_out[...] = list_ref[...]
    w1_out[...] = (0.5 * w1_ref[...].astype(jnp.float32)).T.astype(jnp.bfloat16)
    w2_out[...] = (0.5 * w2_ref[...].astype(jnp.float32)).T.astype(jnp.bfloat16)


def chemistry_kernel(
    list_ref, w1_ref, w2_ref, w3_ref, known_ref, even_ref, odd_ref, cells_ref,
    out_ref, share_ref, state_ref, picked_ref, held_ref, done,
):
    groups, species, cells = state_ref.shape
    slots = list_ref.shape[0]
    blocks = cells // BLK
    state_ref[...] = cells_ref[...]
    hits = known_ref[...] + even_ref[...] + odd_ref[...]
    lane = lax.broadcasted_iota(jnp.int32, hits.shape, 1)
    mine = jnp.where(lane == lax.axis_index("tile"), hits, 0.0)
    held_ref[...] = jnp.sum(mine[0:1], axis=1, keepdims=True) / RECV
    share = pltpu.make_async_copy(held_ref, share_ref, done.at[0])
    share.start()

    def place(j):
        return pl.ds(pl.multiple_of(jnp.minimum(list_ref[j], blocks - 1) * BLK, BLK), BLK)

    for j in range(slots):
        for g in range(groups):
            picked_ref[g * species : (g + 1) * species, j * BLK : (j + 1) * BLK] = state_ref[
                g, :, place(j)
            ].astype(jnp.float32)
    each = 4
    for first in range(0, slots, each):
        x = picked_ref[:, first * BLK : (first + each) * BLK]
        hidden = jnp.dot(w1_ref[...], x.astype(jnp.bfloat16), preferred_element_type=jnp.float32)
        hidden = silu_of_half(hidden).astype(jnp.bfloat16)
        hidden = jnp.dot(w2_ref[...], hidden, preferred_element_type=jnp.float32)
        hidden = silu_of_half(hidden).astype(jnp.bfloat16)
        picked_ref[:, first * BLK : (first + each) * BLK] = x + jnp.dot(
            w3_ref[...], hidden, preferred_element_type=jnp.float32
        )
    for j in range(slots):
        valid = list_ref[j] < blocks
        for g in range(groups):
            fresh = picked_ref[g * species : (g + 1) * species, j * BLK : (j + 1) * BLK]
            now = state_ref[g, :, place(j)].astype(jnp.float32)
            state_ref[g, :, place(j)] = jnp.where(valid, fresh, now).astype(jnp.bfloat16)
    whole = pltpu.make_async_copy(state_ref, out_ref, done.at[1])
    whole.start()
    share.wait()
    whole.wait()


def vmem():
    return pl.BlockSpec(memory_space=pltpu.VMEM)


def anywhere():
    return pl.BlockSpec(memory_space=pl.ANY)


def from_hbm(x):
    return pltpu.with_memory_space_constraint(x, pltpu.HBM)


def cost(us):
    return pl.CostEstimate(flops=int(us * 1e9), bytes_accessed=int(us * 3e6), transcendentals=0)


def shards(
    concentrations, courant, first_weight, middle_weight, last_weight, active_blocks, dest_tile
):
    species, length, cols = concentrations.shape
    dests = lax.axis_size("spec")
    tiles = lax.axis_size("tile")
    cells = length // dests * cols
    slots = active_blocks.shape[-1]
    halves = cols // LANES
    f32, bf16 = jnp.float32, jnp.bfloat16
    params = pltpu.CompilerParams(vmem_limit_bytes=VMEM_BYTES)
    size = halves * (BEHIND * species + SUB) + SUB
    flag = jax.ShapeDtypeStruct((SUB, LANES), f32)

    to_even, to_odd, hits, field, rates = pl.pallas_call(
        functools.partial(pack_kernel, length, halves, cells // BLK),
        out_shape=[jax.ShapeDtypeStruct((size, LANES), f32)] * 2
        + [
            flag,
            jax.ShapeDtypeStruct((species * length * halves, LANES), f32),
            jax.ShapeDtypeStruct((length * halves, LANES), f32),
        ],
        in_specs=[anywhere()] * 4,
        out_specs=[vmem()] * 5,
        scratch_shapes=[
            pltpu.SMEM((slots,), jnp.int32),
            pltpu.SMEM((slots,), jnp.int32),
            pltpu.SemaphoreType.DMA((4,)),
        ],
        compiler_params=params,
        cost_estimate=cost(1.0),
        name="pack_edges",
    )(
        from_hbm(tiled(concentrations, halves).reshape(species * length * halves, LANES)),
        from_hbm(tiled(courant, halves)),
        from_hbm(active_blocks.reshape(-1)),
        from_hbm(dest_tile.reshape(-1)),
    )
    evens = [(t, t ^ 1) for t in range(tiles)]
    odds = [(t, ((t + 1) ^ 1) - 1) for t in range(tiles)]
    odds = [(t, other % tiles) for t, other in odds]
    from_even = lax.ppermute(to_even, "tile", evens)
    from_odd = lax.ppermute(to_odd, "tile", odds)
    every = jax.ShapeDtypeStruct((dests, species, cells), bf16)
    inner = pl.pallas_call(
        functools.partial(inner_kernel, dests, length, halves),
        out_shape=every,
        in_specs=[vmem()] * 2,
        out_specs=vmem(),
        compiler_params=params,
        cost_estimate=cost(1.0),
        name="inner_rows",
    )(field, rates)
    swept, to_even, to_odd, known = pl.pallas_call(
        functools.partial(edge_kernel, length, halves),
        out_shape=[every] + [flag] * 3,
        in_specs=[vmem()] * 6,
        out_specs=[vmem()] * 4,
        compiler_params=params,
        cost_estimate=cost(0.1),
        name="edge_rows",
    )(from_even, from_odd, hits, field, rates, inner)
    gathered = lax.all_to_all(swept, "spec", split_axis=0, concat_axis=0, tiled=True)
    from_even = lax.ppermute(to_even, "tile", evens)
    from_odd = lax.ppermute(to_odd, "tile", odds)
    w1, w2, listing = pl.pallas_call(
        weight_kernel,
        out_shape=[jax.ShapeDtypeStruct(w.shape[::-1], bf16) for w in (first_weight, middle_weight)]
        + [jax.ShapeDtypeStruct((1, slots), jnp.int32)],
        in_specs=[vmem()] * 3 + [anywhere()],
        out_specs=[vmem()] * 3,
        compiler_params=params,
        cost_estimate=cost(0.5),
        name="halved_weights",
    )(first_weight, middle_weight, active_blocks.reshape(1, slots), known)
    out, load_share = pl.pallas_call(
        chemistry_kernel,
        out_shape=[every, jax.ShapeDtypeStruct((1, 1), f32)],
        in_specs=[pl.BlockSpec(memory_space=pltpu.SMEM)] + [vmem()] * 7,
        out_specs=[anywhere()] * 2,
        scratch_shapes=[
            pltpu.VMEM((dests, species, cells), bf16),
            pltpu.VMEM((dests * species, slots * BLK), f32),
            pltpu.VMEM((1, 1), f32),
            pltpu.SemaphoreType.DMA((2,)),
        ],
        compiler_params=params,
        cost_estimate=cost(4.0),
        name="chemistry",
    )(
        listing.reshape(-1),
        w1,
        w2,
        last_weight.T,
        known,
        from_even,
        from_odd,
        gathered,
    )
    return out.reshape(dests * species, cells), load_share


def solution(mesh):
    in_specs = (
        P("spec", "tile", None),
        P("tile", None),
        P(),
        P(),
        P(),
        P("tile", "spec", None),
        P("tile", "spec", None),
    )
    out_specs = (P(None, ("tile", "spec")), P("tile", "spec"))
    return jax.shard_map(shards, mesh=mesh, in_specs=in_specs, out_specs=out_specs, check_vma=False)
```

```python
import functools

import jax
import jax.numpy as jnp
from jax import lax
from jax.experimental import pallas as pl
from jax.experimental.pallas import tpu as pltpu
from jax.sharding import PartitionSpec as P

BLK = 128
RECV = 8
LANES = 128
SUB = 8
BEHIND = 4
AHEAD = 2
VMEM_BYTES = 16 * 1024 * 1024


def silu_of_half(half):
    return half + half * jnp.tanh(half)


def sweep_rows(rows, rates):
    diffs = [b - a for a, b in zip(rows[:-1], rows[1:])]
    fluxes = []
    for at in range(1, len(rows) - 1):
        left, right = diffs[at - 1], diffs[at]
        slope = jnp.maximum(jnp.minimum(left, right), 0.0) + jnp.minimum(
            jnp.maximum(left, right), 0.0
        )
        rate, damp = rates[at]
        fluxes.append(rate * (rows[at] + damp * slope))
    return [rows[at] - fluxes[at - 1] + fluxes[at - 2] for at in range(2, len(rows) - 1)]


def two_sweeps(rows, rates):
    once = sweep_rows(rows, rates)
    return sweep_rows(once, rates[2:-1])


def with_damp(rate, shape):
    rate = jnp.broadcast_to(rate, shape)
    return rate, 0.5 - 0.5 * rate


def tiled(x, halves):
    lead, (rows, cols) = x.shape[:-2], x.shape[-2:]
    x = x.reshape(lead + (rows // SUB, SUB, halves, LANES))
    axes = tuple(range(len(lead)))
    x = x.transpose(axes + tuple(len(lead) + a for a in (0, 2, 1, 3)))
    return x.reshape(lead + (rows * halves, LANES))


def spot(at, half, halves):
    return (at // SUB * halves + half) * SUB + at % SUB


def pack_kernel(
    length, halves, blocks, q_in, rates_in, list_in, dest_in,
    even_ref, odd_ref, hits_ref, q_ref, rates_ref, list_ref, dest_ref, arrived,
):
    pairs = [(q_in, q_ref), (rates_in, rates_ref), (list_in, list_ref), (dest_in, dest_ref)]
    copies = [
        pltpu.make_async_copy(source, target, arrived.at[i])
        for i, (source, target) in enumerate(pairs)
    ]
    for copy in copies:
        copy.start()
    species = q_ref.shape[0] // (length * halves)
    part = BEHIND * species + SUB

    def row(at, half):
        return q_ref[pl.ds(spot(at, half, halves), species, stride=length * halves), :]

    copies[2].wait()
    copies[3].wait()
    lane = lax.broadcasted_iota(jnp.int32, (SUB, LANES), 1)
    hits = jnp.zeros((SUB, LANES), jnp.float32)
    for j in range(list_ref.shape[0]):
        target = jnp.where(list_ref[j] < blocks, dest_ref[j], -1)
        hits = hits + jnp.where(lane == target, 1.0, 0.0)
    hits_ref[...] = hits
    copies[1].wait()
    copies[0].wait()

    def write(up_ref, down_ref):
        for half in range(halves):
            start = half * part
            for j in range(BEHIND):
                up_ref[start + j * species : start + (j + 1) * species, :] = row(
                    length - BEHIND + j, half
                )
            for j in range(AHEAD):
                down_ref[start + j * species : start + (j + 1) * species, :] = row(j, half)
            for j in range(AHEAD, BEHIND):
                down_ref[start + j * species : start + (j + 1) * species, :] = jnp.zeros(
                    (species, LANES), jnp.float32
                )
            high, low = spot(length - SUB, half, halves), spot(0, half, halves)
            up_ref[start + BEHIND * species : start + part, :] = rates_ref[high : high + SUB, :]
            down_ref[start + BEHIND * species : start + part, :] = rates_ref[low : low + SUB, :]
        up_ref[halves * part :, :] = hits
        down_ref[halves * part :, :] = hits

    even = lax.rem(lax.axis_index("tile"), 2) == 0

    @pl.when(even)
    def _():
        write(even_ref, odd_ref)

    @pl.when(jnp.logical_not(even))
    def _():
        write(odd_ref, even_ref)


def inner_kernel(dests, length, halves, q_ref, rates_ref, *out_refs):
    species = out_refs[0].shape[0]
    share = length // dests
    me = lax.axis_index("spec")
    for k in range(dests):
        first = lax.rem(me + k, dests) * share
        below = jnp.maximum(first - SUB, 0)
        above = jnp.minimum(first + share, length - SUB)
        for half in range(halves):

            def start(at):
                if at < 0:
                    return below * halves + spot(at + SUB, half, halves)
                if at >= share:
                    return above * halves + spot(at - share, half, halves)
                return first * halves + spot(at, half, halves)

            reach = range(-BEHIND, share + AHEAD)
            rows = [q_ref[pl.ds(start(at), species, stride=length * halves), :] for at in reach]
            rates = [
                with_damp(rates_ref[pl.ds(start(at), 1), :], (species, LANES)) for at in reach
            ]
            for at, value in enumerate(two_sweeps(rows, rates)):
                place = (at * halves + half) * LANES
                out_refs[k][:, place : place + LANES] = value.astype(jnp.bfloat16)


def edge_kernel(
    dests, length, halves, odd_ref, even_ref, hits_ref, q_ref, rates_ref, *refs
):
    in_refs, out_refs, (to_even_ref, to_odd_ref, known_ref) = (
        refs[:dests], refs[dests : 2 * dests], refs[2 * dests :]
    )
    species, cells = out_refs[0].shape
    me = lax.axis_index("spec")
    part = BEHIND * species + SUB
    reach = BEHIND + AHEAD
    even = lax.rem(lax.axis_index("tile"), 2) == 0
    own, from_even, from_odd = hits_ref[...], even_ref[halves * part :, :], odd_ref[halves * part :, :]
    known_ref[...] = own + from_even + from_odd
    to_even_ref[...] = from_odd
    to_odd_ref[...] = from_even

    def message(behind, at, size):
        a, b = odd_ref[at : at + size, :], even_ref[at : at + size, :]
        return jnp.where(even, a, b) if behind else jnp.where(even, b, a)

    def row(at, half):
        return q_ref[pl.ds(spot(at, half, halves), species, stride=length * halves), :]

    def rates_of(values):
        return [with_damp(value, (species, LANES)) for value in values]

    tops, bottoms = [], []
    for half in range(halves):
        base = half * part
        behind = [message(True, base + j * species, species) for j in range(BEHIND)]
        ahead = [message(False, base + j * species, species) for j in range(AHEAD)]
        before = message(True, base + BEHIND * species, SUB)
        after = message(False, base + BEHIND * species, SUB)

        def own_rates(first):
            places = [spot(first + j, half, halves) for j in range(reach)]
            return [rates_ref[at : at + 1, :] for at in places]

        tops.append(
            two_sweeps(
                behind + [row(j, half) for j in range(reach)],
                rates_of([before[SUB - BEHIND + j :][:1] for j in range(BEHIND)] + own_rates(0)),
            )
        )
        bottoms.append(
            two_sweeps(
                [row(length - reach + j, half) for j in range(reach)] + ahead,
                rates_of(own_rates(length - reach) + [after[j : j + 1] for j in range(AHEAD)]),
            )
        )
    for k, (in_ref, out_ref) in enumerate(zip(in_refs, out_refs)):
        dest = lax.rem(me + k, dests)
        out_ref[...] = in_ref[...]

        @pl.when(dest == 0)
        def _():
            for half in range(halves):
                for j, value in enumerate(tops[half]):
                    at = (j * halves + half) * LANES
                    out_ref[:, at : at + LANES] = value.astype(jnp.bfloat16)

        @pl.when(dest == dests - 1)
        def _():
            for half in range(halves):
                for j, value in enumerate(bottoms[half]):
                    at = cells + ((j - AHEAD) * halves + half) * LANES
                    out_ref[:, at : at + LANES] = value.astype(jnp.bfloat16)


def weight_kernel(w1_ref, w2_ref, list_ref, after_ref, w1_out, w2_out, list_out):
    list_out[...] = list_ref[...]
    w1_out[...] = (0.5 * w1_ref[...].astype(jnp.float32)).T.astype(jnp.bfloat16)
    w2_out[...] = (0.5 * w2_ref[...].astype(jnp.float32)).T.astype(jnp.bfloat16)


def chemistry_kernel(
    groups, list_ref, w1_ref, w2_ref, w3_ref, known_ref, odd_ref, even_ref, *refs
):
    parts, (out_ref, share_ref, state_ref, picked_ref, held_ref, done) = refs[:groups], refs[groups:]
    species, cells = state_ref.shape[1:]
    slots = list_ref.shape[0]
    blocks = cells // BLK
    me = lax.axis_index("spec")
    for k in range(groups):
        state_ref[lax.rem(me - k + groups, groups)] = parts[k][...]
    hits = known_ref[...] + even_ref[...] + odd_ref[...]
    lane = lax.broadcasted_iota(jnp.int32, hits.shape, 1)
    mine = jnp.where(lane == lax.axis_index("tile"), hits, 0.0)
    held_ref[...] = jnp.sum(mine[0:1], axis=1, keepdims=True) / RECV
    share = pltpu.make_async_copy(held_ref, share_ref, done.at[0])
    share.start()

    def place(j):
        return pl.ds(pl.multiple_of(jnp.minimum(list_ref[j], blocks - 1) * BLK, BLK), BLK)

    for j in range(slots):
        for g in range(groups):
            picked_ref[g * species : (g + 1) * species, j * BLK : (j + 1) * BLK] = state_ref[
                g, :, place(j)
            ].astype(jnp.float32)
    each = 4
    for first in range(0, slots, each):
        x = picked_ref[:, first * BLK : (first + each) * BLK]
        hidden = jnp.dot(w1_ref[...], x.astype(jnp.bfloat16), preferred_element_type=jnp.float32)
        hidden = silu_of_half(hidden).astype(jnp.bfloat16)
        hidden = jnp.dot(w2_ref[...], hidden, preferred_element_type=jnp.float32)
        hidden = silu_of_half(hidden).astype(jnp.bfloat16)
        picked_ref[:, first * BLK : (first + each) * BLK] = x + jnp.dot(
            w3_ref[...], hidden, preferred_element_type=jnp.float32
        )
    for j in range(slots):
        valid = list_ref[j] < blocks
        for g in range(groups):
            fresh = picked_ref[g * species : (g + 1) * species, j * BLK : (j + 1) * BLK]
            now = state_ref[g, :, place(j)].astype(jnp.float32)
            state_ref[g, :, place(j)] = jnp.where(valid, fresh, now).astype(jnp.bfloat16)
    whole = pltpu.make_async_copy(state_ref, out_ref, done.at[1])
    whole.start()
    share.wait()
    whole.wait()


def vmem():
    return pl.BlockSpec(memory_space=pltpu.VMEM)


def anywhere():
    return pl.BlockSpec(memory_space=pl.ANY)


def from_hbm(x):
    return pltpu.with_memory_space_constraint(x, pltpu.HBM)


def cost(us):
    return pl.CostEstimate(flops=int(us * 1e9), bytes_accessed=int(us * 3e6), transcendentals=0)


def shards(
    concentrations, courant, first_weight, middle_weight, last_weight, active_blocks, dest_tile
):
    species, length, cols = concentrations.shape
    dests = lax.axis_size("spec")
    tiles = lax.axis_size("tile")
    cells = length // dests * cols
    slots = active_blocks.shape[-1]
    halves = cols // LANES
    f32, bf16 = jnp.float32, jnp.bfloat16
    params = pltpu.CompilerParams(vmem_limit_bytes=VMEM_BYTES)
    size = halves * (BEHIND * species + SUB) + SUB
    flag = jax.ShapeDtypeStruct((SUB, LANES), f32)

    to_even, to_odd, hits, field, rates = pl.pallas_call(
        functools.partial(pack_kernel, length, halves, cells // BLK),
        out_shape=[jax.ShapeDtypeStruct((size, LANES), f32)] * 2
        + [
            flag,
            jax.ShapeDtypeStruct((species * length * halves, LANES), f32),
            jax.ShapeDtypeStruct((length * halves, LANES), f32),
        ],
        in_specs=[anywhere()] * 4,
        out_specs=[vmem()] * 5,
        scratch_shapes=[
            pltpu.SMEM((slots,), jnp.int32),
            pltpu.SMEM((slots,), jnp.int32),
            pltpu.SemaphoreType.DMA((4,)),
        ],
        compiler_params=params,
        cost_estimate=cost(1.0),
        name="pack_edges",
    )(
        from_hbm(tiled(concentrations, halves).reshape(species * length * halves, LANES)),
        from_hbm(tiled(courant, halves)),
        from_hbm(active_blocks.reshape(-1)),
        from_hbm(dest_tile.reshape(-1)),
    )
    evens = [(t, t ^ 1) for t in range(tiles)]
    odds = [(t, ((t + 1) ^ 1) - 1) for t in range(tiles)]
    odds = [(t, other % tiles) for t, other in odds]
    from_odd = lax.ppermute(to_odd, "tile", odds)
    from_even = lax.ppermute(to_even, "tile", evens)
    block = jax.ShapeDtypeStruct((species, cells), bf16)
    blocks = pl.pallas_call(
        functools.partial(inner_kernel, dests, length, halves),
        out_shape=[block] * dests,
        in_specs=[vmem()] * 2,
        out_specs=[vmem()] * dests,
        compiler_params=params,
        cost_estimate=cost(1.0),
        name="inner_rows",
    )(field, rates)
    *blocks, to_even, to_odd, known = pl.pallas_call(
        functools.partial(edge_kernel, dests, length, halves),
        out_shape=[block] * dests + [flag] * 3,
        in_specs=[vmem()] * (5 + dests),
        out_specs=[vmem()] * (dests + 3),
        compiler_params=params,
        cost_estimate=cost(0.1),
        name="edge_rows",
    )(from_odd, from_even, hits, field, rates, *blocks)
    received = [blocks[0]] + [
        lax.ppermute(blocks[k], "spec", [(s, (s + k) % dests) for s in range(dests)])
        for k in range(1, dests)
    ]
    from_odd = lax.ppermute(to_odd, "tile", odds)
    from_even = lax.ppermute(to_even, "tile", evens)
    w1, w2, listing = pl.pallas_call(
        weight_kernel,
        out_shape=[jax.ShapeDtypeStruct(w.shape[::-1], bf16) for w in (first_weight, middle_weight)]
        + [jax.ShapeDtypeStruct((1, slots), jnp.int32)],
        in_specs=[vmem()] * 3 + [anywhere()],
        out_specs=[vmem()] * 3,
        compiler_params=params,
        cost_estimate=cost(0.5),
        name="halved_weights",
    )(first_weight, middle_weight, active_blocks.reshape(1, slots), known)
    out, load_share = pl.pallas_call(
        functools.partial(chemistry_kernel, dests),
        out_shape=[
            jax.ShapeDtypeStruct((dests, species, cells), bf16),
            jax.ShapeDtypeStruct((1, 1), f32),
        ],
        in_specs=[pl.BlockSpec(memory_space=pltpu.SMEM)] + [vmem()] * (6 + dests),
        out_specs=[anywhere()] * 2,
        scratch_shapes=[
            pltpu.VMEM((dests, species, cells), bf16),
            pltpu.VMEM((dests * species, slots * BLK), f32),
            pltpu.VMEM((1, 1), f32),
            pltpu.SemaphoreType.DMA((2,)),
        ],
        compiler_params=params,
        cost_estimate=cost(4.0),
        name="chemistry",
    )(
        listing.reshape(-1),
        w1,
        w2,
        last_weight.T,
        known,
        from_odd,
        from_even,
        *received,
    )
    return out.reshape(dests * species, cells), load_share


def solution(mesh):
    in_specs = (
        P("spec", "tile", None),
        P("tile", None),
        P(),
        P(),
        P(),
        P("tile", "spec", None),
        P("tile", "spec", None),
    )
    out_specs = (P(None, ("tile", "spec")), P("tile", "spec"))
    return jax.shard_map(shards, mesh=mesh, in_specs=in_specs, out_specs=out_specs, check_vma=False)
```

```python
import functools

import jax
import jax.numpy as jnp
from jax import lax
from jax.experimental import pallas as pl
from jax.experimental.pallas import tpu as pltpu
from jax.sharding import PartitionSpec as P

BLK = 128
RECV = 8
LANES = 128
SUB = 8
BEHIND = 4
AHEAD = 2
VMEM_BYTES = 16 * 1024 * 1024


def silu_of_half(half):
    return half + half * jnp.tanh(half)


def sweep_rows(rows, rates):
    diffs = [b - a for a, b in zip(rows[:-1], rows[1:])]
    fluxes = []
    for at in range(1, len(rows) - 1):
        left, right = diffs[at - 1], diffs[at]
        slope = jnp.maximum(jnp.minimum(left, right), 0.0) + jnp.minimum(
            jnp.maximum(left, right), 0.0
        )
        rate, damp = rates[at]
        fluxes.append(rate * (rows[at] + damp * slope))
    return [rows[at] - fluxes[at - 1] + fluxes[at - 2] for at in range(2, len(rows) - 1)]


def two_sweeps(rows, rates):
    once = sweep_rows(rows, rates)
    return sweep_rows(once, rates[2:-1])


def with_damp(rate, shape):
    rate = jnp.broadcast_to(rate, shape)
    return rate, 0.5 - 0.5 * rate


def tiled(x, halves):
    lead, (rows, cols) = x.shape[:-2], x.shape[-2:]
    x = x.reshape(lead + (rows // SUB, SUB, halves, LANES))
    axes = tuple(range(len(lead)))
    x = x.transpose(axes + tuple(len(lead) + a for a in (0, 2, 1, 3)))
    return x.reshape(lead + (rows * halves, LANES))


def spot(at, half, halves):
    return (at // SUB * halves + half) * SUB + at % SUB


def pack_kernel(
    length, halves, blocks, q_in, rates_in, list_in, dest_in,
    even_ref, odd_ref, hits_ref, q_ref, rates_ref, list_ref, dest_ref, arrived,
):
    pairs = [(q_in, q_ref), (rates_in, rates_ref), (list_in, list_ref), (dest_in, dest_ref)]
    copies = [
        pltpu.make_async_copy(source, target, arrived.at[i])
        for i, (source, target) in enumerate(pairs)
    ]
    for copy in copies:
        copy.start()
    species = q_ref.shape[0] // (length * halves)
    part = BEHIND * species + SUB

    def row(at, half):
        return q_ref[pl.ds(spot(at, half, halves), species, stride=length * halves), :]

    copies[2].wait()
    copies[3].wait()
    lane = lax.broadcasted_iota(jnp.int32, hits_ref.shape, 1)
    hits = jnp.zeros(hits_ref.shape, jnp.float32)
    for j in range(list_ref.shape[0]):
        target = jnp.where(list_ref[j] < blocks, dest_ref[j], -1)
        hits = hits + jnp.where(lane == target, 1.0, 0.0)
    hits_ref[...] = hits
    copies[1].wait()
    copies[0].wait()

    def write(up_ref, down_ref):
        for half in range(halves):
            start = half * part
            for j in range(BEHIND):
                up_ref[start + j * species : start + (j + 1) * species, :] = row(
                    length - BEHIND + j, half
                )
            for j in range(AHEAD):
                down_ref[start + j * species : start + (j + 1) * species, :] = row(j, half)
            for j in range(AHEAD, BEHIND):
                down_ref[start + j * species : start + (j + 1) * species, :] = jnp.zeros(
                    (species, LANES), jnp.float32
                )
            high, low = spot(length - SUB, half, halves), spot(0, half, halves)
            up_ref[start + BEHIND * species : start + part, :] = rates_ref[high : high + SUB, :]
            down_ref[start + BEHIND * species : start + part, :] = rates_ref[low : low + SUB, :]

    even = lax.rem(lax.axis_index("tile"), 2) == 0

    @pl.when(even)
    def _():
        write(even_ref, odd_ref)

    @pl.when(jnp.logical_not(even))
    def _():
        write(odd_ref, even_ref)


def inner_kernel(dests, length, halves, q_ref, rates_ref, *out_refs):
    species = out_refs[0].shape[0]
    share = length // dests
    me = lax.axis_index("spec")
    for k in range(dests):
        first = lax.rem(me + k, dests) * share
        below = jnp.maximum(first - SUB, 0)
        above = jnp.minimum(first + share, length - SUB)
        for half in range(halves):

            def start(at):
                if at < 0:
                    return below * halves + spot(at + SUB, half, halves)
                if at >= share:
                    return above * halves + spot(at - share, half, halves)
                return first * halves + spot(at, half, halves)

            reach = range(-BEHIND, share + AHEAD)
            rows = [q_ref[pl.ds(start(at), species, stride=length * halves), :] for at in reach]
            rates = [
                with_damp(rates_ref[pl.ds(start(at), 1), :], (species, LANES)) for at in reach
            ]
            for at, value in enumerate(two_sweeps(rows, rates)):
                place = (at * halves + half) * LANES
                out_refs[k][:, place : place + LANES] = value.astype(jnp.bfloat16)


def edge_kernel(dests, early, late, length, halves, odd_ref, even_ref, q_ref, rates_ref, *refs):
    in_refs, out_refs, small_refs = (
        refs[: len(late)], refs[len(late) : 2 * len(late)], refs[2 * len(late) :]
    )
    species, cells = out_refs[0].shape
    me = lax.axis_index("spec")
    part = BEHIND * species + SUB
    reach = BEHIND + AHEAD
    even = lax.rem(lax.axis_index("tile"), 2) == 0

    def message(behind, at, size):
        a, b = odd_ref[at : at + size, :], even_ref[at : at + size, :]
        return jnp.where(even, a, b) if behind else jnp.where(even, b, a)

    def row(at, half):
        return q_ref[pl.ds(spot(at, half, halves), species, stride=length * halves), :]

    def rates_of(values):
        return [with_damp(value, (species, LANES)) for value in values]

    tops, bottoms = [], []
    for half in range(halves):
        base = half * part
        behind = [message(True, base + j * species, species) for j in range(BEHIND)]
        ahead = [message(False, base + j * species, species) for j in range(AHEAD)]
        before = message(True, base + BEHIND * species, SUB)
        after = message(False, base + BEHIND * species, SUB)

        def own_rates(first):
            places = [spot(first + j, half, halves) for j in range(reach)]
            return [rates_ref[at : at + 1, :] for at in places]

        tops.append(
            two_sweeps(
                behind + [row(j, half) for j in range(reach)],
                rates_of([before[SUB - BEHIND + j :][:1] for j in range(BEHIND)] + own_rates(0)),
            )
        )
        bottoms.append(
            two_sweeps(
                [row(length - reach + j, half) for j in range(reach)] + ahead,
                rates_of(own_rates(length - reach) + [after[j : j + 1] for j in range(AHEAD)]),
            )
        )
    for k, small_ref in zip(early, small_refs):
        low = lax.rem(me + k, dests) == 0
        for half in range(halves):
            for j in range(BEHIND):
                value = tops[half][j]
                if j >= BEHIND - AHEAD:
                    value = jnp.where(low, value, bottoms[half][j - BEHIND + AHEAD])
                at = (j * halves + half) * LANES
                small_ref[:, at : at + LANES] = value.astype(jnp.bfloat16)
    for k, in_ref, out_ref in zip(late, in_refs, out_refs):
        dest = lax.rem(me + k, dests)
        out_ref[...] = in_ref[...]

        @pl.when(dest == 0)
        def _():
            for half in range(halves):
                for j, value in enumerate(tops[half]):
                    at = (j * halves + half) * LANES
                    out_ref[:, at : at + LANES] = value.astype(jnp.bfloat16)

        @pl.when(dest == dests - 1)
        def _():
            for half in range(halves):
                for j, value in enumerate(bottoms[half]):
                    at = cells + ((j - AHEAD) * halves + half) * LANES
                    out_ref[:, at : at + LANES] = value.astype(jnp.bfloat16)


def weight_kernel(w1_ref, w2_ref, list_ref, after_ref, w1_out, w2_out, list_out):
    list_out[...] = list_ref[...]
    w1_out[...] = (0.5 * w1_ref[...].astype(jnp.float32)).T.astype(jnp.bfloat16)
    w2_out[...] = (0.5 * w2_ref[...].astype(jnp.float32)).T.astype(jnp.bfloat16)


def chemistry_kernel(groups, early, list_ref, w1_ref, w2_ref, w3_ref, hits_in, *refs):
    parts, edges, refs = refs[:groups], refs[groups : groups + len(early)], refs[groups + len(early) :]
    out_ref, share_ref, state_ref, picked_ref, hits_ref, held_ref, done = refs
    species, cells = state_ref.shape[1:]
    slots = list_ref.shape[0]
    blocks = cells // BLK
    me = lax.axis_index("spec")

    def source(k):
        return lax.rem(me - k + groups, groups)

    for k in range(groups):
        state_ref[source(k)] = parts[k][...]
    wide = edges[0].shape[1]
    narrow = wide // BEHIND * AHEAD

    @pl.when(me == 0)
    def _():
        for k, edge in zip(early, edges):
            state_ref[source(k), :, 0:wide] = edge[...]

    @pl.when(me == groups - 1)
    def _():
        for k, edge in zip(early, edges):
            state_ref[source(k), :, cells - narrow :] = edge[:, wide - narrow :]

    naming = pltpu.make_async_copy(hits_in, hits_ref, done.at[2])
    naming.start()

    def place(j):
        return pl.ds(pl.multiple_of(jnp.minimum(list_ref[j], blocks - 1) * BLK, BLK), BLK)

    for j in range(slots):
        for g in range(groups):
            picked_ref[g * species : (g + 1) * species, j * BLK : (j + 1) * BLK] = state_ref[
                g, :, place(j)
            ].astype(jnp.float32)
    each = 4
    for first in range(0, slots, each):
        x = picked_ref[:, first * BLK : (first + each) * BLK]
        hidden = jnp.dot(w1_ref[...], x.astype(jnp.bfloat16), preferred_element_type=jnp.float32)
        hidden = silu_of_half(hidden).astype(jnp.bfloat16)
        hidden = jnp.dot(w2_ref[...], hidden, preferred_element_type=jnp.float32)
        hidden = silu_of_half(hidden).astype(jnp.bfloat16)
        picked_ref[:, first * BLK : (first + each) * BLK] = x + jnp.dot(
            w3_ref[...], hidden, preferred_element_type=jnp.float32
        )
    for j in range(slots):
        valid = list_ref[j] < blocks
        for g in range(groups):
            fresh = picked_ref[g * species : (g + 1) * species, j * BLK : (j + 1) * BLK]
            now = state_ref[g, :, place(j)].astype(jnp.float32)
            state_ref[g, :, place(j)] = jnp.where(valid, fresh, now).astype(jnp.bfloat16)
    whole = pltpu.make_async_copy(state_ref, out_ref, done.at[1])
    whole.start()
    naming.wait()
    lane = lax.broadcasted_iota(jnp.int32, hits_ref.shape, 1)
    mine = jnp.where(lane == lax.axis_index("tile"), hits_ref[...], 0.0)
    mine = jnp.sum(mine, axis=0, keepdims=True)
    held_ref[...] = jnp.sum(mine, axis=1, keepdims=True) / RECV
    share = pltpu.make_async_copy(held_ref, share_ref, done.at[0])
    share.start()
    share.wait()
    whole.wait()


def vmem():
    return pl.BlockSpec(memory_space=pltpu.VMEM)


def anywhere():
    return pl.BlockSpec(memory_space=pl.ANY)


def from_hbm(x):
    return pltpu.with_memory_space_constraint(x, pltpu.HBM)


def cost(us):
    return pl.CostEstimate(flops=int(us * 1e9), bytes_accessed=int(us * 3e6), transcendentals=0)


def shards(
    concentrations, courant, first_weight, middle_weight, last_weight, active_blocks, dest_tile
):
    species, length, cols = concentrations.shape
    dests = lax.axis_size("spec")
    tiles = lax.axis_size("tile")
    cells = length // dests * cols
    slots = active_blocks.shape[-1]
    halves = cols // LANES
    f32, bf16 = jnp.float32, jnp.bfloat16
    params = pltpu.CompilerParams(vmem_limit_bytes=VMEM_BYTES)
    size = halves * (BEHIND * species + SUB)
    flag = jax.ShapeDtypeStruct((1, LANES), f32)

    to_even, to_odd, hits, field, rates = pl.pallas_call(
        functools.partial(pack_kernel, length, halves, cells // BLK),
        out_shape=[jax.ShapeDtypeStruct((size, LANES), f32)] * 2
        + [
            flag,
            jax.ShapeDtypeStruct((species * length * halves, LANES), f32),
            jax.ShapeDtypeStruct((length * halves, LANES), f32),
        ],
        in_specs=[anywhere()] * 4,
        out_specs=[vmem()] * 5,
        scratch_shapes=[
            pltpu.SMEM((slots,), jnp.int32),
            pltpu.SMEM((slots,), jnp.int32),
            pltpu.SemaphoreType.DMA((4,)),
        ],
        compiler_params=params,
        cost_estimate=cost(1.0),
        name="pack_edges",
    )(
        from_hbm(tiled(concentrations, halves).reshape(species * length * halves, LANES)),
        from_hbm(tiled(courant, halves)),
        from_hbm(active_blocks.reshape(-1)),
        from_hbm(dest_tile.reshape(-1)),
    )
    evens = [(t, t ^ 1) for t in range(tiles)]
    odds = [(t, ((t + 1) ^ 1) - 1) for t in range(tiles)]
    odds = [(t, other % tiles) for t, other in odds]
    from_odd = lax.ppermute(to_odd, "tile", odds)
    from_even = lax.ppermute(to_even, "tile", evens)
    block = jax.ShapeDtypeStruct((species, cells), bf16)
    blocks = pl.pallas_call(
        functools.partial(inner_kernel, dests, length, halves),
        out_shape=[block] * dests,
        in_specs=[vmem()] * 2,
        out_specs=[vmem()] * dests,
        compiler_params=params,
        cost_estimate=cost(1.0),
        name="inner_rows",
    )(field, rates)
    def ring(k, x):
        return lax.ppermute(x, "spec", [(s, (s + k) % dests) for s in range(dests)])

    early, late = [1], [0] + list(range(2, dests))
    edge = jax.ShapeDtypeStruct((species, BEHIND * cols), bf16)
    whole = pl.pallas_call(
        functools.partial(edge_kernel, dests, early, late, length, halves),
        out_shape=[block] * len(late) + [edge] * len(early),
        in_specs=[vmem()] * (4 + len(late)),
        out_specs=[vmem()] * dests,
        compiler_params=params,
        cost_estimate=cost(0.1),
        name="edge_rows",
    )(from_odd, from_even, field, rates, *[blocks[k] for k in late])
    full, edges = whole[: len(late)], whole[len(late) :]
    received = {k: ring(k, blocks[k]) for k in early}
    received |= {k: ring(k, x) if k else x for k, x in zip(late, full)}
    edges = [ring(k, x) for k, x in zip(early, edges)]
    hits = lax.all_gather(hits, "tile", axis=0, tiled=True)
    w1, w2, listing = pl.pallas_call(
        weight_kernel,
        out_shape=[jax.ShapeDtypeStruct(w.shape[::-1], bf16) for w in (first_weight, middle_weight)]
        + [jax.ShapeDtypeStruct((1, slots), jnp.int32)],
        in_specs=[vmem()] * 3 + [anywhere()],
        out_specs=[vmem()] * 3,
        compiler_params=params,
        cost_estimate=cost(0.5),
        name="halved_weights",
    )(first_weight, middle_weight, active_blocks.reshape(1, slots), full[0])
    out, load_share = pl.pallas_call(
        functools.partial(chemistry_kernel, dests, early),
        out_shape=[
            jax.ShapeDtypeStruct((dests, species, cells), bf16),
            jax.ShapeDtypeStruct((1, 1), f32),
        ],
        in_specs=[pl.BlockSpec(memory_space=pltpu.SMEM)]
        + [vmem()] * 3
        + [anywhere()]
        + [vmem()] * (dests + len(early)),
        out_specs=[anywhere()] * 2,
        scratch_shapes=[
            pltpu.VMEM((dests, species, cells), bf16),
            pltpu.VMEM((dests * species, slots * BLK), f32),
            pltpu.VMEM((tiles, LANES), f32),
            pltpu.VMEM((1, 1), f32),
            pltpu.SemaphoreType.DMA((3,)),
        ],
        compiler_params=params,
        cost_estimate=cost(4.0),
        name="chemistry",
    )(
        listing.reshape(-1),
        w1,
        w2,
        last_weight.T,
        from_hbm(hits),
        *[received[k] for k in range(dests)],
        *edges,
    )
    return out.reshape(dests * species, cells), load_share


def solution(mesh):
    in_specs = (
        P("spec", "tile", None),
        P("tile", None),
        P(),
        P(),
        P(),
        P("tile", "spec", None),
        P("tile", "spec", None),
    )
    out_specs = (P(None, ("tile", "spec")), P("tile", "spec"))
    return jax.shard_map(shards, mesh=mesh, in_specs=in_specs, out_specs=out_specs, check_vma=False)
```

```python
import functools

import jax
import jax.numpy as jnp
from jax import lax
from jax.experimental import pallas as pl
from jax.experimental.pallas import tpu as pltpu
from jax.sharding import PartitionSpec as P

BLK = 128
RECV = 8
LANES = 128
SUB = 8
BEHIND = 4
AHEAD = 2
VMEM_BYTES = 16 * 1024 * 1024


def silu_of_half(half):
    return half + half * jnp.tanh(half)


def sweep_rows(rows, rates):
    diffs = [b - a for a, b in zip(rows[:-1], rows[1:])]
    fluxes = []
    for at in range(1, len(rows) - 1):
        left, right = diffs[at - 1], diffs[at]
        slope = jnp.maximum(jnp.minimum(left, right), 0.0) + jnp.minimum(
            jnp.maximum(left, right), 0.0
        )
        rate, damp = rates[at]
        fluxes.append(rate * (rows[at] + damp * slope))
    return [rows[at] - fluxes[at - 1] + fluxes[at - 2] for at in range(2, len(rows) - 1)]


def two_sweeps(rows, rates):
    once = sweep_rows(rows, rates)
    return sweep_rows(once, rates[2:-1])


def with_damp(rate, shape):
    rate = jnp.broadcast_to(rate, shape)
    return rate, 0.5 - 0.5 * rate


def tiled(x, halves):
    lead, (rows, cols) = x.shape[:-2], x.shape[-2:]
    x = x.reshape(lead + (rows // SUB, SUB, halves, LANES))
    axes = tuple(range(len(lead)))
    x = x.transpose(axes + tuple(len(lead) + a for a in (0, 2, 1, 3)))
    return x.reshape(lead + (rows * halves, LANES))


def spot(at, half, halves):
    return (at // SUB * halves + half) * SUB + at % SUB


def load_kernel(*refs):
    *refs, arrived = refs
    count = len(refs) // 2
    copies = [
        pltpu.make_async_copy(refs[i], refs[count + i], arrived.at[i]) for i in range(count)
    ]
    for copy in copies:
        copy.start()
    for copy in copies:
        copy.wait()


def pack_kernel(
    length, halves, blocks, q_ref, rates_ref, list_ref, dest_ref, other_list_ref, other_dest_ref,
    even_ref, odd_ref, hits_ref,
):
    species = q_ref.shape[0] // (length * halves)
    part = BEHIND * species + SUB

    def row(at, half):
        return q_ref[pl.ds(spot(at, half, halves), species, stride=length * halves), :]

    tile = lax.broadcasted_iota(jnp.int32, (hits_ref.shape[0], list_ref.shape[1]), 0)
    named = jnp.zeros(tile.shape, jnp.float32)
    for listed_ref, target_ref in ((list_ref, dest_ref), (other_list_ref, other_dest_ref)):
        target = jnp.where(listed_ref[...] < blocks, target_ref[...], -1)
        named = named + jnp.where(tile == target, 1.0, 0.0)
    hits = jnp.broadcast_to(jnp.sum(named, axis=1, keepdims=True), hits_ref.shape)
    hits_ref[...] = hits

    def write(up_ref, down_ref):
        for half in range(halves):
            start = half * part
            for j in range(BEHIND):
                up_ref[start + j * species : start + (j + 1) * species, :] = row(
                    length - BEHIND + j, half
                )
            for j in range(AHEAD):
                down_ref[start + j * species : start + (j + 1) * species, :] = row(j, half)
            for j in range(AHEAD, BEHIND):
                down_ref[start + j * species : start + (j + 1) * species, :] = jnp.zeros(
                    (species, LANES), jnp.float32
                )
            high, low = spot(length - SUB, half, halves), spot(0, half, halves)
            up_ref[start + BEHIND * species : start + part, :] = rates_ref[high : high + SUB, :]
            down_ref[start + BEHIND * species : start + part, :] = rates_ref[low : low + SUB, :]
        up_ref[halves * part :, :] = hits
        down_ref[halves * part :, :] = hits

    even = lax.rem(lax.axis_index("tile"), 2) == 0

    @pl.when(even)
    def _():
        write(even_ref, odd_ref)

    @pl.when(jnp.logical_not(even))
    def _():
        write(odd_ref, even_ref)


def inner_kernel(dests, length, halves, q_ref, rates_ref, *out_refs):
    species = out_refs[0].shape[0]
    share = length // dests
    me = lax.axis_index("spec")
    for k in range(dests):
        first = lax.rem(me + k, dests) * share
        below = jnp.maximum(first - SUB, 0)
        above = jnp.minimum(first + share, length - SUB)
        for half in range(halves):

            def start(at):
                if at < 0:
                    return below * halves + spot(at + SUB, half, halves)
                if at >= share:
                    return above * halves + spot(at - share, half, halves)
                return first * halves + spot(at, half, halves)

            reach = range(-BEHIND, share + AHEAD)
            rows = [q_ref[pl.ds(start(at), species, stride=length * halves), :] for at in reach]
            rates = [
                with_damp(rates_ref[pl.ds(start(at), 1), :], (species, LANES)) for at in reach
            ]
            for at, value in enumerate(two_sweeps(rows, rates)):
                place = (at * halves + half) * LANES
                out_refs[k][:, place : place + LANES] = value.astype(jnp.bfloat16)


def edge_kernel(
    dests, early, late, length, halves, odd_ref, even_ref, hits_ref, q_ref, rates_ref, *refs
):
    in_refs, out_refs, refs = refs[: len(late)], refs[len(late) : 2 * len(late)], refs[2 * len(late) :]
    *small_refs, known_ref, to_even_ref = refs
    species, cells = out_refs[0].shape
    me = lax.axis_index("spec")
    part = BEHIND * species + SUB
    reach = BEHIND + AHEAD
    even = lax.rem(lax.axis_index("tile"), 2) == 0
    known_ref[...] = hits_ref[...] + odd_ref[halves * part :, :]
    to_even_ref[...] = odd_ref[halves * part :, :]

    def message(behind, at, size):
        a, b = odd_ref[at : at + size, :], even_ref[at : at + size, :]
        return jnp.where(even, a, b) if behind else jnp.where(even, b, a)

    def row(at, half):
        return q_ref[pl.ds(spot(at, half, halves), species, stride=length * halves), :]

    def rates_of(values):
        return [with_damp(value, (species, LANES)) for value in values]

    tops, bottoms = [], []
    for half in range(halves):
        base = half * part
        behind = [message(True, base + j * species, species) for j in range(BEHIND)]
        ahead = [message(False, base + j * species, species) for j in range(AHEAD)]
        before = message(True, base + BEHIND * species, SUB)
        after = message(False, base + BEHIND * species, SUB)

        def own_rates(first):
            places = [spot(first + j, half, halves) for j in range(reach)]
            return [rates_ref[at : at + 1, :] for at in places]

        tops.append(
            two_sweeps(
                behind + [row(j, half) for j in range(reach)],
                rates_of([before[SUB - BEHIND + j :][:1] for j in range(BEHIND)] + own_rates(0)),
            )
        )
        bottoms.append(
            two_sweeps(
                [row(length - reach + j, half) for j in range(reach)] + ahead,
                rates_of(own_rates(length - reach) + [after[j : j + 1] for j in range(AHEAD)]),
            )
        )
    for k, small_ref in zip(early, small_refs):
        low = lax.rem(me + k, dests) == 0
        for half in range(halves):
            for j in range(BEHIND):
                value = tops[half][j]
                if j >= BEHIND - AHEAD:
                    value = jnp.where(low, value, bottoms[half][j - BEHIND + AHEAD])
                at = (j * halves + half) * LANES
                small_ref[:, at : at + LANES] = value.astype(jnp.bfloat16)
    for k, in_ref, out_ref in zip(late, in_refs, out_refs):
        dest = lax.rem(me + k, dests)
        out_ref[...] = in_ref[...]

        @pl.when(dest == 0)
        def _():
            for half in range(halves):
                for j, value in enumerate(tops[half]):
                    at = (j * halves + half) * LANES
                    out_ref[:, at : at + LANES] = value.astype(jnp.bfloat16)

        @pl.when(dest == dests - 1)
        def _():
            for half in range(halves):
                for j, value in enumerate(bottoms[half]):
                    at = cells + ((j - AHEAD) * halves + half) * LANES
                    out_ref[:, at : at + LANES] = value.astype(jnp.bfloat16)


def weight_kernel(w1_ref, w2_ref, after_ref, w1_out, w2_out):
    w1_out[...] = (0.5 * w1_ref[...].astype(jnp.float32)).T.astype(jnp.bfloat16)
    w2_out[...] = (0.5 * w2_ref[...].astype(jnp.float32)).T.astype(jnp.bfloat16)


def chemistry_kernel(
    groups, early, list_ref, w1_ref, w2_ref, w3_ref, known_ref, even_ref, *refs
):
    parts, edges, refs = refs[:groups], refs[groups : groups + len(early)], refs[groups + len(early) :]
    out_ref, share_ref, state_ref, picked_ref, held_ref, done = refs
    species, cells = state_ref.shape[1:]
    slots = list_ref.shape[0]
    blocks = cells // BLK
    me = lax.axis_index("spec")

    def source(k):
        return lax.rem(me - k + groups, groups)

    for k in range(groups):
        state_ref[source(k)] = parts[k][...]
    wide = edges[0].shape[1]
    narrow = wide // BEHIND * AHEAD

    @pl.when(me == 0)
    def _():
        for k, edge in zip(early, edges):
            state_ref[source(k), :, 0:wide] = edge[...]

    @pl.when(me == groups - 1)
    def _():
        for k, edge in zip(early, edges):
            state_ref[source(k), :, cells - narrow :] = edge[:, wide - narrow :]

    def place(j):
        return pl.ds(pl.multiple_of(jnp.minimum(list_ref[j], blocks - 1) * BLK, BLK), BLK)

    for j in range(slots):
        for g in range(groups):
            picked_ref[g * species : (g + 1) * species, j * BLK : (j + 1) * BLK] = state_ref[
                g, :, place(j)
            ].astype(jnp.float32)
    each = 4
    for first in range(0, slots, each):
        x = picked_ref[:, first * BLK : (first + each) * BLK]
        hidden = jnp.dot(w1_ref[...], x.astype(jnp.bfloat16), preferred_element_type=jnp.float32)
        hidden = silu_of_half(hidden).astype(jnp.bfloat16)
        hidden = jnp.dot(w2_ref[...], hidden, preferred_element_type=jnp.float32)
        hidden = silu_of_half(hidden).astype(jnp.bfloat16)
        picked_ref[:, first * BLK : (first + each) * BLK] = x + jnp.dot(
            w3_ref[...], hidden, preferred_element_type=jnp.float32
        )
    for j in range(slots):
        valid = list_ref[j] < blocks
        for g in range(groups):
            fresh = picked_ref[g * species : (g + 1) * species, j * BLK : (j + 1) * BLK]
            now = state_ref[g, :, place(j)].astype(jnp.float32)
            state_ref[g, :, place(j)] = jnp.where(valid, fresh, now).astype(jnp.bfloat16)
    whole = pltpu.make_async_copy(state_ref, out_ref, done.at[1])
    whole.start()
    hits = known_ref[...] + even_ref[...]
    tile = lax.broadcasted_iota(jnp.int32, hits.shape, 0)
    mine = jnp.where(tile == lax.axis_index("tile"), hits, 0.0)
    held_ref[...] = jnp.sum(mine, axis=0, keepdims=True)[:, 0:1] / RECV
    share = pltpu.make_async_copy(held_ref, share_ref, done.at[0])
    share.start()
    share.wait()
    whole.wait()


def vmem():
    return pl.BlockSpec(memory_space=pltpu.VMEM)


def anywhere():
    return pl.BlockSpec(memory_space=pl.ANY)


def from_hbm(x):
    return pltpu.with_memory_space_constraint(x, pltpu.HBM)


def cost(us):
    return pl.CostEstimate(flops=int(us * 1e9), bytes_accessed=int(us * 3e6), transcendentals=0)


def shards(
    concentrations, courant, first_weight, middle_weight, last_weight, active_blocks, dest_tile
):
    species, length, cols = concentrations.shape
    dests = lax.axis_size("spec")
    tiles = lax.axis_size("tile")
    cells = length // dests * cols
    slots = active_blocks.shape[-1]
    halves = cols // LANES
    f32, bf16 = jnp.float32, jnp.bfloat16
    params = pltpu.CompilerParams(vmem_limit_bytes=VMEM_BYTES)
    size = halves * (BEHIND * species + SUB) + tiles
    flag = jax.ShapeDtypeStruct((tiles, LANES), f32)

    evens = [(t, t ^ 1) for t in range(tiles)]
    odds = [(t, ((t + 1) ^ 1) - 1) for t in range(tiles)]
    odds = [(t, other % tiles) for t, other in odds]
    other_list = lax.ppermute(active_blocks, "tile", evens)
    other_dest = lax.ppermute(dest_tile, "tile", evens)
    sources = [
        tiled(concentrations, halves).reshape(species * length * halves, LANES),
        tiled(courant, halves),
        active_blocks.reshape(1, slots),
        dest_tile.reshape(1, slots),
    ]
    field, rates, listing, targets = pl.pallas_call(
        load_kernel,
        out_shape=[jax.ShapeDtypeStruct(x.shape, x.dtype) for x in sources],
        in_specs=[anywhere()] * 4,
        out_specs=[vmem()] * 4,
        scratch_shapes=[pltpu.SemaphoreType.DMA((4,))],
        compiler_params=params,
        cost_estimate=cost(1.0),
        name="load_operands",
    )(*[from_hbm(x) for x in sources])
    to_even, to_odd, hits = pl.pallas_call(
        functools.partial(pack_kernel, length, halves, cells // BLK),
        out_shape=[jax.ShapeDtypeStruct((size, LANES), f32)] * 2 + [flag],
        in_specs=[vmem()] * 6,
        out_specs=[vmem()] * 3,
        compiler_params=params,
        cost_estimate=cost(0.1),
        name="pack_edges",
    )(
        field,
        rates,
        listing,
        targets,
        other_list.reshape(1, slots),
        other_dest.reshape(1, slots),
    )
    from_odd = lax.ppermute(to_odd, "tile", odds)
    from_even = lax.ppermute(to_even, "tile", evens)
    block = jax.ShapeDtypeStruct((species, cells), bf16)
    blocks = pl.pallas_call(
        functools.partial(inner_kernel, dests, length, halves),
        out_shape=[block] * dests,
        in_specs=[vmem()] * 2,
        out_specs=[vmem()] * dests,
        compiler_params=params,
        cost_estimate=cost(1.0),
        name="inner_rows",
    )(field, rates)
    def ring(k, x):
        return lax.ppermute(x, "spec", [(s, (s + k) % dests) for s in range(dests)])

    early, late = [1], [0] + list(range(2, dests))
    edge = jax.ShapeDtypeStruct((species, BEHIND * cols), bf16)
    whole = pl.pallas_call(
        functools.partial(edge_kernel, dests, early, late, length, halves),
        out_shape=[block] * len(late) + [edge] * len(early) + [flag] * 2,
        in_specs=[vmem()] * (5 + len(late)),
        out_specs=[vmem()] * (dests + 2),
        compiler_params=params,
        cost_estimate=cost(0.1),
        name="edge_rows",
    )(from_odd, from_even, hits, field, rates, *[blocks[k] for k in late])
    full, edges, (known, to_even) = whole[: len(late)], whole[len(late) : dests], whole[dests:]
    received = {k: ring(k, blocks[k]) for k in early}
    received |= {k: ring(k, x) if k else x for k, x in zip(late, full)}
    edges = [ring(k, x) for k, x in zip(early, edges)]
    from_even = lax.ppermute(to_even, "tile", evens)
    w1, w2 = pl.pallas_call(
        weight_kernel,
        out_shape=[jax.ShapeDtypeStruct(w.shape[::-1], bf16) for w in (first_weight, middle_weight)],
        in_specs=[vmem()] * 2 + [anywhere()],
        out_specs=[vmem()] * 2,
        compiler_params=params,
        cost_estimate=cost(0.5),
        name="halved_weights",
    )(first_weight, middle_weight, full[0])
    out, load_share = pl.pallas_call(
        functools.partial(chemistry_kernel, dests, early),
        out_shape=[
            jax.ShapeDtypeStruct((dests, species, cells), bf16),
            jax.ShapeDtypeStruct((1, 1), f32),
        ],
        in_specs=[pl.BlockSpec(memory_space=pltpu.SMEM)] + [vmem()] * (5 + dests + len(early)),
        out_specs=[anywhere()] * 2,
        scratch_shapes=[
            pltpu.VMEM((dests, species, cells), bf16),
            pltpu.VMEM((dests * species, slots * BLK), f32),
            pltpu.VMEM((1, 1), f32),
            pltpu.SemaphoreType.DMA((2,)),
        ],
        compiler_params=params,
        cost_estimate=cost(4.0),
        name="chemistry",
    )(
        listing.reshape(-1),
        w1,
        w2,
        last_weight.T,
        known,
        from_even,
        *[received[k] for k in range(dests)],
        *edges,
    )
    return out.reshape(dests * species, cells), load_share


def solution(mesh):
    in_specs = (
        P("spec", "tile", None),
        P("tile", None),
        P(),
        P(),
        P(),
        P("tile", "spec", None),
        P("tile", "spec", None),
    )
    out_specs = (P(None, ("tile", "spec")), P("tile", "spec"))
    return jax.shard_map(shards, mesh=mesh, in_specs=in_specs, out_specs=out_specs, check_vma=False)
```

```python
import functools

import jax
import jax.numpy as jnp
from jax import lax
from jax.experimental import pallas as pl
from jax.experimental.pallas import tpu as pltpu
from jax.sharding import PartitionSpec as P

BLK = 128
RECV = 8
LANES = 128
SUB = 8
BEHIND = 4
AHEAD = 2
VMEM_BYTES = 16 * 1024 * 1024


def silu_of_half(half):
    half = half.astype(jnp.bfloat16)
    return half + half * jnp.tanh(half)


def sweep_rows(rows, rates):
    diffs = [b - a for a, b in zip(rows[:-1], rows[1:])]
    fluxes = []
    for at in range(1, len(rows) - 1):
        left, right = diffs[at - 1], diffs[at]
        slope = jnp.maximum(jnp.minimum(left, right), 0.0) + jnp.minimum(
            jnp.maximum(left, right), 0.0
        )
        rate, damp = rates[at]
        fluxes.append(rate * (rows[at] + damp * slope))
    return [rows[at] - fluxes[at - 1] + fluxes[at - 2] for at in range(2, len(rows) - 1)]


def two_sweeps(rows, rates):
    once = sweep_rows(rows, rates)
    return sweep_rows(once, rates[2:-1])


def with_damp(rate, shape):
    rate = jnp.broadcast_to(rate, shape)
    return rate, 0.5 - 0.5 * rate


def tiled(x, halves):
    lead, (rows, cols) = x.shape[:-2], x.shape[-2:]
    x = x.reshape(lead + (rows // SUB, SUB, halves, LANES))
    axes = tuple(range(len(lead)))
    x = x.transpose(axes + tuple(len(lead) + a for a in (0, 2, 1, 3)))
    return x.reshape(lead + (rows * halves, LANES))


def spot(at, half, halves):
    return (at // SUB * halves + half) * SUB + at % SUB


def pack_kernel(
    length, halves, blocks, q_in, rates_in, list_in, dest_in,
    even_ref, odd_ref, hits_ref, low_ref, high_ref, rates_ref, list_ref, dest_ref, arrived,
):
    species, rows = q_in.shape[:2]
    tile = halves * SUB
    part = BEHIND * species + SUB
    shape = (species, tile, LANES)
    pairs = [
        (q_in.at[:, rows - tile :], high_ref.reshape(shape)),
        (q_in.at[:, :tile], low_ref.reshape(shape)),
        (rates_in.at[rows - tile :], rates_ref.at[tile:]),
        (rates_in.at[:tile], rates_ref.at[:tile]),
        (list_in, list_ref),
        (dest_in, dest_ref),
    ]
    copies = [
        pltpu.make_async_copy(source, target, arrived.at[i])
        for i, (source, target) in enumerate(pairs)
    ]
    for copy in copies:
        copy.start()
    copies[4].wait()
    copies[5].wait()
    lane = lax.broadcasted_iota(jnp.int32, (SUB, LANES), 1)
    hits = jnp.zeros((SUB, LANES), jnp.float32)
    for j in range(list_ref.shape[0]):
        target = jnp.where(list_ref[j] < blocks, dest_ref[j], -1)
        hits = hits + jnp.where(lane == target, 1.0, 0.0)
    hits_ref[...] = hits
    for copy in copies[:4]:
        copy.wait()

    def write(up_ref, down_ref):
        for half in range(halves):
            start = half * part
            for j in range(BEHIND):
                at = start + j * species
                up_ref[at : at + species, :] = high_ref[
                    pl.ds(half * SUB + SUB - BEHIND + j, species, stride=tile), :
                ]
                if j < AHEAD:
                    value = low_ref[pl.ds(half * SUB + j, species, stride=tile), :]
                else:
                    value = jnp.zeros((species, LANES), jnp.float32)
                down_ref[at : at + species, :] = value
            at = start + BEHIND * species
            up_ref[at : at + SUB, :] = rates_ref[tile + half * SUB : tile + (half + 1) * SUB, :]
            down_ref[at : at + SUB, :] = rates_ref[half * SUB : (half + 1) * SUB, :]
        up_ref[halves * part :, :] = hits
        down_ref[halves * part :, :] = hits

    even = lax.rem(lax.axis_index("tile"), 2) == 0

    @pl.when(even)
    def _():
        write(even_ref, odd_ref)

    @pl.when(jnp.logical_not(even))
    def _():
        write(odd_ref, even_ref)


def inner_kernel(dests, length, halves, q_ref, rates_ref, *out_refs):
    species = out_refs[0].shape[0]
    share = length // dests
    me = lax.axis_index("spec")
    for k in range(dests):
        first = lax.rem(me + k, dests) * share
        below = jnp.maximum(first - SUB, 0)
        above = jnp.minimum(first + share, length - SUB)
        for half in range(halves):

            def start(at):
                if at < 0:
                    return below * halves + spot(at + SUB, half, halves)
                if at >= share:
                    return above * halves + spot(at - share, half, halves)
                return first * halves + spot(at, half, halves)

            reach = range(-BEHIND, share + AHEAD)
            rows = [q_ref[pl.ds(start(at), species, stride=length * halves), :] for at in reach]
            rates = [
                with_damp(rates_ref[pl.ds(start(at), 1), :], (species, LANES)) for at in reach
            ]
            for at, value in enumerate(two_sweeps(rows, rates)):
                place = (at * halves + half) * LANES
                out_refs[k][:, place : place + LANES] = value.astype(jnp.bfloat16)


def edge_kernel(
    dests, length, halves, odd_ref, even_ref, hits_ref, q_ref, rates_ref, *refs
):
    in_refs, out_refs, (to_even_ref, to_odd_ref, known_ref) = (
        refs[:dests], refs[dests : 2 * dests], refs[2 * dests :]
    )
    species, cells = out_refs[0].shape
    me = lax.axis_index("spec")
    part = BEHIND * species + SUB
    reach = BEHIND + AHEAD
    even = lax.rem(lax.axis_index("tile"), 2) == 0
    own, from_even, from_odd = hits_ref[...], even_ref[halves * part :, :], odd_ref[halves * part :, :]
    known_ref[...] = own + from_even + from_odd
    to_even_ref[...] = from_odd
    to_odd_ref[...] = from_even

    def message(behind, at, size):
        a, b = odd_ref[at : at + size, :], even_ref[at : at + size, :]
        return jnp.where(even, a, b) if behind else jnp.where(even, b, a)

    def row(at, half):
        return q_ref[pl.ds(spot(at, half, halves), species, stride=length * halves), :]

    def rates_of(values):
        return [with_damp(value, (species, LANES)) for value in values]

    tops, bottoms = [], []
    for half in range(halves):
        base = half * part
        behind = [message(True, base + j * species, species) for j in range(BEHIND)]
        ahead = [message(False, base + j * species, species) for j in range(AHEAD)]
        before = message(True, base + BEHIND * species, SUB)
        after = message(False, base + BEHIND * species, SUB)

        def own_rates(first):
            places = [spot(first + j, half, halves) for j in range(reach)]
            return [rates_ref[at : at + 1, :] for at in places]

        tops.append(
            two_sweeps(
                behind + [row(j, half) for j in range(reach)],
                rates_of([before[SUB - BEHIND + j :][:1] for j in range(BEHIND)] + own_rates(0)),
            )
        )
        bottoms.append(
            two_sweeps(
                [row(length - reach + j, half) for j in range(reach)] + ahead,
                rates_of(own_rates(length - reach) + [after[j : j + 1] for j in range(AHEAD)]),
            )
        )
    for k, (in_ref, out_ref) in enumerate(zip(in_refs, out_refs)):
        dest = lax.rem(me + k, dests)
        out_ref[...] = in_ref[...]

        @pl.when(dest == 0)
        def _():
            for half in range(halves):
                for j, value in enumerate(tops[half]):
                    at = (j * halves + half) * LANES
                    out_ref[:, at : at + LANES] = value.astype(jnp.bfloat16)

        @pl.when(dest == dests - 1)
        def _():
            for half in range(halves):
                for j, value in enumerate(bottoms[half]):
                    at = cells + ((j - AHEAD) * halves + half) * LANES
                    out_ref[:, at : at + LANES] = value.astype(jnp.bfloat16)


def weight_kernel(w1_ref, w2_ref, list_ref, after_ref, w1_out, w2_out, list_out):
    list_out[...] = list_ref[...]
    w1_out[...] = (0.5 * w1_ref[...].astype(jnp.float32)).T.astype(jnp.bfloat16)
    w2_out[...] = (0.5 * w2_ref[...].astype(jnp.float32)).T.astype(jnp.bfloat16)


def chemistry_kernel(
    groups, list_ref, w1_ref, w2_ref, w3_ref, known_ref, odd_ref, even_ref, *refs
):
    parts, (out_ref, share_ref, state_ref, picked_ref, held_ref, done) = refs[:groups], refs[groups:]
    species, cells = state_ref.shape[1:]
    slots = list_ref.shape[0]
    blocks = cells // BLK
    me = lax.axis_index("spec")
    for k in range(groups):
        state_ref[lax.rem(me - k + groups, groups)] = parts[k][...]
    hits = known_ref[...] + even_ref[...] + odd_ref[...]
    lane = lax.broadcasted_iota(jnp.int32, hits.shape, 1)
    mine = jnp.where(lane == lax.axis_index("tile"), hits, 0.0)
    held_ref[...] = jnp.sum(mine[0:1], axis=1, keepdims=True) / RECV
    share = pltpu.make_async_copy(held_ref, share_ref, done.at[0])
    share.start()

    def place(j):
        return pl.ds(pl.multiple_of(jnp.minimum(list_ref[j], blocks - 1) * BLK, BLK), BLK)

    for j in range(slots):
        for g in range(groups):
            picked_ref[g * species : (g + 1) * species, j * BLK : (j + 1) * BLK] = state_ref[
                g, :, place(j)
            ].astype(jnp.float32)
    each = 4
    for first in range(0, slots, each):
        x = picked_ref[:, first * BLK : (first + each) * BLK]
        hidden = jnp.dot(w1_ref[...], x.astype(jnp.bfloat16), preferred_element_type=jnp.float32)
        hidden = silu_of_half(hidden)
        hidden = jnp.dot(w2_ref[...], hidden, preferred_element_type=jnp.float32)
        hidden = silu_of_half(hidden)
        picked_ref[:, first * BLK : (first + each) * BLK] = x + jnp.dot(
            w3_ref[...], hidden, preferred_element_type=jnp.float32
        )
    for j in range(slots):
        valid = list_ref[j] < blocks
        for g in range(groups):
            fresh = picked_ref[g * species : (g + 1) * species, j * BLK : (j + 1) * BLK]
            now = state_ref[g, :, place(j)].astype(jnp.float32)
            state_ref[g, :, place(j)] = jnp.where(valid, fresh, now).astype(jnp.bfloat16)
    whole = pltpu.make_async_copy(state_ref, out_ref, done.at[1])
    whole.start()
    share.wait()
    whole.wait()


def vmem():
    return pl.BlockSpec(memory_space=pltpu.VMEM)


def anywhere():
    return pl.BlockSpec(memory_space=pl.ANY)


def from_hbm(x):
    return pltpu.with_memory_space_constraint(x, pltpu.HBM)


def cost(us):
    return pl.CostEstimate(flops=int(us * 1e9), bytes_accessed=int(us * 3e6), transcendentals=0)


def shards(
    concentrations, courant, first_weight, middle_weight, last_weight, active_blocks, dest_tile
):
    species, length, cols = concentrations.shape
    dests = lax.axis_size("spec")
    tiles = lax.axis_size("tile")
    cells = length // dests * cols
    slots = active_blocks.shape[-1]
    halves = cols // LANES
    f32, bf16 = jnp.float32, jnp.bfloat16
    params = pltpu.CompilerParams(vmem_limit_bytes=VMEM_BYTES)
    size = halves * (BEHIND * species + SUB) + SUB
    flag = jax.ShapeDtypeStruct((SUB, LANES), f32)

    field, rates = tiled(concentrations, halves), tiled(courant, halves)
    to_even, to_odd, hits = pl.pallas_call(
        functools.partial(pack_kernel, length, halves, cells // BLK),
        out_shape=[jax.ShapeDtypeStruct((size, LANES), f32)] * 2 + [flag],
        in_specs=[anywhere()] * 4,
        out_specs=[vmem()] * 3,
        scratch_shapes=[
            pltpu.VMEM((species * halves * SUB, LANES), f32),
            pltpu.VMEM((species * halves * SUB, LANES), f32),
            pltpu.VMEM((2 * halves * SUB, LANES), f32),
            pltpu.SMEM((slots,), jnp.int32),
            pltpu.SMEM((slots,), jnp.int32),
            pltpu.SemaphoreType.DMA((6,)),
        ],
        compiler_params=params,
        cost_estimate=cost(1.0),
        name="pack_edges",
    )(
        from_hbm(field),
        from_hbm(rates),
        from_hbm(active_blocks.reshape(-1)),
        from_hbm(dest_tile.reshape(-1)),
    )
    field = field.reshape(species * length * halves, LANES)
    evens = [(t, t ^ 1) for t in range(tiles)]
    odds = [(t, ((t + 1) ^ 1) - 1) for t in range(tiles)]
    odds = [(t, other % tiles) for t, other in odds]
    from_odd = lax.ppermute(to_odd, "tile", odds)
    from_even = lax.ppermute(to_even, "tile", evens)
    block = jax.ShapeDtypeStruct((species, cells), bf16)
    blocks = pl.pallas_call(
        functools.partial(inner_kernel, dests, length, halves),
        out_shape=[block] * dests,
        in_specs=[vmem()] * 2,
        out_specs=[vmem()] * dests,
        compiler_params=params,
        cost_estimate=cost(1.0),
        name="inner_rows",
    )(field, rates)
    *blocks, to_even, to_odd, known = pl.pallas_call(
        functools.partial(edge_kernel, dests, length, halves),
        out_shape=[block] * dests + [flag] * 3,
        in_specs=[vmem()] * (5 + dests),
        out_specs=[vmem()] * (dests + 3),
        compiler_params=params,
        cost_estimate=cost(0.1),
        name="edge_rows",
    )(from_odd, from_even, hits, field, rates, *blocks)
    received = [blocks[0]] + [
        lax.ppermute(blocks[k], "spec", [(s, (s + k) % dests) for s in range(dests)])
        for k in range(1, dests)
    ]
    from_odd = lax.ppermute(to_odd, "tile", odds)
    from_even = lax.ppermute(to_even, "tile", evens)
    w1, w2, listing = pl.pallas_call(
        weight_kernel,
        out_shape=[jax.ShapeDtypeStruct(w.shape[::-1], bf16) for w in (first_weight, middle_weight)]
        + [jax.ShapeDtypeStruct((1, slots), jnp.int32)],
        in_specs=[vmem()] * 3 + [anywhere()],
        out_specs=[vmem()] * 3,
        compiler_params=params,
        cost_estimate=cost(0.5),
        name="halved_weights",
    )(first_weight, middle_weight, active_blocks.reshape(1, slots), known)
    out, load_share = pl.pallas_call(
        functools.partial(chemistry_kernel, dests),
        out_shape=[
            jax.ShapeDtypeStruct((dests, species, cells), bf16),
            jax.ShapeDtypeStruct((1, 1), f32),
        ],
        in_specs=[pl.BlockSpec(memory_space=pltpu.SMEM)] + [vmem()] * (6 + dests),
        out_specs=[anywhere()] * 2,
        scratch_shapes=[
            pltpu.VMEM((dests, species, cells), bf16),
            pltpu.VMEM((dests * species, slots * BLK), f32),
            pltpu.VMEM((1, 1), f32),
            pltpu.SemaphoreType.DMA((2,)),
        ],
        compiler_params=params,
        cost_estimate=cost(4.0),
        name="chemistry",
    )(
        listing.reshape(-1),
        w1,
        w2,
        last_weight.T,
        known,
        from_odd,
        from_even,
        *received,
    )
    return out.reshape(dests * species, cells), load_share


def solution(mesh):
    in_specs = (
        P("spec", "tile", None),
        P("tile", None),
        P(),
        P(),
        P(),
        P("tile", "spec", None),
        P("tile", "spec", None),
    )
    out_specs = (P(None, ("tile", "spec")), P("tile", "spec"))
    return jax.shard_map(shards, mesh=mesh, in_specs=in_specs, out_specs=out_specs, check_vma=False)
```

```python
import functools

import jax
import jax.numpy as jnp
from jax import lax
from jax.experimental import pallas as pl
from jax.experimental.pallas import tpu as pltpu
from jax.sharding import PartitionSpec as P

BLK = 128
RECV = 8
LANES = 128
SUB = 8
BEHIND = 4
AHEAD = 2
VMEM_BYTES = 16 * 1024 * 1024


def silu_of_half(half):
    return half + half * jnp.tanh(half)


def sweep_rows(rows, rates):
    diffs = [b - a for a, b in zip(rows[:-1], rows[1:])]
    fluxes = []
    for at in range(1, len(rows) - 1):
        left, right = diffs[at - 1], diffs[at]
        slope = jnp.maximum(jnp.minimum(left, right), 0.0) + jnp.minimum(
            jnp.maximum(left, right), 0.0
        )
        rate, damp = rates[at]
        fluxes.append(rate * (rows[at] + damp * slope))
    return [rows[at] - fluxes[at - 1] + fluxes[at - 2] for at in range(2, len(rows) - 1)]


def two_sweeps(rows, rates):
    once = sweep_rows(rows, rates)
    return sweep_rows(once, rates[2:-1])


def with_damp(rate, shape):
    rate = jnp.broadcast_to(rate, shape)
    return rate, 0.5 - 0.5 * rate


def tiled(x, halves):
    lead, (rows, cols) = x.shape[:-2], x.shape[-2:]
    x = x.reshape(lead + (rows // SUB, SUB, halves, LANES))
    axes = tuple(range(len(lead)))
    x = x.transpose(axes + tuple(len(lead) + a for a in (0, 2, 1, 3)))
    return x.reshape(lead + (rows * halves, LANES))


def spot(at, half, halves):
    return (at // SUB * halves + half) * SUB + at % SUB


def pack_kernel(
    length, halves, blocks, q_in, rates_in, list_in, dest_in,
    even_ref, odd_ref, hits_ref, low_ref, high_ref, rates_ref, list_ref, dest_ref, arrived,
):
    species, rows = q_in.shape[:2]
    tile = halves * SUB
    part = BEHIND * species + SUB
    shape = (species, tile, LANES)
    pairs = [
        (q_in.at[:, rows - tile :], high_ref.reshape(shape)),
        (q_in.at[:, :tile], low_ref.reshape(shape)),
        (rates_in.at[rows - tile :], rates_ref.at[tile:]),
        (rates_in.at[:tile], rates_ref.at[:tile]),
        (list_in, list_ref),
        (dest_in, dest_ref),
    ]
    copies = [
        pltpu.make_async_copy(source, target, arrived.at[i])
        for i, (source, target) in enumerate(pairs)
    ]
    for copy in copies:
        copy.start()
    copies[4].wait()
    copies[5].wait()
    lane = lax.broadcasted_iota(jnp.int32, (SUB, LANES), 1)
    hits = jnp.zeros((SUB, LANES), jnp.float32)
    for j in range(list_ref.shape[0]):
        target = jnp.where(list_ref[j] < blocks, dest_ref[j], -1)
        hits = hits + jnp.where(lane == target, 1.0, 0.0)
    hits_ref[...] = hits
    for copy in copies[:4]:
        copy.wait()

    def write(up_ref, down_ref):
        for half in range(halves):
            start = half * part
            for j in range(BEHIND):
                at = start + j * species
                up_ref[at : at + species, :] = high_ref[
                    pl.ds(half * SUB + SUB - BEHIND + j, species, stride=tile), :
                ]
                if j < AHEAD:
                    value = low_ref[pl.ds(half * SUB + j, species, stride=tile), :]
                else:
                    value = jnp.zeros((species, LANES), jnp.float32)
                down_ref[at : at + species, :] = value
            at = start + BEHIND * species
            up_ref[at : at + SUB, :] = rates_ref[tile + half * SUB : tile + (half + 1) * SUB, :]
            down_ref[at : at + SUB, :] = rates_ref[half * SUB : (half + 1) * SUB, :]
        up_ref[halves * part :, :] = hits
        down_ref[halves * part :, :] = hits

    even = lax.rem(lax.axis_index("tile"), 2) == 0

    @pl.when(even)
    def _():
        write(even_ref, odd_ref)

    @pl.when(jnp.logical_not(even))
    def _():
        write(odd_ref, even_ref)


def inner_kernel(dests, length, halves, q_ref, rates_ref, *out_refs):
    species = out_refs[0].shape[0]
    share = length // dests
    me = lax.axis_index("spec")
    for k in range(dests):
        first = lax.rem(me + k, dests) * share
        below = jnp.maximum(first - SUB, 0)
        above = jnp.minimum(first + share, length - SUB)
        for half in range(halves):

            def start(at):
                if at < 0:
                    return below * halves + spot(at + SUB, half, halves)
                if at >= share:
                    return above * halves + spot(at - share, half, halves)
                return first * halves + spot(at, half, halves)

            reach = range(-BEHIND, share + AHEAD)
            rows = [q_ref[pl.ds(start(at), species, stride=length * halves), :] for at in reach]
            rates = [
                with_damp(rates_ref[pl.ds(start(at), 1), :], (species, LANES)) for at in reach
            ]
            for at, value in enumerate(two_sweeps(rows, rates)):
                place = (at * halves + half) * LANES
                out_refs[k][:, place : place + LANES] = value.astype(jnp.bfloat16)


def edge_kernel(
    dests, length, halves, odd_ref, even_ref, hits_ref, q_ref, rates_ref, *refs
):
    in_refs, out_refs, (to_even_ref, to_odd_ref, known_ref) = (
        refs[:dests], refs[dests : 2 * dests], refs[2 * dests :]
    )
    species, cells = out_refs[0].shape
    me = lax.axis_index("spec")
    part = BEHIND * species + SUB
    reach = BEHIND + AHEAD
    even = lax.rem(lax.axis_index("tile"), 2) == 0
    own, from_even, from_odd = hits_ref[...], even_ref[halves * part :, :], odd_ref[halves * part :, :]
    known_ref[...] = own + from_even + from_odd
    to_even_ref[...] = from_odd
    to_odd_ref[...] = from_even

    def message(behind, at, size):
        a, b = odd_ref[at : at + size, :], even_ref[at : at + size, :]
        return jnp.where(even, a, b) if behind else jnp.where(even, b, a)

    def row(at, half):
        return q_ref[pl.ds(spot(at, half, halves), species, stride=length * halves), :]

    def rates_of(values):
        return [with_damp(value, (species, LANES)) for value in values]

    tops, bottoms = [], []
    for half in range(halves):
        base = half * part
        behind = [message(True, base + j * species, species) for j in range(BEHIND)]
        ahead = [message(False, base + j * species, species) for j in range(AHEAD)]
        before = message(True, base + BEHIND * species, SUB)
        after = message(False, base + BEHIND * species, SUB)

        def own_rates(first):
            places = [spot(first + j, half, halves) for j in range(reach)]
            return [rates_ref[at : at + 1, :] for at in places]

        tops.append(
            two_sweeps(
                behind + [row(j, half) for j in range(reach)],
                rates_of([before[SUB - BEHIND + j :][:1] for j in range(BEHIND)] + own_rates(0)),
            )
        )
        bottoms.append(
            two_sweeps(
                [row(length - reach + j, half) for j in range(reach)] + ahead,
                rates_of(own_rates(length - reach) + [after[j : j + 1] for j in range(AHEAD)]),
            )
        )
    for k, (in_ref, out_ref) in enumerate(zip(in_refs, out_refs)):
        dest = lax.rem(me + k, dests)
        out_ref[...] = in_ref[...]

        @pl.when(dest == 0)
        def _():
            for half in range(halves):
                for j, value in enumerate(tops[half]):
                    at = (j * halves + half) * LANES
                    out_ref[:, at : at + LANES] = value.astype(jnp.bfloat16)

        @pl.when(dest == dests - 1)
        def _():
            for half in range(halves):
                for j, value in enumerate(bottoms[half]):
                    at = cells + ((j - AHEAD) * halves + half) * LANES
                    out_ref[:, at : at + LANES] = value.astype(jnp.bfloat16)


def weight_kernel(blocks, w1_ref, w2_ref, list_ref, after_ref, w1_out, w2_out, listed_out):
    slots = list_ref.shape[0]
    for j in range(slots + 1):
        listed_out[j] = blocks
    count = jnp.int32(0)
    for j in range(slots):
        block = list_ref[j]
        listed_out[count] = block
        count = count + jnp.where(block < blocks, 1, 0)
    listed_out[count] = blocks
    listed_out[slots] = count
    w1_out[...] = (0.5 * w1_ref[...].astype(jnp.float32)).T.astype(jnp.bfloat16)
    w2_out[...] = (0.5 * w2_ref[...].astype(jnp.float32)).T.astype(jnp.bfloat16)


def chemistry_kernel(
    groups, list_ref, w1_ref, w2_ref, w3_ref, known_ref, odd_ref, even_ref, *refs
):
    parts, (out_ref, share_ref, state_ref, picked_ref, held_ref, done) = refs[:groups], refs[groups:]
    species, cells = state_ref.shape[1:]
    slots = list_ref.shape[0] - 1
    blocks = cells // BLK
    me = lax.axis_index("spec")
    for k in range(groups):
        state_ref[lax.rem(me - k + groups, groups)] = parts[k][...]
    hits = known_ref[...] + even_ref[...] + odd_ref[...]
    lane = lax.broadcasted_iota(jnp.int32, hits.shape, 1)
    mine = jnp.where(lane == lax.axis_index("tile"), hits, 0.0)
    held_ref[...] = jnp.sum(mine[0:1], axis=1, keepdims=True) / RECV
    share = pltpu.make_async_copy(held_ref, share_ref, done.at[0])
    share.start()

    def place(j):
        return pl.ds(pl.multiple_of(jnp.minimum(list_ref[j], blocks - 1) * BLK, BLK), BLK)

    count = list_ref[slots]
    each = 4
    for first in range(0, slots, each):

        @pl.when(first < count)
        def _():
            for j in range(each):
                for g in range(groups):
                    picked_ref[g * species : (g + 1) * species, j * BLK : (j + 1) * BLK] = state_ref[
                        g, :, place(first + j)
                    ].astype(jnp.float32)
            x = picked_ref[...]
            hidden = jnp.dot(
                w1_ref[...], x.astype(jnp.bfloat16), preferred_element_type=jnp.float32
            )
            hidden = silu_of_half(hidden).astype(jnp.bfloat16)
            hidden = jnp.dot(w2_ref[...], hidden, preferred_element_type=jnp.float32)
            hidden = silu_of_half(hidden).astype(jnp.bfloat16)
            fresh = x + jnp.dot(w3_ref[...], hidden, preferred_element_type=jnp.float32)
            for j in range(each):
                valid = first + j < count
                for g in range(groups):
                    now = state_ref[g, :, place(first + j)].astype(jnp.float32)
                    new = fresh[g * species : (g + 1) * species, j * BLK : (j + 1) * BLK]
                    state_ref[g, :, place(first + j)] = jnp.where(valid, new, now).astype(
                        jnp.bfloat16
                    )

    whole = pltpu.make_async_copy(state_ref, out_ref, done.at[1])
    whole.start()
    share.wait()
    whole.wait()


def vmem():
    return pl.BlockSpec(memory_space=pltpu.VMEM)


def anywhere():
    return pl.BlockSpec(memory_space=pl.ANY)


def from_hbm(x):
    return pltpu.with_memory_space_constraint(x, pltpu.HBM)


def cost(us):
    return pl.CostEstimate(flops=int(us * 1e9), bytes_accessed=int(us * 3e6), transcendentals=0)


def shards(
    concentrations, courant, first_weight, middle_weight, last_weight, active_blocks, dest_tile
):
    species, length, cols = concentrations.shape
    dests = lax.axis_size("spec")
    tiles = lax.axis_size("tile")
    cells = length // dests * cols
    slots = active_blocks.shape[-1]
    halves = cols // LANES
    f32, bf16 = jnp.float32, jnp.bfloat16
    params = pltpu.CompilerParams(vmem_limit_bytes=VMEM_BYTES)
    size = halves * (BEHIND * species + SUB) + SUB
    flag = jax.ShapeDtypeStruct((SUB, LANES), f32)

    field, rates = tiled(concentrations, halves), tiled(courant, halves)
    to_even, to_odd, hits = pl.pallas_call(
        functools.partial(pack_kernel, length, halves, cells // BLK),
        out_shape=[jax.ShapeDtypeStruct((size, LANES), f32)] * 2 + [flag],
        in_specs=[anywhere()] * 4,
        out_specs=[vmem()] * 3,
        scratch_shapes=[
            pltpu.VMEM((species * halves * SUB, LANES), f32),
            pltpu.VMEM((species * halves * SUB, LANES), f32),
            pltpu.VMEM((2 * halves * SUB, LANES), f32),
            pltpu.SMEM((slots,), jnp.int32),
            pltpu.SMEM((slots,), jnp.int32),
            pltpu.SemaphoreType.DMA((6,)),
        ],
        compiler_params=params,
        cost_estimate=cost(1.0),
        name="pack_edges",
    )(
        from_hbm(field),
        from_hbm(rates),
        from_hbm(active_blocks.reshape(-1)),
        from_hbm(dest_tile.reshape(-1)),
    )
    field = field.reshape(species * length * halves, LANES)
    evens = [(t, t ^ 1) for t in range(tiles)]
    odds = [(t, ((t + 1) ^ 1) - 1) for t in range(tiles)]
    odds = [(t, other % tiles) for t, other in odds]
    from_odd = lax.ppermute(to_odd, "tile", odds)
    from_even = lax.ppermute(to_even, "tile", evens)
    block = jax.ShapeDtypeStruct((species, cells), bf16)
    blocks = pl.pallas_call(
        functools.partial(inner_kernel, dests, length, halves),
        out_shape=[block] * dests,
        in_specs=[vmem()] * 2,
        out_specs=[vmem()] * dests,
        compiler_params=params,
        cost_estimate=cost(1.0),
        name="inner_rows",
    )(field, rates)
    *blocks, to_even, to_odd, known = pl.pallas_call(
        functools.partial(edge_kernel, dests, length, halves),
        out_shape=[block] * dests + [flag] * 3,
        in_specs=[vmem()] * (5 + dests),
        out_specs=[vmem()] * (dests + 3),
        compiler_params=params,
        cost_estimate=cost(0.1),
        name="edge_rows",
    )(from_odd, from_even, hits, field, rates, *blocks)
    received = [blocks[0]] + [
        lax.ppermute(blocks[k], "spec", [(s, (s + k) % dests) for s in range(dests)])
        for k in range(1, dests)
    ]
    from_odd = lax.ppermute(to_odd, "tile", odds)
    from_even = lax.ppermute(to_even, "tile", evens)
    w1, w2, listing = pl.pallas_call(
        functools.partial(weight_kernel, cells // BLK),
        out_shape=[jax.ShapeDtypeStruct(w.shape[::-1], bf16) for w in (first_weight, middle_weight)]
        + [jax.ShapeDtypeStruct((slots + 1,), jnp.int32)],
        in_specs=[vmem()] * 2 + [pl.BlockSpec(memory_space=pltpu.SMEM), anywhere()],
        out_specs=[vmem()] * 2 + [pl.BlockSpec(memory_space=pltpu.SMEM)],
        compiler_params=params,
        cost_estimate=cost(0.5),
        name="halved_weights",
    )(first_weight, middle_weight, active_blocks.reshape(-1), known)
    out, load_share = pl.pallas_call(
        functools.partial(chemistry_kernel, dests),
        out_shape=[
            jax.ShapeDtypeStruct((dests, species, cells), bf16),
            jax.ShapeDtypeStruct((1, 1), f32),
        ],
        in_specs=[pl.BlockSpec(memory_space=pltpu.SMEM)] + [vmem()] * (6 + dests),
        out_specs=[anywhere()] * 2,
        scratch_shapes=[
            pltpu.VMEM((dests, species, cells), bf16),
            pltpu.VMEM((dests * species, 4 * BLK), f32),
            pltpu.VMEM((1, 1), f32),
            pltpu.SemaphoreType.DMA((2,)),
        ],
        compiler_params=params,
        cost_estimate=cost(4.0),
        name="chemistry",
    )(
        listing,
        w1,
        w2,
        last_weight.T,
        known,
        from_odd,
        from_even,
        *received,
    )
    return out.reshape(dests * species, cells), load_share


def solution(mesh):
    in_specs = (
        P("spec", "tile", None),
        P("tile", None),
        P(),
        P(),
        P(),
        P("tile", "spec", None),
        P("tile", "spec", None),
    )
    out_specs = (P(None, ("tile", "spec")), P("tile", "spec"))
    return jax.shard_map(shards, mesh=mesh, in_specs=in_specs, out_specs=out_specs, check_vma=False)
```

```python
import functools

import jax
import jax.numpy as jnp
from jax import lax
from jax.experimental import pallas as pl
from jax.experimental.pallas import tpu as pltpu
from jax.sharding import PartitionSpec as P

BLK = 128
RECV = 8
LANES = 128
SUB = 8
EACH = 4
BEHIND = 4
AHEAD = 2
VMEM_BYTES = 16 * 1024 * 1024


def silu_of_half(half):
    return half + half * jnp.tanh(half)


def sweep_rows(rows, rates):
    diffs = [b - a for a, b in zip(rows[:-1], rows[1:])]
    fluxes = []
    for at in range(1, len(rows) - 1):
        left, right = diffs[at - 1], diffs[at]
        slope = jnp.maximum(jnp.minimum(left, right), 0.0) + jnp.minimum(
            jnp.maximum(left, right), 0.0
        )
        rate, damp = rates[at]
        fluxes.append(rate * (rows[at] + damp * slope))
    return [rows[at] - fluxes[at - 1] + fluxes[at - 2] for at in range(2, len(rows) - 1)]


def two_sweeps(rows, rates):
    once = sweep_rows(rows, rates)
    return sweep_rows(once, rates[2:-1])


def with_damp(rate, shape):
    rate = jnp.broadcast_to(rate, shape)
    return rate, 0.5 - 0.5 * rate


def tiled(x, halves):
    lead, (rows, cols) = x.shape[:-2], x.shape[-2:]
    x = x.reshape(lead + (rows // SUB, SUB, halves, LANES))
    axes = tuple(range(len(lead)))
    x = x.transpose(axes + tuple(len(lead) + a for a in (0, 2, 1, 3)))
    return x.reshape(lead + (rows * halves, LANES))


def spot(at, half, halves):
    return (at // SUB * halves + half) * SUB + at % SUB


def pack_kernel(
    length, halves, blocks, q_in, rates_in, list_in, dest_in,
    even_ref, odd_ref, hits_ref, low_ref, high_ref, rates_ref, list_ref, dest_ref, arrived,
):
    species, rows = q_in.shape[:2]
    tile = halves * SUB
    part = BEHIND * species + SUB
    shape = (species, tile, LANES)
    pairs = [
        (q_in.at[:, rows - tile :], high_ref.reshape(shape)),
        (q_in.at[:, :tile], low_ref.reshape(shape)),
        (rates_in.at[rows - tile :], rates_ref.at[tile:]),
        (rates_in.at[:tile], rates_ref.at[:tile]),
        (list_in, list_ref),
        (dest_in, dest_ref),
    ]
    copies = [
        pltpu.make_async_copy(source, target, arrived.at[i])
        for i, (source, target) in enumerate(pairs)
    ]
    for copy in copies:
        copy.start()
    copies[4].wait()
    copies[5].wait()
    lane = lax.broadcasted_iota(jnp.int32, (SUB, LANES), 1)
    hits = jnp.zeros((SUB, LANES), jnp.float32)
    for j in range(list_ref.shape[0]):
        target = jnp.where(list_ref[j] < blocks, dest_ref[j], -1)
        hits = hits + jnp.where(lane == target, 1.0, 0.0)
    hits_ref[...] = hits
    for copy in copies[:4]:
        copy.wait()

    def write(up_ref, down_ref):
        for half in range(halves):
            start = half * part
            for j in range(BEHIND):
                at = start + j * species
                up_ref[at : at + species, :] = high_ref[
                    pl.ds(half * SUB + SUB - BEHIND + j, species, stride=tile), :
                ]
                if j < AHEAD:
                    value = low_ref[pl.ds(half * SUB + j, species, stride=tile), :]
                else:
                    value = jnp.zeros((species, LANES), jnp.float32)
                down_ref[at : at + species, :] = value
            at = start + BEHIND * species
            up_ref[at : at + SUB, :] = rates_ref[tile + half * SUB : tile + (half + 1) * SUB, :]
            down_ref[at : at + SUB, :] = rates_ref[half * SUB : (half + 1) * SUB, :]
        up_ref[halves * part :, :] = hits
        down_ref[halves * part :, :] = hits

    even = lax.rem(lax.axis_index("tile"), 2) == 0

    @pl.when(even)
    def _():
        write(even_ref, odd_ref)

    @pl.when(jnp.logical_not(even))
    def _():
        write(odd_ref, even_ref)


def inner_kernel(dests, length, halves, q_ref, rates_ref, *out_refs):
    species = out_refs[0].shape[0]
    share = length // dests
    me = lax.axis_index("spec")
    for k in range(dests):
        first = lax.rem(me + k, dests) * share
        below = jnp.maximum(first - SUB, 0)
        above = jnp.minimum(first + share, length - SUB)
        for half in range(halves):

            def start(at):
                if at < 0:
                    return below * halves + spot(at + SUB, half, halves)
                if at >= share:
                    return above * halves + spot(at - share, half, halves)
                return first * halves + spot(at, half, halves)

            reach = range(-BEHIND, share + AHEAD)
            rows = [q_ref[pl.ds(start(at), species, stride=length * halves), :] for at in reach]
            rates = [
                with_damp(rates_ref[pl.ds(start(at), 1), :], (species, LANES)) for at in reach
            ]
            for at, value in enumerate(two_sweeps(rows, rates)):
                place = (at * halves + half) * LANES
                out_refs[k][:, place : place + LANES] = value.astype(jnp.bfloat16)


def edge_kernel(
    dests, length, halves, odd_ref, even_ref, hits_ref, q_ref, rates_ref, *refs
):
    in_refs, out_refs, (to_even_ref, to_odd_ref, known_ref) = (
        refs[:dests], refs[dests : 2 * dests], refs[2 * dests :]
    )
    species, cells = out_refs[0].shape
    me = lax.axis_index("spec")
    part = BEHIND * species + SUB
    reach = BEHIND + AHEAD
    even = lax.rem(lax.axis_index("tile"), 2) == 0
    own, from_even, from_odd = hits_ref[...], even_ref[halves * part :, :], odd_ref[halves * part :, :]
    known_ref[...] = own + from_even + from_odd
    to_even_ref[...] = from_odd
    to_odd_ref[...] = from_even

    def message(behind, at, size):
        a, b = odd_ref[at : at + size, :], even_ref[at : at + size, :]
        return jnp.where(even, a, b) if behind else jnp.where(even, b, a)

    def row(at, half):
        return q_ref[pl.ds(spot(at, half, halves), species, stride=length * halves), :]

    def rates_of(values):
        return [with_damp(value, (species, LANES)) for value in values]

    tops, bottoms = [], []
    for half in range(halves):
        base = half * part
        behind = [message(True, base + j * species, species) for j in range(BEHIND)]
        ahead = [message(False, base + j * species, species) for j in range(AHEAD)]
        before = message(True, base + BEHIND * species, SUB)
        after = message(False, base + BEHIND * species, SUB)

        def own_rates(first):
            places = [spot(first + j, half, halves) for j in range(reach)]
            return [rates_ref[at : at + 1, :] for at in places]

        tops.append(
            two_sweeps(
                behind + [row(j, half) for j in range(reach)],
                rates_of([before[SUB - BEHIND + j :][:1] for j in range(BEHIND)] + own_rates(0)),
            )
        )
        bottoms.append(
            two_sweeps(
                [row(length - reach + j, half) for j in range(reach)] + ahead,
                rates_of(own_rates(length - reach) + [after[j : j + 1] for j in range(AHEAD)]),
            )
        )
    for k, (in_ref, out_ref) in enumerate(zip(in_refs, out_refs)):
        dest = lax.rem(me + k, dests)
        out_ref[...] = in_ref[...]

        @pl.when(dest == 0)
        def _():
            for half in range(halves):
                for j, value in enumerate(tops[half]):
                    at = (j * halves + half) * LANES
                    out_ref[:, at : at + LANES] = value.astype(jnp.bfloat16)

        @pl.when(dest == dests - 1)
        def _():
            for half in range(halves):
                for j, value in enumerate(bottoms[half]):
                    at = cells + ((j - AHEAD) * halves + half) * LANES
                    out_ref[:, at : at + LANES] = value.astype(jnp.bfloat16)


def weight_kernel(blocks, w1_ref, w2_ref, list_ref, after_ref, w1_out, w2_out, listed_out):
    slots = list_ref.shape[0]
    for j in range(slots + 1):
        listed_out[j] = blocks
    count = jnp.int32(0)
    for j in range(slots):
        block = list_ref[j]
        listed_out[count] = block
        count = count + jnp.where(block < blocks, 1, 0)
    listed_out[count] = blocks
    listed_out[slots] = count
    w1_out[...] = (0.5 * w1_ref[...].astype(jnp.float32)).T.astype(jnp.bfloat16)
    w2_out[...] = (0.5 * w2_ref[...].astype(jnp.float32)).T.astype(jnp.bfloat16)


def chemistry_kernel(
    groups, list_ref, w1_ref, w2_ref, w3_ref, known_ref, odd_ref, even_ref, *refs
):
    parts, (out_ref, share_ref, picked_ref, fresh_ref, held_ref, done) = refs[:groups], refs[groups:]
    species, cells = parts[0].shape
    slots = list_ref.shape[0] - 1
    blocks = cells // BLK
    me = lax.axis_index("spec")
    sources = [lax.rem(me - k + groups, groups) for k in range(groups)]
    copies = [
        pltpu.make_async_copy(part, out_ref.at[source], done.at[k])
        for k, (part, source) in enumerate(zip(parts, sources))
    ]
    for copy in copies:
        copy.start()
    hits = known_ref[...] + odd_ref[...] + even_ref[...]
    lane = lax.broadcasted_iota(jnp.int32, hits.shape, 1)
    mine = jnp.where(lane == lax.axis_index("tile"), hits, 0.0)
    held_ref[...] = jnp.sum(mine[0:1], axis=1, keepdims=True) / RECV
    copies.append(pltpu.make_async_copy(held_ref, share_ref, done.at[groups]))
    copies[groups].start()
    count = list_ref[slots]

    def place(j):
        return pl.ds(pl.multiple_of(jnp.minimum(list_ref[j], blocks - 1) * BLK, BLK), BLK)

    def integrate(first, number):
        for j in range(number):
            for part, source in zip(parts, sources):
                rows = pl.ds(pl.multiple_of(source * species, species), species)
                picked_ref[rows, j * BLK : (j + 1) * BLK] = part[:, place(first + j)].astype(
                    jnp.float32
                )
        width = min(number, EACH) * BLK
        spans = [slice(at, at + width) for at in range(0, number * BLK, width)]
        x = [picked_ref[:, span] for span in spans]
        hidden = [
            jnp.dot(w1_ref[...], v.astype(jnp.bfloat16), preferred_element_type=jnp.float32)
            for v in x
        ]
        hidden = [silu_of_half(v).astype(jnp.bfloat16) for v in hidden]
        hidden = [jnp.dot(w2_ref[...], v, preferred_element_type=jnp.float32) for v in hidden]
        hidden = [silu_of_half(v).astype(jnp.bfloat16) for v in hidden]
        for i, (v, h) in enumerate(zip(x, hidden)):
            v = v + jnp.dot(w3_ref[...], h, preferred_element_type=jnp.float32)
            for j in range(width // BLK):
                for g in range(groups):
                    fresh_ref[first + i * width // BLK + j, g] = v[
                        g * species : (g + 1) * species, j * BLK : (j + 1) * BLK
                    ].astype(jnp.bfloat16)

    for first in range(0, slots, 2 * EACH):
        left = count - first

        @pl.when((left > 0) & (left <= EACH))
        def _():
            integrate(first, EACH)

        @pl.when(left > EACH)
        def _():
            integrate(first, 2 * EACH)

    for copy in copies:
        copy.wait()

    def for_listed(act):
        for first in range(0, slots, EACH):

            @pl.when(first < count)
            def _():
                for j in range(first, first + EACH):

                    @pl.when(j < count)
                    def _():
                        act(
                            pltpu.make_async_copy(
                                fresh_ref.at[j], out_ref.at[:, :, place(j)], done.at[groups + 1 + j]
                            )
                        )

    for_listed(lambda copy: copy.start())
    for_listed(lambda copy: copy.wait())


def vmem():
    return pl.BlockSpec(memory_space=pltpu.VMEM)


def anywhere():
    return pl.BlockSpec(memory_space=pl.ANY)


def from_hbm(x):
    return pltpu.with_memory_space_constraint(x, pltpu.HBM)


def cost(us):
    return pl.CostEstimate(flops=int(us * 1e9), bytes_accessed=int(us * 3e6), transcendentals=0)


def shards(
    concentrations, courant, first_weight, middle_weight, last_weight, active_blocks, dest_tile
):
    species, length, cols = concentrations.shape
    dests = lax.axis_size("spec")
    tiles = lax.axis_size("tile")
    cells = length // dests * cols
    slots = active_blocks.shape[-1]
    halves = cols // LANES
    f32, bf16 = jnp.float32, jnp.bfloat16
    params = pltpu.CompilerParams(vmem_limit_bytes=VMEM_BYTES)
    size = halves * (BEHIND * species + SUB) + SUB
    flag = jax.ShapeDtypeStruct((SUB, LANES), f32)

    field, rates = tiled(concentrations, halves), tiled(courant, halves)
    to_even, to_odd, hits = pl.pallas_call(
        functools.partial(pack_kernel, length, halves, cells // BLK),
        out_shape=[jax.ShapeDtypeStruct((size, LANES), f32)] * 2 + [flag],
        in_specs=[anywhere()] * 4,
        out_specs=[vmem()] * 3,
        scratch_shapes=[
            pltpu.VMEM((species * halves * SUB, LANES), f32),
            pltpu.VMEM((species * halves * SUB, LANES), f32),
            pltpu.VMEM((2 * halves * SUB, LANES), f32),
            pltpu.SMEM((slots,), jnp.int32),
            pltpu.SMEM((slots,), jnp.int32),
            pltpu.SemaphoreType.DMA((6,)),
        ],
        compiler_params=params,
        cost_estimate=cost(1.0),
        name="pack_edges",
    )(
        from_hbm(field),
        from_hbm(rates),
        from_hbm(active_blocks.reshape(-1)),
        from_hbm(dest_tile.reshape(-1)),
    )
    field = field.reshape(species * length * halves, LANES)
    evens = [(t, t ^ 1) for t in range(tiles)]
    odds = [(t, ((t + 1) ^ 1) - 1) for t in range(tiles)]
    odds = [(t, other % tiles) for t, other in odds]
    from_odd = lax.ppermute(to_odd, "tile", odds)
    from_even = lax.ppermute(to_even, "tile", evens)
    block = jax.ShapeDtypeStruct((species, cells), bf16)
    blocks = pl.pallas_call(
        functools.partial(inner_kernel, dests, length, halves),
        out_shape=[block] * dests,
        in_specs=[vmem()] * 2,
        out_specs=[vmem()] * dests,
        compiler_params=params,
        cost_estimate=cost(1.0),
        name="inner_rows",
    )(field, rates)
    *blocks, to_even, to_odd, known = pl.pallas_call(
        functools.partial(edge_kernel, dests, length, halves),
        out_shape=[block] * dests + [flag] * 3,
        in_specs=[vmem()] * (5 + dests),
        out_specs=[vmem()] * (dests + 3),
        compiler_params=params,
        cost_estimate=cost(0.1),
        name="edge_rows",
    )(from_odd, from_even, hits, field, rates, *blocks)
    received = [blocks[0]] + [
        lax.ppermute(blocks[k], "spec", [(s, (s + k) % dests) for s in range(dests)])
        for k in range(1, dests)
    ]
    from_odd = lax.ppermute(to_odd, "tile", odds)
    from_even = lax.ppermute(to_even, "tile", evens)
    w1, w2, listing = pl.pallas_call(
        functools.partial(weight_kernel, cells // BLK),
        out_shape=[jax.ShapeDtypeStruct(w.shape[::-1], bf16) for w in (first_weight, middle_weight)]
        + [jax.ShapeDtypeStruct((slots + 1,), jnp.int32)],
        in_specs=[vmem()] * 2 + [pl.BlockSpec(memory_space=pltpu.SMEM), anywhere()],
        out_specs=[vmem()] * 2 + [pl.BlockSpec(memory_space=pltpu.SMEM)],
        compiler_params=params,
        cost_estimate=cost(0.5),
        name="halved_weights",
    )(first_weight, middle_weight, active_blocks.reshape(-1), known)
    out, load_share = pl.pallas_call(
        functools.partial(chemistry_kernel, dests),
        out_shape=[
            jax.ShapeDtypeStruct((dests, species, cells), bf16),
            jax.ShapeDtypeStruct((1, 1), f32),
        ],
        in_specs=[pl.BlockSpec(memory_space=pltpu.SMEM)] + [vmem()] * (6 + dests),
        out_specs=[anywhere()] * 2,
        scratch_shapes=[
            pltpu.VMEM((dests * species, 2 * EACH * BLK), f32),
            pltpu.VMEM((slots, dests, species, BLK), bf16),
            pltpu.VMEM((1, 1), f32),
            pltpu.SemaphoreType.DMA((dests + 1 + slots,)),
        ],
        compiler_params=params,
        cost_estimate=cost(4.0),
        name="chemistry",
    )(
        listing,
        w1,
        w2,
        last_weight.T,
        known,
        from_odd,
        from_even,
        *received,
    )
    return out.reshape(dests * species, cells), load_share


def solution(mesh):
    in_specs = (
        P("spec", "tile", None),
        P("tile", None),
        P(),
        P(),
        P(),
        P("tile", "spec", None),
        P("tile", "spec", None),
    )
    out_specs = (P(None, ("tile", "spec")), P("tile", "spec"))
    return jax.shard_map(shards, mesh=mesh, in_specs=in_specs, out_specs=out_specs, check_vma=False)
```

```python
import functools

import jax
import jax.numpy as jnp
from jax import lax
from jax.experimental import pallas as pl
from jax.experimental.pallas import tpu as pltpu
from jax.sharding import PartitionSpec as P

BLK = 128
RECV = 8
LANES = 128
SUB = 8
EACH = 4
COPIES = 5
BEHIND = 4
AHEAD = 2
VMEM_BYTES = 16 * 1024 * 1024


def silu_of_half(half):
    return half + half * jnp.tanh(half)


def sweep_rows(rows, rates):
    diffs = [b - a for a, b in zip(rows[:-1], rows[1:])]
    fluxes = []
    for at in range(1, len(rows) - 1):
        left, right = diffs[at - 1], diffs[at]
        slope = jnp.maximum(jnp.minimum(left, right), 0.0) + jnp.minimum(
            jnp.maximum(left, right), 0.0
        )
        rate, damp = rates[at]
        fluxes.append(rate * (rows[at] + damp * slope))
    return [rows[at] - fluxes[at - 1] + fluxes[at - 2] for at in range(2, len(rows) - 1)]


def two_sweeps(rows, rates):
    once = sweep_rows(rows, rates)
    return sweep_rows(once, rates[2:-1])


def with_damp(rate, shape):
    rate = jnp.broadcast_to(rate, shape)
    return rate, 0.5 - 0.5 * rate


def tiled(x, halves):
    lead, (rows, cols) = x.shape[:-2], x.shape[-2:]
    x = x.reshape(lead + (rows // SUB, SUB, halves, LANES))
    axes = tuple(range(len(lead)))
    x = x.transpose(axes + tuple(len(lead) + a for a in (0, 2, 1, 3)))
    return x.reshape(lead + (rows * halves, LANES))


def spot(at, half, halves):
    return (at // SUB * halves + half) * SUB + at % SUB


def pack_kernel(
    length, halves, blocks, q_in, rates_in, list_in, dest_in, row_in,
    even_ref, odd_ref, hits_ref, row_ref, low_ref, high_ref, rates_ref, list_ref, dest_ref, arrived,
):
    species, rows = q_in.shape[:2]
    tile = halves * SUB
    part = BEHIND * species + SUB
    shape = (species, tile, LANES)
    pairs = [
        (q_in.at[:, rows - tile :], high_ref.reshape(shape)),
        (q_in.at[:, :tile], low_ref.reshape(shape)),
        (rates_in.at[rows - tile :], rates_ref.at[tile:]),
        (rates_in.at[:tile], rates_ref.at[:tile]),
        (list_in, list_ref),
        (dest_in, dest_ref),
        (row_in, row_ref),
    ]
    copies = [
        pltpu.make_async_copy(source, target, arrived.at[i])
        for i, (source, target) in enumerate(pairs)
    ]
    for copy in copies:
        copy.start()
    copies[4].wait()
    copies[5].wait()
    lane = lax.broadcasted_iota(jnp.int32, (SUB, LANES), 1)
    hits = jnp.zeros((SUB, LANES), jnp.float32)
    for j in range(list_ref.shape[0]):
        target = jnp.where(list_ref[j] < blocks, dest_ref[j], -1)
        hits = hits + jnp.where(lane == target, 1.0, 0.0)
    hits_ref[...] = hits
    for copy in copies[:4] + copies[6:]:
        copy.wait()

    def write(up_ref, down_ref):
        for half in range(halves):
            start = half * part
            for j in range(BEHIND):
                at = start + j * species
                up_ref[at : at + species, :] = high_ref[
                    pl.ds(half * SUB + SUB - BEHIND + j, species, stride=tile), :
                ]
                if j < AHEAD:
                    value = low_ref[pl.ds(half * SUB + j, species, stride=tile), :]
                else:
                    value = jnp.zeros((species, LANES), jnp.float32)
                down_ref[at : at + species, :] = value
            at = start + BEHIND * species
            up_ref[at : at + SUB, :] = rates_ref[tile + half * SUB : tile + (half + 1) * SUB, :]
            down_ref[at : at + SUB, :] = rates_ref[half * SUB : (half + 1) * SUB, :]
        up_ref[halves * part :, :] = hits
        down_ref[halves * part :, :] = hits

    even = lax.rem(lax.axis_index("tile"), 2) == 0

    @pl.when(even)
    def _():
        write(even_ref, odd_ref)

    @pl.when(jnp.logical_not(even))
    def _():
        write(odd_ref, even_ref)


def inner_kernel(dests, length, halves, q_ref, rates_ref, *out_refs):
    species = out_refs[0].shape[0]
    share = length // dests
    me = lax.axis_index("spec")
    for k in range(dests):
        first = lax.rem(me + k, dests) * share
        below = jnp.maximum(first - SUB, 0)
        above = jnp.minimum(first + share, length - SUB)
        for half in range(halves):

            def start(at):
                if at < 0:
                    return below * halves + spot(at + SUB, half, halves)
                if at >= share:
                    return above * halves + spot(at - share, half, halves)
                return first * halves + spot(at, half, halves)

            reach = range(-BEHIND, share + AHEAD)
            rows = [q_ref[pl.ds(start(at), species, stride=length * halves), :] for at in reach]
            rates = [
                with_damp(rates_ref[pl.ds(start(at), 1), :], (species, LANES)) for at in reach
            ]
            for at, value in enumerate(two_sweeps(rows, rates)):
                place = (at * halves + half) * LANES
                out_refs[k][:, place : place + LANES] = value.astype(jnp.bfloat16)


def edge_kernel(
    dests, early, late, length, halves, odd_ref, even_ref, hits_ref, q_ref, rates_ref, *refs
):
    in_refs, out_refs, refs = refs[: len(late)], refs[len(late) : 2 * len(late)], refs[2 * len(late) :]
    *small_refs, to_even_ref, to_odd_ref, known_ref = refs
    species, cells = out_refs[0].shape
    me = lax.axis_index("spec")
    part = BEHIND * species + SUB
    reach = BEHIND + AHEAD
    even = lax.rem(lax.axis_index("tile"), 2) == 0
    own, from_even, from_odd = hits_ref[...], even_ref[halves * part :, :], odd_ref[halves * part :, :]
    known_ref[...] = own + from_even + from_odd
    to_even_ref[...] = from_odd
    to_odd_ref[...] = jnp.concatenate([from_even] * COPIES)

    def message(behind, at, size):
        a, b = odd_ref[at : at + size, :], even_ref[at : at + size, :]
        return jnp.where(even, a, b) if behind else jnp.where(even, b, a)

    def row(at, half):
        return q_ref[pl.ds(spot(at, half, halves), species, stride=length * halves), :]

    def rates_of(values):
        return [with_damp(value, (species, LANES)) for value in values]

    tops, bottoms = [], []
    for half in range(halves):
        base = half * part
        behind = [message(True, base + j * species, species) for j in range(BEHIND)]
        ahead = [message(False, base + j * species, species) for j in range(AHEAD)]
        before = message(True, base + BEHIND * species, SUB)
        after = message(False, base + BEHIND * species, SUB)

        def own_rates(first):
            places = [spot(first + j, half, halves) for j in range(reach)]
            return [rates_ref[at : at + 1, :] for at in places]

        tops.append(
            two_sweeps(
                behind + [row(j, half) for j in range(reach)],
                rates_of([before[SUB - BEHIND + j :][:1] for j in range(BEHIND)] + own_rates(0)),
            )
        )
        bottoms.append(
            two_sweeps(
                [row(length - reach + j, half) for j in range(reach)] + ahead,
                rates_of(own_rates(length - reach) + [after[j : j + 1] for j in range(AHEAD)]),
            )
        )
    for k, small_ref in zip(early, small_refs):
        low = lax.rem(me + k, dests) == 0
        for half in range(halves):
            for j in range(BEHIND):
                value = tops[half][j]
                if j >= BEHIND - AHEAD:
                    value = jnp.where(low, value, bottoms[half][j - BEHIND + AHEAD])
                at = (j * halves + half) * LANES
                small_ref[:, at : at + LANES] = value.astype(jnp.bfloat16)
    for k, in_ref, out_ref in zip(late, in_refs, out_refs):
        dest = lax.rem(me + k, dests)
        out_ref[...] = in_ref[...]

        @pl.when(dest == 0)
        def _():
            for half in range(halves):
                for j, value in enumerate(tops[half]):
                    at = (j * halves + half) * LANES
                    out_ref[:, at : at + LANES] = value.astype(jnp.bfloat16)

        @pl.when(dest == dests - 1)
        def _():
            for half in range(halves):
                for j, value in enumerate(bottoms[half]):
                    at = cells + ((j - AHEAD) * halves + half) * LANES
                    out_ref[:, at : at + LANES] = value.astype(jnp.bfloat16)


def weight_kernel(w1_ref, w2_ref, after_ref, w1_out, w2_out):
    w1_out[...] = (0.5 * w1_ref[...].astype(jnp.float32)).T.astype(jnp.bfloat16)
    w2_out[...] = (0.5 * w2_ref[...].astype(jnp.float32)).T.astype(jnp.bfloat16)


def chemistry_kernel(
    groups, early, named_ref, w1_ref, w2_ref, w3_ref, *refs
):
    parts, edges, refs = list(refs[:groups]), refs[groups : groups + len(early)], refs[groups + len(early) :]
    (known_ref, odd_ref, even_ref), refs = refs[:3], refs[3:]
    out_ref, share_ref, list_ref, whole_ref, picked_ref, fresh_ref, held_ref, done = refs
    species, cells = parts[0].shape
    slots = named_ref.shape[0]
    blocks = cells // BLK
    me = lax.axis_index("spec")
    sources = [lax.rem(me - k + groups, groups) for k in range(groups)]
    wide = edges[0].shape[1]
    narrow = wide // BEHIND * AHEAD
    for i, k in enumerate(early):
        whole_ref[i] = parts[k][...]
        parts[k] = whole_ref.at[i]

    @pl.when(me == 0)
    def _():
        for k, edge in zip(early, edges):
            parts[k][:, :wide] = edge[...]

    @pl.when(me == groups - 1)
    def _():
        for k, edge in zip(early, edges):
            parts[k][:, cells - narrow :] = edge[:, wide - narrow :]

    copies = [
        pltpu.make_async_copy(part, out_ref.at[source], done.at[k])
        for k, (part, source) in enumerate(zip(parts, sources))
    ]
    for copy in copies:
        copy.start()
    hits = known_ref[...] + odd_ref[:SUB] + even_ref[...]
    lane = lax.broadcasted_iota(jnp.int32, hits.shape, 1)
    mine = jnp.where(lane == lax.axis_index("tile"), hits, 0.0)
    held_ref[...] = jnp.sum(mine[0:1], axis=1, keepdims=True) / RECV
    copies.append(pltpu.make_async_copy(held_ref, share_ref, done.at[groups]))
    copies[groups].start()
    for j in range(slots):
        list_ref[j] = blocks
    count = jnp.int32(0)
    for j in range(slots):
        block = named_ref[j]
        list_ref[count] = block
        count = count + jnp.where(block < blocks, 1, 0)

    def place(j):
        return pl.ds(pl.multiple_of(jnp.minimum(list_ref[j], blocks - 1) * BLK, BLK), BLK)

    def integrate(number):
        for j in range(number):
            for part, source in zip(parts, sources):
                rows = pl.ds(pl.multiple_of(source * species, species), species)
                picked_ref[rows, j * BLK : (j + 1) * BLK] = part[:, place(j)].astype(
                    jnp.float32
                )
        width = EACH * BLK
        spans = [slice(at, at + width) for at in range(0, number * BLK, width)]
        x = [picked_ref[:, span] for span in spans]
        hidden = [
            jnp.dot(w1_ref[...], v.astype(jnp.bfloat16), preferred_element_type=jnp.float32)
            for v in x
        ]
        hidden = [silu_of_half(v).astype(jnp.bfloat16) for v in hidden]
        hidden = [jnp.dot(w2_ref[...], v, preferred_element_type=jnp.float32) for v in hidden]
        hidden = [silu_of_half(v).astype(jnp.bfloat16) for v in hidden]
        for i, (v, h) in enumerate(zip(x, hidden)):
            v = v + jnp.dot(w3_ref[...], h, preferred_element_type=jnp.float32)
            for j in range(width // BLK):
                for g in range(groups):
                    fresh_ref[i * EACH + j, g] = v[
                        g * species : (g + 1) * species, j * BLK : (j + 1) * BLK
                    ].astype(jnp.bfloat16)

    for number in range(EACH, slots + 1, EACH):

        @pl.when((count > number - EACH) & (count <= number))
        def _():
            integrate(number)

    for copy in copies:
        copy.wait()

    def for_listed(act):
        for first in range(0, slots, EACH):

            @pl.when(first < count)
            def _():
                for j in range(first, first + EACH):

                    @pl.when(j < count)
                    def _():
                        act(
                            pltpu.make_async_copy(
                                fresh_ref.at[j], out_ref.at[:, :, place(j)], done.at[groups + 1 + j]
                            )
                        )

    for_listed(lambda copy: copy.start())
    for_listed(lambda copy: copy.wait())


def vmem():
    return pl.BlockSpec(memory_space=pltpu.VMEM)


def anywhere():
    return pl.BlockSpec(memory_space=pl.ANY)


def from_hbm(x):
    return pltpu.with_memory_space_constraint(x, pltpu.HBM)


def cost(us):
    return pl.CostEstimate(flops=int(us * 1e9), bytes_accessed=int(us * 3e6), transcendentals=0)


def shards(
    concentrations, courant, first_weight, middle_weight, last_weight, active_blocks, dest_tile
):
    species, length, cols = concentrations.shape
    dests = lax.axis_size("spec")
    tiles = lax.axis_size("tile")
    cells = length // dests * cols
    slots = active_blocks.shape[-1]
    halves = cols // LANES
    f32, bf16 = jnp.float32, jnp.bfloat16
    params = pltpu.CompilerParams(vmem_limit_bytes=VMEM_BYTES)
    size = halves * (BEHIND * species + SUB) + SUB
    flag = jax.ShapeDtypeStruct((SUB, LANES), f32)

    field, rates = tiled(concentrations, halves), tiled(courant, halves)
    to_even, to_odd, hits, listing = pl.pallas_call(
        functools.partial(pack_kernel, length, halves, cells // BLK),
        out_shape=[jax.ShapeDtypeStruct((size, LANES), f32)] * 2
        + [flag, jax.ShapeDtypeStruct((1, slots), jnp.int32)],
        in_specs=[anywhere()] * 5,
        out_specs=[vmem()] * 4,
        scratch_shapes=[
            pltpu.VMEM((species * halves * SUB, LANES), f32),
            pltpu.VMEM((species * halves * SUB, LANES), f32),
            pltpu.VMEM((2 * halves * SUB, LANES), f32),
            pltpu.SMEM((slots,), jnp.int32),
            pltpu.SMEM((slots,), jnp.int32),
            pltpu.SemaphoreType.DMA((7,)),
        ],
        compiler_params=params,
        cost_estimate=cost(1.0),
        name="pack_edges",
    )(
        from_hbm(field),
        from_hbm(rates),
        from_hbm(active_blocks.reshape(-1)),
        from_hbm(dest_tile.reshape(-1)),
        from_hbm(active_blocks.reshape(1, slots)),
    )
    field = field.reshape(species * length * halves, LANES)
    evens = [(t, t ^ 1) for t in range(tiles)]
    odds = [(t, ((t + 1) ^ 1) - 1) for t in range(tiles)]
    odds = [(t, other % tiles) for t, other in odds]
    from_odd = lax.ppermute(to_odd, "tile", odds)
    from_even = lax.ppermute(to_even, "tile", evens)
    block = jax.ShapeDtypeStruct((species, cells), bf16)
    blocks = pl.pallas_call(
        functools.partial(inner_kernel, dests, length, halves),
        out_shape=[block] * dests,
        in_specs=[vmem()] * 2,
        out_specs=[vmem()] * dests,
        compiler_params=params,
        cost_estimate=cost(1.0),
        name="inner_rows",
    )(field, rates)
    def ring(k, x):
        return lax.ppermute(x, "spec", [(s, (s + k) % dests) for s in range(dests)])

    early = [dests // 2]
    late = [k for k in range(dests) if k not in early]
    edge = jax.ShapeDtypeStruct((species, BEHIND * cols), bf16)
    whole = pl.pallas_call(
        functools.partial(edge_kernel, dests, early, late, length, halves),
        out_shape=[block] * len(late)
        + [edge] * len(early)
        + [flag, jax.ShapeDtypeStruct((COPIES * SUB, LANES), f32), flag],
        in_specs=[vmem()] * (5 + len(late)),
        out_specs=[vmem()] * (dests + 3),
        compiler_params=params,
        cost_estimate=cost(0.1),
        name="edge_rows",
    )(from_odd, from_even, hits, field, rates, *[blocks[k] for k in late])
    full, edges, (to_even, to_odd, known) = whole[: len(late)], whole[len(late) : dests], whole[dests:]
    received = {k: ring(k, blocks[k]) for k in early}
    received |= {k: ring(k, x) if k else x for k, x in zip(late, full)}
    edges = [ring(k, x) for k, x in zip(early, edges)]
    from_odd = lax.ppermute(to_odd, "tile", odds)
    from_even = lax.ppermute(to_even, "tile", evens)
    w1, w2 = pl.pallas_call(
        weight_kernel,
        out_shape=[jax.ShapeDtypeStruct(w.shape[::-1], bf16) for w in (first_weight, middle_weight)],
        in_specs=[vmem()] * 2 + [anywhere()],
        out_specs=[vmem()] * 2,
        compiler_params=params,
        cost_estimate=cost(0.5),
        name="halved_weights",
    )(first_weight, middle_weight, known)
    out, load_share = pl.pallas_call(
        functools.partial(chemistry_kernel, dests, early),
        out_shape=[
            jax.ShapeDtypeStruct((dests, species, cells), bf16),
            jax.ShapeDtypeStruct((1, 1), f32),
        ],
        in_specs=[pl.BlockSpec(memory_space=pltpu.SMEM)] + [vmem()] * (6 + dests + len(early)),
        out_specs=[anywhere()] * 2,
        scratch_shapes=[
            pltpu.SMEM((slots + 1,), jnp.int32),
            pltpu.VMEM((len(early), species, cells), bf16),
            pltpu.VMEM((dests * species, slots * BLK), f32),
            pltpu.VMEM((slots, dests, species, BLK), bf16),
            pltpu.VMEM((1, 1), f32),
            pltpu.SemaphoreType.DMA((dests + 1 + slots,)),
        ],
        compiler_params=params,
        cost_estimate=cost(4.0),
        name="chemistry",
    )(
        listing.reshape(-1),
        w1,
        w2,
        last_weight.T,
        *[received[k] for k in range(dests)],
        *edges,
        known,
        from_odd,
        from_even,
    )
    return out.reshape(dests * species, cells), load_share


def solution(mesh):
    in_specs = (
        P("spec", "tile", None),
        P("tile", None),
        P(),
        P(),
        P(),
        P("tile", "spec", None),
        P("tile", "spec", None),
    )
    out_specs = (P(None, ("tile", "spec")), P("tile", "spec"))
    return jax.shard_map(shards, mesh=mesh, in_specs=in_specs, out_specs=out_specs, check_vma=False)
```

```python
import functools

import jax
import jax.numpy as jnp
from jax import lax
from jax.experimental import pallas as pl
from jax.experimental.pallas import tpu as pltpu
from jax.sharding import PartitionSpec as P

BLK = 128
RECV = 8
LANES = 128
SUB = 8
EACH = 4
BEHIND = 4
AHEAD = 2
VMEM_BYTES = 16 * 1024 * 1024


def silu_of_half(half):
    return half + half * jnp.tanh(half)


def sweep_rows(rows, rates):
    diffs = [b - a for a, b in zip(rows[:-1], rows[1:])]
    fluxes = []
    for at in range(1, len(rows) - 1):
        left, right = diffs[at - 1], diffs[at]
        slope = jnp.maximum(jnp.minimum(left, right), 0.0) + jnp.minimum(
            jnp.maximum(left, right), 0.0
        )
        rate, damp = rates[at]
        fluxes.append(rate * (rows[at] + damp * slope))
    return [rows[at] - fluxes[at - 1] + fluxes[at - 2] for at in range(2, len(rows) - 1)]


def two_sweeps(rows, rates):
    once = sweep_rows(rows, rates)
    return sweep_rows(once, rates[2:-1])


def with_damp(rate, shape):
    rate = jnp.broadcast_to(rate, shape)
    return rate, 0.5 - 0.5 * rate


def tiled(x, halves):
    lead, (rows, cols) = x.shape[:-2], x.shape[-2:]
    x = x.reshape(lead + (rows // SUB, SUB, halves, LANES))
    axes = tuple(range(len(lead)))
    x = x.transpose(axes + tuple(len(lead) + a for a in (0, 2, 1, 3)))
    return x.reshape(lead + (rows * halves, LANES))


def spot(at, half, halves):
    return (at // SUB * halves + half) * SUB + at % SUB


def pack_kernel(
    length, halves, blocks, q_in, rates_in, list_in, dest_in, row_in,
    even_ref, odd_ref, hits_ref, row_ref, low_ref, high_ref, rates_ref, list_ref, dest_ref, arrived,
):
    species, rows = q_in.shape[:2]
    tile = halves * SUB
    part = BEHIND * species + SUB
    shape = (species, tile, LANES)
    pairs = [
        (q_in.at[:, rows - tile :], high_ref.reshape(shape)),
        (q_in.at[:, :tile], low_ref.reshape(shape)),
        (rates_in.at[rows - tile :], rates_ref.at[tile:]),
        (rates_in.at[:tile], rates_ref.at[:tile]),
        (list_in, list_ref),
        (dest_in, dest_ref),
        (row_in, row_ref),
    ]
    copies = [
        pltpu.make_async_copy(source, target, arrived.at[i])
        for i, (source, target) in enumerate(pairs)
    ]
    for copy in copies:
        copy.start()
    copies[4].wait()
    copies[5].wait()
    lane = lax.broadcasted_iota(jnp.int32, (SUB, LANES), 1)
    hits = jnp.zeros((SUB, LANES), jnp.float32)
    for j in range(list_ref.shape[0]):
        target = jnp.where(list_ref[j] < blocks, dest_ref[j], -1)
        hits = hits + jnp.where(lane == target, 1.0, 0.0)
    hits_ref[...] = hits
    for copy in copies[:4] + copies[6:]:
        copy.wait()

    def write(up_ref, down_ref):
        for half in range(halves):
            start = half * part
            for j in range(BEHIND):
                at = start + j * species
                up_ref[at : at + species, :] = high_ref[
                    pl.ds(half * SUB + SUB - BEHIND + j, species, stride=tile), :
                ]
                if j < AHEAD:
                    value = low_ref[pl.ds(half * SUB + j, species, stride=tile), :]
                else:
                    value = jnp.zeros((species, LANES), jnp.float32)
                down_ref[at : at + species, :] = value
            at = start + BEHIND * species
            up_ref[at : at + SUB, :] = rates_ref[tile + half * SUB : tile + (half + 1) * SUB, :]
            down_ref[at : at + SUB, :] = rates_ref[half * SUB : (half + 1) * SUB, :]
        up_ref[halves * part :, :] = hits
        down_ref[halves * part :, :] = hits

    even = lax.rem(lax.axis_index("tile"), 2) == 0

    @pl.when(even)
    def _():
        write(even_ref, odd_ref)

    @pl.when(jnp.logical_not(even))
    def _():
        write(odd_ref, even_ref)


def inner_kernel(dests, length, halves, q_ref, rates_ref, *out_refs):
    species = out_refs[0].shape[0]
    share = length // dests
    me = lax.axis_index("spec")
    for k in range(dests):
        first = lax.rem(me + k, dests) * share
        below = jnp.maximum(first - SUB, 0)
        above = jnp.minimum(first + share, length - SUB)
        for half in range(halves):

            def start(at):
                if at < 0:
                    return below * halves + spot(at + SUB, half, halves)
                if at >= share:
                    return above * halves + spot(at - share, half, halves)
                return first * halves + spot(at, half, halves)

            reach = range(-BEHIND, share + AHEAD)
            rows = [q_ref[pl.ds(start(at), species, stride=length * halves), :] for at in reach]
            rates = [
                with_damp(rates_ref[pl.ds(start(at), 1), :], (species, LANES)) for at in reach
            ]
            for at, value in enumerate(two_sweeps(rows, rates)):
                place = (at * halves + half) * LANES
                out_refs[k][:, place : place + LANES] = value.astype(jnp.bfloat16)


def edge_kernel(
    dests, length, halves, odd_ref, even_ref, hits_ref, q_ref, rates_ref, *refs
):
    in_refs, out_refs, (to_even_ref, to_odd_ref, known_ref) = (
        refs[:dests], refs[dests : 2 * dests], refs[2 * dests :]
    )
    species, cells = out_refs[0].shape
    me = lax.axis_index("spec")
    part = BEHIND * species + SUB
    reach = BEHIND + AHEAD
    even = lax.rem(lax.axis_index("tile"), 2) == 0
    own, from_even, from_odd = hits_ref[...], even_ref[halves * part :, :], odd_ref[halves * part :, :]
    known_ref[...] = own + from_even + from_odd
    to_even_ref[...] = from_odd
    to_odd_ref[...] = from_even

    def message(behind, at, size):
        a, b = odd_ref[at : at + size, :], even_ref[at : at + size, :]
        return jnp.where(even, a, b) if behind else jnp.where(even, b, a)

    def row(at, half):
        return q_ref[pl.ds(spot(at, half, halves), species, stride=length * halves), :]

    def rates_of(values):
        return [with_damp(value, (species, LANES)) for value in values]

    tops, bottoms = [], []
    for half in range(halves):
        base = half * part
        behind = [message(True, base + j * species, species) for j in range(BEHIND)]
        ahead = [message(False, base + j * species, species) for j in range(AHEAD)]
        before = message(True, base + BEHIND * species, SUB)
        after = message(False, base + BEHIND * species, SUB)

        def own_rates(first):
            places = [spot(first + j, half, halves) for j in range(reach)]
            return [rates_ref[at : at + 1, :] for at in places]

        tops.append(
            two_sweeps(
                behind + [row(j, half) for j in range(reach)],
                rates_of([before[SUB - BEHIND + j :][:1] for j in range(BEHIND)] + own_rates(0)),
            )
        )
        bottoms.append(
            two_sweeps(
                [row(length - reach + j, half) for j in range(reach)] + ahead,
                rates_of(own_rates(length - reach) + [after[j : j + 1] for j in range(AHEAD)]),
            )
        )
    for k, (in_ref, out_ref) in enumerate(zip(in_refs, out_refs)):
        dest = lax.rem(me + k, dests)
        out_ref[...] = in_ref[...]

        @pl.when(dest == 0)
        def _():
            for half in range(halves):
                for j, value in enumerate(tops[half]):
                    at = (j * halves + half) * LANES
                    out_ref[:, at : at + LANES] = value.astype(jnp.bfloat16)

        @pl.when(dest == dests - 1)
        def _():
            for half in range(halves):
                for j, value in enumerate(bottoms[half]):
                    at = cells + ((j - AHEAD) * halves + half) * LANES
                    out_ref[:, at : at + LANES] = value.astype(jnp.bfloat16)


def weight_kernel(w1_ref, w2_ref, after_ref, w1_out, w2_out):
    w1_out[...] = (0.5 * w1_ref[...].astype(jnp.float32)).T.astype(jnp.bfloat16)
    w2_out[...] = (0.5 * w2_ref[...].astype(jnp.float32)).T.astype(jnp.bfloat16)


def chemistry_kernel(
    groups, named_ref, w1_ref, w2_ref, w3_ref, *refs
):
    parts, (known_ref, odd_ref, even_ref), refs = (
        refs[:groups], refs[groups : groups + 3], refs[groups + 3 :]
    )
    out_ref, share_ref, list_ref, picked_ref, fresh_ref, held_ref, done = refs
    species, cells = parts[0].shape
    slots = named_ref.shape[0]
    blocks = cells // BLK
    me = lax.axis_index("spec")
    sources = [lax.rem(me - k + groups, groups) for k in range(groups)]
    copies = [
        pltpu.make_async_copy(part, out_ref.at[source], done.at[k])
        for k, (part, source) in enumerate(zip(parts, sources))
    ]
    for copy in copies:
        copy.start()
    hits = known_ref[...] + odd_ref[...] + even_ref[...]
    lane = lax.broadcasted_iota(jnp.int32, hits.shape, 1)
    mine = jnp.where(lane == lax.axis_index("tile"), hits, 0.0)
    held_ref[...] = jnp.sum(mine[0:1], axis=1, keepdims=True) / RECV
    copies.append(pltpu.make_async_copy(held_ref, share_ref, done.at[groups]))
    copies[groups].start()
    for j in range(slots):
        list_ref[j] = blocks
    count = jnp.int32(0)
    for j in range(slots):
        block = named_ref[j]
        list_ref[count] = block
        count = count + jnp.where(block < blocks, 1, 0)

    def place(j):
        return pl.ds(pl.multiple_of(jnp.minimum(list_ref[j], blocks - 1) * BLK, BLK), BLK)

    def integrate(number):
        for j in range(number):
            for part, source in zip(parts, sources):
                rows = pl.ds(pl.multiple_of(source * species, species), species)
                picked_ref[rows, j * BLK : (j + 1) * BLK] = part[:, place(j)].astype(
                    jnp.float32
                )
        width = EACH * BLK
        spans = [slice(at, at + width) for at in range(0, number * BLK, width)]
        x = [picked_ref[:, span] for span in spans]
        hidden = [
            jnp.dot(w1_ref[...], v.astype(jnp.bfloat16), preferred_element_type=jnp.float32)
            for v in x
        ]
        hidden = [silu_of_half(v).astype(jnp.bfloat16) for v in hidden]
        hidden = [jnp.dot(w2_ref[...], v, preferred_element_type=jnp.float32) for v in hidden]
        hidden = [silu_of_half(v).astype(jnp.bfloat16) for v in hidden]
        for i, (v, h) in enumerate(zip(x, hidden)):
            v = v + jnp.dot(w3_ref[...], h, preferred_element_type=jnp.float32)
            for j in range(width // BLK):
                for g in range(groups):
                    fresh_ref[i * EACH + j, g] = v[
                        g * species : (g + 1) * species, j * BLK : (j + 1) * BLK
                    ].astype(jnp.bfloat16)

    for number in range(EACH, slots + 1, EACH):

        @pl.when((count > number - EACH) & (count <= number))
        def _():
            integrate(number)

    for copy in copies:
        copy.wait()

    def for_listed(act):
        for first in range(0, slots, EACH):

            @pl.when(first < count)
            def _():
                for j in range(first, first + EACH):

                    @pl.when(j < count)
                    def _():
                        act(
                            pltpu.make_async_copy(
                                fresh_ref.at[j], out_ref.at[:, :, place(j)], done.at[groups + 1 + j]
                            )
                        )

    for_listed(lambda copy: copy.start())
    for_listed(lambda copy: copy.wait())


def vmem():
    return pl.BlockSpec(memory_space=pltpu.VMEM)


def anywhere():
    return pl.BlockSpec(memory_space=pl.ANY)


def from_hbm(x):
    return pltpu.with_memory_space_constraint(x, pltpu.HBM)


def cost(us):
    return pl.CostEstimate(flops=int(us * 1e9), bytes_accessed=int(us * 3e6), transcendentals=0)


def shards(
    concentrations, courant, first_weight, middle_weight, last_weight, active_blocks, dest_tile
):
    species, length, cols = concentrations.shape
    dests = lax.axis_size("spec")
    tiles = lax.axis_size("tile")
    cells = length // dests * cols
    slots = active_blocks.shape[-1]
    halves = cols // LANES
    f32, bf16 = jnp.float32, jnp.bfloat16
    params = pltpu.CompilerParams(vmem_limit_bytes=VMEM_BYTES)
    size = halves * (BEHIND * species + SUB) + SUB
    flag = jax.ShapeDtypeStruct((SUB, LANES), f32)

    field, rates = tiled(concentrations, halves), tiled(courant, halves)
    to_even, to_odd, hits, listing = pl.pallas_call(
        functools.partial(pack_kernel, length, halves, cells // BLK),
        out_shape=[jax.ShapeDtypeStruct((size, LANES), f32)] * 2
        + [flag, jax.ShapeDtypeStruct((1, slots), jnp.int32)],
        in_specs=[anywhere()] * 5,
        out_specs=[vmem()] * 4,
        scratch_shapes=[
            pltpu.VMEM((species * halves * SUB, LANES), f32),
            pltpu.VMEM((species * halves * SUB, LANES), f32),
            pltpu.VMEM((2 * halves * SUB, LANES), f32),
            pltpu.SMEM((slots,), jnp.int32),
            pltpu.SMEM((slots,), jnp.int32),
            pltpu.SemaphoreType.DMA((7,)),
        ],
        compiler_params=params,
        cost_estimate=cost(1.0),
        name="pack_edges",
    )(
        from_hbm(field),
        from_hbm(rates),
        from_hbm(active_blocks.reshape(-1)),
        from_hbm(dest_tile.reshape(-1)),
        from_hbm(active_blocks.reshape(1, slots)),
    )
    field = field.reshape(species * length * halves, LANES)
    evens = [(t, t ^ 1) for t in range(tiles)]
    odds = [(t, ((t + 1) ^ 1) - 1) for t in range(tiles)]
    odds = [(t, other % tiles) for t, other in odds]
    from_odd = lax.ppermute(to_odd, "tile", odds)
    from_even = lax.ppermute(to_even, "tile", evens)
    block = jax.ShapeDtypeStruct((species, cells), bf16)
    blocks = pl.pallas_call(
        functools.partial(inner_kernel, dests, length, halves),
        out_shape=[block] * dests,
        in_specs=[vmem()] * 2,
        out_specs=[vmem()] * dests,
        compiler_params=params,
        cost_estimate=cost(1.0),
        name="inner_rows",
    )(field, rates)
    *blocks, to_even, to_odd, known = pl.pallas_call(
        functools.partial(edge_kernel, dests, length, halves),
        out_shape=[block] * dests + [flag] * 3,
        in_specs=[vmem()] * (5 + dests),
        out_specs=[vmem()] * (dests + 3),
        compiler_params=params,
        cost_estimate=cost(0.1),
        name="edge_rows",
    )(from_odd, from_even, hits, field, rates, *blocks)
    received = [blocks[0]] + [
        lax.ppermute(blocks[k], "spec", [(s, (s + k) % dests) for s in range(dests)])
        for k in range(1, dests)
    ]
    from_odd = lax.ppermute(to_odd, "tile", odds)
    from_even = lax.ppermute(to_even, "tile", evens)
    w1, w2 = pl.pallas_call(
        weight_kernel,
        out_shape=[jax.ShapeDtypeStruct(w.shape[::-1], bf16) for w in (first_weight, middle_weight)],
        in_specs=[vmem()] * 2 + [anywhere()],
        out_specs=[vmem()] * 2,
        compiler_params=params,
        cost_estimate=cost(0.5),
        name="halved_weights",
    )(first_weight, middle_weight, known)
    out, load_share = pl.pallas_call(
        functools.partial(chemistry_kernel, dests),
        out_shape=[
            jax.ShapeDtypeStruct((dests, species, cells), bf16),
            jax.ShapeDtypeStruct((1, 1), f32),
        ],
        in_specs=[pl.BlockSpec(memory_space=pltpu.SMEM)] + [vmem()] * (6 + dests),
        out_specs=[anywhere()] * 2,
        scratch_shapes=[
            pltpu.SMEM((slots + 1,), jnp.int32),
            pltpu.VMEM((dests * species, slots * BLK), f32),
            pltpu.VMEM((slots, dests, species, BLK), bf16),
            pltpu.VMEM((1, 1), f32),
            pltpu.SemaphoreType.DMA((dests + 1 + slots,)),
        ],
        compiler_params=params,
        cost_estimate=cost(4.0),
        name="chemistry",
    )(
        listing.reshape(-1),
        w1,
        w2,
        last_weight.T,
        *received,
        known,
        from_odd,
        from_even,
    )
    return out.reshape(dests * species, cells), load_share


def solution(mesh):
    in_specs = (
        P("spec", "tile", None),
        P("tile", None),
        P(),
        P(),
        P(),
        P("tile", "spec", None),
        P("tile", "spec", None),
    )
    out_specs = (P(None, ("tile", "spec")), P("tile", "spec"))
    return jax.shard_map(shards, mesh=mesh, in_specs=in_specs, out_specs=out_specs, check_vma=False)
```

```python
import functools

import jax
import jax.numpy as jnp
from jax import lax
from jax.experimental import pallas as pl
from jax.experimental.pallas import tpu as pltpu
from jax.sharding import PartitionSpec as P

BLK = 128
RECV = 8
LANES = 128
SUB = 8
EACH = 4
BEHIND = 4
AHEAD = 2
VMEM_BYTES = 16 * 1024 * 1024


def silu_of_half(half):
    return half + half * jnp.tanh(half)


def sweep_rows(rows, rates):
    diffs = [b - a for a, b in zip(rows[:-1], rows[1:])]
    fluxes = []
    for at in range(1, len(rows) - 1):
        left, right = diffs[at - 1], diffs[at]
        slope = jnp.maximum(jnp.minimum(left, right), 0.0) + jnp.minimum(
            jnp.maximum(left, right), 0.0
        )
        rate, damp = rates[at]
        fluxes.append(rate * (rows[at] + damp * slope))
    return [rows[at] - fluxes[at - 1] + fluxes[at - 2] for at in range(2, len(rows) - 1)]


def two_sweeps(rows, rates):
    once = sweep_rows(rows, rates)
    return sweep_rows(once, rates[2:-1])


def with_damp(rate, shape):
    rate = jnp.broadcast_to(rate, shape)
    return rate, 0.5 - 0.5 * rate


def tiled(x, halves):
    lead, (rows, cols) = x.shape[:-2], x.shape[-2:]
    x = x.reshape(lead + (rows // SUB, SUB, halves, LANES))
    axes = tuple(range(len(lead)))
    x = x.transpose(axes + tuple(len(lead) + a for a in (0, 2, 1, 3)))
    return x.reshape(lead + (rows * halves, LANES))


def spot(at, half, halves):
    return (at // SUB * halves + half) * SUB + at % SUB


def pack_kernel(
    length, halves, blocks, q_in, rates_in, list_in, dest_in, row_in,
    even_ref, odd_ref, hits_ref, row_ref, low_ref, high_ref, rates_ref, list_ref, dest_ref, arrived,
):
    species, rows = q_in.shape[:2]
    tile = halves * SUB
    part = BEHIND * species + SUB
    shape = (species, tile, LANES)
    pairs = [
        (q_in.at[:, rows - tile :], high_ref.reshape(shape)),
        (q_in.at[:, :tile], low_ref.reshape(shape)),
        (rates_in.at[rows - tile :], rates_ref.at[tile:]),
        (rates_in.at[:tile], rates_ref.at[:tile]),
        (list_in, list_ref),
        (dest_in, dest_ref),
        (row_in, row_ref),
    ]
    copies = [
        pltpu.make_async_copy(source, target, arrived.at[i])
        for i, (source, target) in enumerate(pairs)
    ]
    for copy in copies:
        copy.start()
    copies[4].wait()
    copies[5].wait()
    lane = lax.broadcasted_iota(jnp.int32, (SUB, LANES), 1)
    hits = jnp.zeros((SUB, LANES), jnp.float32)
    for j in range(list_ref.shape[0]):
        target = jnp.where(list_ref[j] < blocks, dest_ref[j], -1)
        hits = hits + jnp.where(lane == target, 1.0, 0.0)
    hits_ref[...] = hits
    for copy in copies[:4] + copies[6:]:
        copy.wait()

    def write(up_ref, down_ref):
        for half in range(halves):
            start = half * part
            for j in range(BEHIND):
                at = start + j * species
                up_ref[at : at + species, :] = high_ref[
                    pl.ds(half * SUB + SUB - BEHIND + j, species, stride=tile), :
                ]
                if j < AHEAD:
                    value = low_ref[pl.ds(half * SUB + j, species, stride=tile), :]
                else:
                    value = jnp.zeros((species, LANES), jnp.float32)
                down_ref[at : at + species, :] = value
            at = start + BEHIND * species
            up_ref[at : at + SUB, :] = rates_ref[tile + half * SUB : tile + (half + 1) * SUB, :]
            down_ref[at : at + SUB, :] = rates_ref[half * SUB : (half + 1) * SUB, :]
        up_ref[halves * part :, :] = hits
        down_ref[halves * part :, :] = hits

    even = lax.rem(lax.axis_index("tile"), 2) == 0

    @pl.when(even)
    def _():
        write(even_ref, odd_ref)

    @pl.when(jnp.logical_not(even))
    def _():
        write(odd_ref, even_ref)


def inner_kernel(dests, length, halves, q_ref, rates_ref, *out_refs):
    species = out_refs[0].shape[0]
    share = length // dests
    me = lax.axis_index("spec")
    for k in range(dests):
        first = lax.rem(me + k, dests) * share
        below = jnp.maximum(first - SUB, 0)
        above = jnp.minimum(first + share, length - SUB)
        for half in range(halves):

            def start(at):
                if at < 0:
                    return below * halves + spot(at + SUB, half, halves)
                if at >= share:
                    return above * halves + spot(at - share, half, halves)
                return first * halves + spot(at, half, halves)

            reach = range(-BEHIND, share + AHEAD)
            rows = [q_ref[pl.ds(start(at), species, stride=length * halves), :] for at in reach]
            rates = [
                with_damp(rates_ref[pl.ds(start(at), 1), :], (species, LANES)) for at in reach
            ]
            for at, value in enumerate(two_sweeps(rows, rates)):
                place = (at * halves + half) * LANES
                out_refs[k][:, place : place + LANES] = value.astype(jnp.bfloat16)


def edge_kernel(
    dests, length, halves, odd_ref, even_ref, hits_ref, q_ref, rates_ref, *refs
):
    in_refs, out_refs, (to_even_ref, to_odd_ref, known_ref) = (
        refs[:dests], refs[dests : 2 * dests], refs[2 * dests :]
    )
    species, cells = out_refs[0].shape
    me = lax.axis_index("spec")
    part = BEHIND * species + SUB
    reach = BEHIND + AHEAD
    even = lax.rem(lax.axis_index("tile"), 2) == 0
    own, from_even, from_odd = hits_ref[...], even_ref[halves * part :, :], odd_ref[halves * part :, :]
    known_ref[...] = own + from_even + from_odd
    to_even_ref[...] = from_odd
    to_odd_ref[...] = from_even

    def message(behind, at, size):
        a, b = odd_ref[at : at + size, :], even_ref[at : at + size, :]
        return jnp.where(even, a, b) if behind else jnp.where(even, b, a)

    def row(at, half):
        return q_ref[pl.ds(spot(at, half, halves), species, stride=length * halves), :]

    def rates_of(values):
        return [with_damp(value, (species, LANES)) for value in values]

    tops, bottoms = [], []
    for half in range(halves):
        base = half * part
        behind = [message(True, base + j * species, species) for j in range(BEHIND)]
        ahead = [message(False, base + j * species, species) for j in range(AHEAD)]
        before = message(True, base + BEHIND * species, SUB)
        after = message(False, base + BEHIND * species, SUB)

        def own_rates(first):
            places = [spot(first + j, half, halves) for j in range(reach)]
            return [rates_ref[at : at + 1, :] for at in places]

        tops.append(
            two_sweeps(
                behind + [row(j, half) for j in range(reach)],
                rates_of([before[SUB - BEHIND + j :][:1] for j in range(BEHIND)] + own_rates(0)),
            )
        )
        bottoms.append(
            two_sweeps(
                [row(length - reach + j, half) for j in range(reach)] + ahead,
                rates_of(own_rates(length - reach) + [after[j : j + 1] for j in range(AHEAD)]),
            )
        )
    for k, (in_ref, out_ref) in enumerate(zip(in_refs, out_refs)):
        dest = lax.rem(me + k, dests)
        out_ref[...] = in_ref[...]

        @pl.when(dest == 0)
        def _():
            for half in range(halves):
                for j, value in enumerate(tops[half]):
                    at = (j * halves + half) * LANES
                    out_ref[:, at : at + LANES] = value.astype(jnp.bfloat16)

        @pl.when(dest == dests - 1)
        def _():
            for half in range(halves):
                for j, value in enumerate(bottoms[half]):
                    at = cells + ((j - AHEAD) * halves + half) * LANES
                    out_ref[:, at : at + LANES] = value.astype(jnp.bfloat16)


def weight_kernel(w1_ref, w2_ref, after_ref, w1_out, w2_out):
    w1_out[...] = (0.5 * w1_ref[...].astype(jnp.float32)).T.astype(jnp.bfloat16)
    w2_out[...] = (0.5 * w2_ref[...].astype(jnp.float32)).T.astype(jnp.bfloat16)


def chemistry_kernel(
    groups, named_in, w1_ref, w2_ref, w3_ref, *refs
):
    parts, (known_ref, odd_ref, even_ref), refs = (
        refs[:groups], refs[groups : groups + 3], refs[groups + 3 :]
    )
    out_ref, share_ref, named_ref, list_ref, picked_ref, fresh_ref, held_ref, done = refs
    listing = pltpu.make_async_copy(named_in, named_ref, done.at[groups + 1])
    listing.start()
    species, cells = parts[0].shape
    slots = named_ref.shape[1]
    blocks = cells // BLK
    me = lax.axis_index("spec")
    sources = [lax.rem(me - k + groups, groups) for k in range(groups)]
    copies = [
        pltpu.make_async_copy(part, out_ref.at[source], done.at[k])
        for k, (part, source) in enumerate(zip(parts, sources))
    ]
    for copy in copies:
        copy.start()
    hits = known_ref[...] + odd_ref[...] + even_ref[...]
    lane = lax.broadcasted_iota(jnp.int32, hits.shape, 1)
    mine = jnp.where(lane == lax.axis_index("tile"), hits, 0.0)
    held_ref[...] = jnp.sum(mine[0:1], axis=1, keepdims=True) / RECV
    copies.append(pltpu.make_async_copy(held_ref, share_ref, done.at[groups]))
    copies[groups].start()
    listing.wait()
    for j in range(slots):
        list_ref[j] = blocks
    count = jnp.int32(0)
    for j in range(slots):
        block = named_ref[0, j]
        list_ref[count] = block
        count = count + jnp.where(block < blocks, 1, 0)

    def place(j):
        return pl.ds(pl.multiple_of(jnp.minimum(list_ref[j], blocks - 1) * BLK, BLK), BLK)

    def integrate(number):
        for j in range(number):
            for part, source in zip(parts, sources):
                rows = pl.ds(pl.multiple_of(source * species, species), species)
                picked_ref[rows, j * BLK : (j + 1) * BLK] = part[:, place(j)].astype(
                    jnp.float32
                )
        width = EACH * BLK
        spans = [slice(at, at + width) for at in range(0, number * BLK, width)]
        x = [picked_ref[:, span] for span in spans]
        hidden = [
            jnp.dot(w1_ref[...], v.astype(jnp.bfloat16), preferred_element_type=jnp.float32)
            for v in x
        ]
        hidden = [silu_of_half(v).astype(jnp.bfloat16) for v in hidden]
        hidden = [jnp.dot(w2_ref[...], v, preferred_element_type=jnp.float32) for v in hidden]
        hidden = [silu_of_half(v).astype(jnp.bfloat16) for v in hidden]
        for i, (v, h) in enumerate(zip(x, hidden)):
            v = v + jnp.dot(w3_ref[...], h, preferred_element_type=jnp.float32)
            for j in range(width // BLK):
                for g in range(groups):
                    fresh_ref[i * EACH + j, g] = v[
                        g * species : (g + 1) * species, j * BLK : (j + 1) * BLK
                    ].astype(jnp.bfloat16)

    for number in range(EACH, slots + 1, EACH):

        @pl.when((count > number - EACH) & (count <= number))
        def _():
            integrate(number)

    for copy in copies:
        copy.wait()

    def for_listed(act):
        for first in range(0, slots, EACH):

            @pl.when(first < count)
            def _():
                for j in range(first, first + EACH):

                    @pl.when(j < count)
                    def _():
                        act(
                            pltpu.make_async_copy(
                                fresh_ref.at[j], out_ref.at[:, :, place(j)], done.at[groups + 2 + j]
                            )
                        )

    for_listed(lambda copy: copy.start())
    for_listed(lambda copy: copy.wait())


def vmem():
    return pl.BlockSpec(memory_space=pltpu.VMEM)


def anywhere():
    return pl.BlockSpec(memory_space=pl.ANY)


def from_hbm(x):
    return pltpu.with_memory_space_constraint(x, pltpu.HBM)


def cost(us):
    return pl.CostEstimate(flops=int(us * 1e9), bytes_accessed=int(us * 3e6), transcendentals=0)


def shards(
    concentrations, courant, first_weight, middle_weight, last_weight, active_blocks, dest_tile
):
    species, length, cols = concentrations.shape
    dests = lax.axis_size("spec")
    tiles = lax.axis_size("tile")
    cells = length // dests * cols
    slots = active_blocks.shape[-1]
    halves = cols // LANES
    f32, bf16 = jnp.float32, jnp.bfloat16
    params = pltpu.CompilerParams(vmem_limit_bytes=VMEM_BYTES)
    size = halves * (BEHIND * species + SUB) + SUB
    flag = jax.ShapeDtypeStruct((SUB, LANES), f32)

    field, rates = tiled(concentrations, halves), tiled(courant, halves)
    to_even, to_odd, hits, listing = pl.pallas_call(
        functools.partial(pack_kernel, length, halves, cells // BLK),
        out_shape=[jax.ShapeDtypeStruct((size, LANES), f32)] * 2
        + [flag, jax.ShapeDtypeStruct((1, slots), jnp.int32)],
        in_specs=[anywhere()] * 5,
        out_specs=[vmem()] * 4,
        scratch_shapes=[
            pltpu.VMEM((species * halves * SUB, LANES), f32),
            pltpu.VMEM((species * halves * SUB, LANES), f32),
            pltpu.VMEM((2 * halves * SUB, LANES), f32),
            pltpu.SMEM((slots,), jnp.int32),
            pltpu.SMEM((slots,), jnp.int32),
            pltpu.SemaphoreType.DMA((7,)),
        ],
        compiler_params=params,
        cost_estimate=cost(1.0),
        name="pack_edges",
    )(
        from_hbm(field),
        from_hbm(rates),
        from_hbm(active_blocks.reshape(-1)),
        from_hbm(dest_tile.reshape(-1)),
        from_hbm(active_blocks.reshape(1, slots)),
    )
    field = field.reshape(species * length * halves, LANES)
    evens = [(t, t ^ 1) for t in range(tiles)]
    odds = [(t, ((t + 1) ^ 1) - 1) for t in range(tiles)]
    odds = [(t, other % tiles) for t, other in odds]
    from_odd = lax.ppermute(to_odd, "tile", odds)
    from_even = lax.ppermute(to_even, "tile", evens)
    block = jax.ShapeDtypeStruct((species, cells), bf16)
    blocks = pl.pallas_call(
        functools.partial(inner_kernel, dests, length, halves),
        out_shape=[block] * dests,
        in_specs=[vmem()] * 2,
        out_specs=[vmem()] * dests,
        compiler_params=params,
        cost_estimate=cost(1.0),
        name="inner_rows",
    )(field, rates)
    *blocks, to_even, to_odd, known = pl.pallas_call(
        functools.partial(edge_kernel, dests, length, halves),
        out_shape=[block] * dests + [flag] * 3,
        in_specs=[vmem()] * (5 + dests),
        out_specs=[vmem()] * (dests + 3),
        compiler_params=params,
        cost_estimate=cost(0.1),
        name="edge_rows",
    )(from_odd, from_even, hits, field, rates, *blocks)
    received = [blocks[0]] + [
        lax.ppermute(blocks[k], "spec", [(s, (s + k) % dests) for s in range(dests)])
        for k in range(1, dests)
    ]
    from_odd = lax.ppermute(to_odd, "tile", odds)
    from_even = lax.ppermute(to_even, "tile", evens)
    w1, w2 = pl.pallas_call(
        weight_kernel,
        out_shape=[jax.ShapeDtypeStruct(w.shape[::-1], bf16) for w in (first_weight, middle_weight)],
        in_specs=[vmem()] * 2 + [anywhere()],
        out_specs=[vmem()] * 2,
        compiler_params=params,
        cost_estimate=cost(0.5),
        name="halved_weights",
    )(first_weight, middle_weight, known)
    out, load_share = pl.pallas_call(
        functools.partial(chemistry_kernel, dests),
        out_shape=[
            jax.ShapeDtypeStruct((dests, species, cells), bf16),
            jax.ShapeDtypeStruct((1, 1), f32),
        ],
        in_specs=[anywhere()] + [vmem()] * (6 + dests),
        out_specs=[anywhere()] * 2,
        scratch_shapes=[
            pltpu.SMEM((1, slots), jnp.int32),
            pltpu.SMEM((slots + 1,), jnp.int32),
            pltpu.VMEM((dests * species, slots * BLK), f32),
            pltpu.VMEM((slots, dests, species, BLK), bf16),
            pltpu.VMEM((1, 1), f32),
            pltpu.SemaphoreType.DMA((dests + 2 + slots,)),
        ],
        compiler_params=params,
        cost_estimate=cost(4.0),
        name="chemistry",
    )(
        listing,
        w1,
        w2,
        last_weight.T,
        *received,
        known,
        from_odd,
        from_even,
    )
    return out.reshape(dests * species, cells), load_share


def solution(mesh):
    in_specs = (
        P("spec", "tile", None),
        P("tile", None),
        P(),
        P(),
        P(),
        P("tile", "spec", None),
        P("tile", "spec", None),
    )
    out_specs = (P(None, ("tile", "spec")), P("tile", "spec"))
    return jax.shard_map(shards, mesh=mesh, in_specs=in_specs, out_specs=out_specs, check_vma=False)
```

```python
import functools

import jax
import jax.numpy as jnp
from jax import lax
from jax.experimental import pallas as pl
from jax.experimental.pallas import tpu as pltpu
from jax.sharding import PartitionSpec as P

BLK = 128
RECV = 8
LANES = 128
SUB = 8
EACH = 4
BEHIND = 4
AHEAD = 2
VMEM_BYTES = 16 * 1024 * 1024


def silu_of_half(half):
    return half + half * jnp.tanh(half)


def sweep_rows(rows, rates):
    diffs = [b - a for a, b in zip(rows[:-1], rows[1:])]
    fluxes = []
    for at in range(1, len(rows) - 1):
        left, right = diffs[at - 1], diffs[at]
        slope = jnp.maximum(jnp.minimum(left, right), 0.0) + jnp.minimum(
            jnp.maximum(left, right), 0.0
        )
        rate, damp = rates[at]
        fluxes.append(rate * (rows[at] + damp * slope))
    return [rows[at] - fluxes[at - 1] + fluxes[at - 2] for at in range(2, len(rows) - 1)]


def two_sweeps(rows, rates):
    once = sweep_rows(rows, rates)
    return sweep_rows(once, rates[2:-1])


def with_damp(rate, shape):
    rate = jnp.broadcast_to(rate, shape)
    return rate, 0.5 - 0.5 * rate


def tiled(x, halves):
    lead, (rows, cols) = x.shape[:-2], x.shape[-2:]
    x = x.reshape(lead + (rows // SUB, SUB, halves, LANES))
    axes = tuple(range(len(lead)))
    x = x.transpose(axes + tuple(len(lead) + a for a in (0, 2, 1, 3)))
    return x.reshape(lead + (rows * halves, LANES))


def spot(at, half, halves):
    return (at // SUB * halves + half) * SUB + at % SUB


def pack_kernel(
    length, halves, blocks, q_in, rates_in, list_in, dest_in, row_in,
    even_ref, odd_ref, hits_ref, row_ref, low_ref, high_ref, rates_ref, list_ref, dest_ref, arrived,
):
    species, rows = q_in.shape[:2]
    tile = halves * SUB
    part = BEHIND * species + SUB
    shape = (species, tile, LANES)
    pairs = [
        (q_in.at[:, rows - tile :], high_ref.reshape(shape)),
        (q_in.at[:, :tile], low_ref.reshape(shape)),
        (rates_in.at[rows - tile :], rates_ref.at[tile:]),
        (rates_in.at[:tile], rates_ref.at[:tile]),
        (list_in, list_ref),
        (dest_in, dest_ref),
        (row_in, row_ref),
    ]
    copies = [
        pltpu.make_async_copy(source, target, arrived.at[i])
        for i, (source, target) in enumerate(pairs)
    ]
    for copy in copies:
        copy.start()
    copies[4].wait()
    copies[5].wait()
    lane = lax.broadcasted_iota(jnp.int32, (SUB, LANES), 1)
    hits = jnp.zeros((SUB, LANES), jnp.float32)
    for j in range(list_ref.shape[0]):
        target = jnp.where(list_ref[j] < blocks, dest_ref[j], -1)
        hits = hits + jnp.where(lane == target, 1.0, 0.0)
    hits_ref[...] = hits
    for copy in copies[:4] + copies[6:]:
        copy.wait()

    def write(up_ref, down_ref):
        for half in range(halves):
            start = half * part
            for j in range(BEHIND):
                at = start + j * species
                up_ref[at : at + species, :] = high_ref[
                    pl.ds(half * SUB + SUB - BEHIND + j, species, stride=tile), :
                ]
                if j < AHEAD:
                    value = low_ref[pl.ds(half * SUB + j, species, stride=tile), :]
                else:
                    value = jnp.zeros((species, LANES), jnp.float32)
                down_ref[at : at + species, :] = value
            at = start + BEHIND * species
            up_ref[at : at + SUB, :] = rates_ref[tile + half * SUB : tile + (half + 1) * SUB, :]
            down_ref[at : at + SUB, :] = rates_ref[half * SUB : (half + 1) * SUB, :]
        up_ref[halves * part :, :] = hits
        down_ref[halves * part :, :] = hits

    even = lax.rem(lax.axis_index("tile"), 2) == 0

    @pl.when(even)
    def _():
        write(even_ref, odd_ref)

    @pl.when(jnp.logical_not(even))
    def _():
        write(odd_ref, even_ref)


def inner_kernel(dests, length, halves, q_ref, rates_ref, *out_refs):
    species = out_refs[0].shape[0]
    share = length // dests
    me = lax.axis_index("spec")
    for k in range(dests):
        first = lax.rem(me + k, dests) * share
        below = jnp.maximum(first - SUB, 0)
        above = jnp.minimum(first + share, length - SUB)
        for half in range(halves):

            def start(at):
                if at < 0:
                    return below * halves + spot(at + SUB, half, halves)
                if at >= share:
                    return above * halves + spot(at - share, half, halves)
                return first * halves + spot(at, half, halves)

            reach = range(-BEHIND, share + AHEAD)
            rows = [q_ref[pl.ds(start(at), species, stride=length * halves), :] for at in reach]
            rates = [
                with_damp(rates_ref[pl.ds(start(at), 1), :], (species, LANES)) for at in reach
            ]
            for at, value in enumerate(two_sweeps(rows, rates)):
                place = (at * halves + half) * LANES
                out_refs[k][:, place : place + LANES] = value.astype(jnp.bfloat16)


def edge_kernel(
    dests, length, halves, odd_ref, even_ref, hits_ref, q_ref, rates_ref, *refs
):
    in_refs, out_refs, (to_even_ref, to_odd_ref, known_ref) = (
        refs[:dests], refs[dests : 2 * dests], refs[2 * dests :]
    )
    species, cells = out_refs[0].shape
    me = lax.axis_index("spec")
    part = BEHIND * species + SUB
    reach = BEHIND + AHEAD
    even = lax.rem(lax.axis_index("tile"), 2) == 0
    own, from_even, from_odd = hits_ref[...], even_ref[halves * part :, :], odd_ref[halves * part :, :]
    known_ref[...] = own + from_even + from_odd
    to_even_ref[...] = from_odd
    to_odd_ref[...] = from_even

    def message(behind, at, size):
        a, b = odd_ref[at : at + size, :], even_ref[at : at + size, :]
        return jnp.where(even, a, b) if behind else jnp.where(even, b, a)

    def row(at, half):
        return q_ref[pl.ds(spot(at, half, halves), species, stride=length * halves), :]

    def rates_of(values):
        return [with_damp(value, (species, LANES)) for value in values]

    tops, bottoms = [], []
    for half in range(halves):
        base = half * part
        behind = [message(True, base + j * species, species) for j in range(BEHIND)]
        ahead = [message(False, base + j * species, species) for j in range(AHEAD)]
        before = message(True, base + BEHIND * species, SUB)
        after = message(False, base + BEHIND * species, SUB)

        def own_rates(first):
            places = [spot(first + j, half, halves) for j in range(reach)]
            return [rates_ref[at : at + 1, :] for at in places]

        tops.append(
            two_sweeps(
                behind + [row(j, half) for j in range(reach)],
                rates_of([before[SUB - BEHIND + j :][:1] for j in range(BEHIND)] + own_rates(0)),
            )
        )
        bottoms.append(
            two_sweeps(
                [row(length - reach + j, half) for j in range(reach)] + ahead,
                rates_of(own_rates(length - reach) + [after[j : j + 1] for j in range(AHEAD)]),
            )
        )
    for k, (in_ref, out_ref) in enumerate(zip(in_refs, out_refs)):
        dest = lax.rem(me + k, dests)
        out_ref[...] = in_ref[...]

        @pl.when(dest == 0)
        def _():
            for half in range(halves):
                for j, value in enumerate(tops[half]):
                    at = (j * halves + half) * LANES
                    out_ref[:, at : at + LANES] = value.astype(jnp.bfloat16)

        @pl.when(dest == dests - 1)
        def _():
            for half in range(halves):
                for j, value in enumerate(bottoms[half]):
                    at = cells + ((j - AHEAD) * halves + half) * LANES
                    out_ref[:, at : at + LANES] = value.astype(jnp.bfloat16)


def weight_kernel(w1_ref, w2_ref, after_ref, w1_out, w2_out):
    w1_out[...] = (0.5 * w1_ref[...].astype(jnp.float32)).T.astype(jnp.bfloat16)
    w2_out[...] = (0.5 * w2_ref[...].astype(jnp.float32)).T.astype(jnp.bfloat16)


def ring_order(count):
    return [0, 1] + list(range(count - 1, 1, -1))


def chemistry_kernel(
    groups, named_in, w1_ref, w2_ref, w3_ref, *refs
):
    parts, (known_ref, odd_ref, even_ref), refs = (
        refs[:groups], refs[groups : groups + 3], refs[groups + 3 :]
    )
    out_ref, share_ref, named_ref, list_ref, picked_ref, fresh_ref, held_ref, done = refs
    listing = pltpu.make_async_copy(named_in, named_ref, done.at[groups + 1])
    listing.start()
    species, cells = parts[0].shape
    slots = named_ref.shape[1]
    blocks = cells // BLK
    me = lax.axis_index("spec")
    sources = [lax.rem(me - k + groups, groups) for k in ring_order(groups)]
    copies = [
        pltpu.make_async_copy(part, out_ref.at[source], done.at[k])
        for k, (part, source) in enumerate(zip(parts, sources))
    ]
    for copy in copies:
        copy.start()
    hits = known_ref[...] + odd_ref[...] + even_ref[...]
    lane = lax.broadcasted_iota(jnp.int32, hits.shape, 1)
    mine = jnp.where(lane == lax.axis_index("tile"), hits, 0.0)
    held_ref[...] = jnp.sum(mine[0:1], axis=1, keepdims=True) / RECV
    copies.append(pltpu.make_async_copy(held_ref, share_ref, done.at[groups]))
    copies[groups].start()
    listing.wait()
    for j in range(slots):
        list_ref[j] = blocks
    count = jnp.int32(0)
    for j in range(slots):
        block = named_ref[0, j]
        list_ref[count] = block
        count = count + jnp.where(block < blocks, 1, 0)

    def place(j):
        return pl.ds(pl.multiple_of(jnp.minimum(list_ref[j], blocks - 1) * BLK, BLK), BLK)

    def integrate(number):
        for j in range(number):
            for part, source in zip(parts, sources):
                rows = pl.ds(pl.multiple_of(source * species, species), species)
                picked_ref[rows, j * BLK : (j + 1) * BLK] = part[:, place(j)].astype(
                    jnp.float32
                )
        width = EACH * BLK
        spans = [slice(at, at + width) for at in range(0, number * BLK, width)]
        x = [picked_ref[:, span] for span in spans]
        hidden = [
            jnp.dot(w1_ref[...], v.astype(jnp.bfloat16), preferred_element_type=jnp.float32)
            for v in x
        ]
        hidden = [silu_of_half(v).astype(jnp.bfloat16) for v in hidden]
        hidden = [jnp.dot(w2_ref[...], v, preferred_element_type=jnp.float32) for v in hidden]
        hidden = [silu_of_half(v).astype(jnp.bfloat16) for v in hidden]
        for i, (v, h) in enumerate(zip(x, hidden)):
            v = v + jnp.dot(w3_ref[...], h, preferred_element_type=jnp.float32)
            for j in range(width // BLK):
                for g in range(groups):
                    fresh_ref[i * EACH + j, g] = v[
                        g * species : (g + 1) * species, j * BLK : (j + 1) * BLK
                    ].astype(jnp.bfloat16)

    for number in range(EACH, slots + 1, EACH):

        @pl.when((count > number - EACH) & (count <= number))
        def _():
            integrate(number)

    for copy in copies:
        copy.wait()

    def for_listed(act):
        for first in range(0, slots, EACH):

            @pl.when(first < count)
            def _():
                for j in range(first, first + EACH):

                    @pl.when(j < count)
                    def _():
                        act(
                            pltpu.make_async_copy(
                                fresh_ref.at[j], out_ref.at[:, :, place(j)], done.at[groups + 2 + j]
                            )
                        )

    for_listed(lambda copy: copy.start())
    for_listed(lambda copy: copy.wait())


def vmem():
    return pl.BlockSpec(memory_space=pltpu.VMEM)


def anywhere():
    return pl.BlockSpec(memory_space=pl.ANY)


def from_hbm(x):
    return pltpu.with_memory_space_constraint(x, pltpu.HBM)


def cost(us):
    return pl.CostEstimate(flops=int(us * 1e9), bytes_accessed=int(us * 3e6), transcendentals=0)


def shards(
    concentrations, courant, first_weight, middle_weight, last_weight, active_blocks, dest_tile
):
    species, length, cols = concentrations.shape
    dests = lax.axis_size("spec")
    tiles = lax.axis_size("tile")
    cells = length // dests * cols
    slots = active_blocks.shape[-1]
    halves = cols // LANES
    f32, bf16 = jnp.float32, jnp.bfloat16
    params = pltpu.CompilerParams(vmem_limit_bytes=VMEM_BYTES)
    size = halves * (BEHIND * species + SUB) + SUB
    flag = jax.ShapeDtypeStruct((SUB, LANES), f32)

    field, rates = tiled(concentrations, halves), tiled(courant, halves)
    to_even, to_odd, hits, listing = pl.pallas_call(
        functools.partial(pack_kernel, length, halves, cells // BLK),
        out_shape=[jax.ShapeDtypeStruct((size, LANES), f32)] * 2
        + [flag, jax.ShapeDtypeStruct((1, slots), jnp.int32)],
        in_specs=[anywhere()] * 5,
        out_specs=[vmem()] * 4,
        scratch_shapes=[
            pltpu.VMEM((species * halves * SUB, LANES), f32),
            pltpu.VMEM((species * halves * SUB, LANES), f32),
            pltpu.VMEM((2 * halves * SUB, LANES), f32),
            pltpu.SMEM((slots,), jnp.int32),
            pltpu.SMEM((slots,), jnp.int32),
            pltpu.SemaphoreType.DMA((7,)),
        ],
        compiler_params=params,
        cost_estimate=cost(1.0),
        name="pack_edges",
    )(
        from_hbm(field),
        from_hbm(rates),
        from_hbm(active_blocks.reshape(-1)),
        from_hbm(dest_tile.reshape(-1)),
        from_hbm(active_blocks.reshape(1, slots)),
    )
    field = field.reshape(species * length * halves, LANES)
    evens = [(t, t ^ 1) for t in range(tiles)]
    odds = [(t, ((t + 1) ^ 1) - 1) for t in range(tiles)]
    odds = [(t, other % tiles) for t, other in odds]
    from_odd = lax.ppermute(to_odd, "tile", odds)
    from_even = lax.ppermute(to_even, "tile", evens)
    block = jax.ShapeDtypeStruct((species, cells), bf16)
    blocks = pl.pallas_call(
        functools.partial(inner_kernel, dests, length, halves),
        out_shape=[block] * dests,
        in_specs=[vmem()] * 2,
        out_specs=[vmem()] * dests,
        compiler_params=params,
        cost_estimate=cost(1.0),
        name="inner_rows",
    )(field, rates)
    *blocks, to_even, to_odd, known = pl.pallas_call(
        functools.partial(edge_kernel, dests, length, halves),
        out_shape=[block] * dests + [flag] * 3,
        in_specs=[vmem()] * (5 + dests),
        out_specs=[vmem()] * (dests + 3),
        compiler_params=params,
        cost_estimate=cost(0.1),
        name="edge_rows",
    )(from_odd, from_even, hits, field, rates, *blocks)
    received = [blocks[0]] + [
        lax.ppermute(blocks[k], "spec", [(s, (s + k) % dests) for s in range(dests)])
        for k in range(1, dests)
    ]
    from_odd = lax.ppermute(to_odd, "tile", odds)
    from_even = lax.ppermute(to_even, "tile", evens)
    w1, w2 = pl.pallas_call(
        weight_kernel,
        out_shape=[jax.ShapeDtypeStruct(w.shape[::-1], bf16) for w in (first_weight, middle_weight)],
        in_specs=[vmem()] * 2 + [anywhere()],
        out_specs=[vmem()] * 2,
        compiler_params=params,
        cost_estimate=cost(0.5),
        name="halved_weights",
    )(first_weight, middle_weight, known)
    out, load_share = pl.pallas_call(
        functools.partial(chemistry_kernel, dests),
        out_shape=[
            jax.ShapeDtypeStruct((dests, species, cells), bf16),
            jax.ShapeDtypeStruct((1, 1), f32),
        ],
        in_specs=[anywhere()] + [vmem()] * (6 + dests),
        out_specs=[anywhere()] * 2,
        scratch_shapes=[
            pltpu.SMEM((1, slots), jnp.int32),
            pltpu.SMEM((slots + 1,), jnp.int32),
            pltpu.VMEM((dests * species, slots * BLK), f32),
            pltpu.VMEM((slots, dests, species, BLK), bf16),
            pltpu.VMEM((1, 1), f32),
            pltpu.SemaphoreType.DMA((dests + 2 + slots,)),
        ],
        compiler_params=params,
        cost_estimate=cost(4.0),
        name="chemistry",
    )(
        listing,
        w1,
        w2,
        last_weight.T,
        *[received[k] for k in ring_order(dests)],
        known,
        from_odd,
        from_even,
    )
    return out.reshape(dests * species, cells), load_share


def solution(mesh):
    in_specs = (
        P("spec", "tile", None),
        P("tile", None),
        P(),
        P(),
        P(),
        P("tile", "spec", None),
        P("tile", "spec", None),
    )
    out_specs = (P(None, ("tile", "spec")), P("tile", "spec"))
    return jax.shard_map(shards, mesh=mesh, in_specs=in_specs, out_specs=out_specs, check_vma=False)
```
